128 devices in a mesh: section: 2 (over core), dp: 16 (over y, x), tensor: 4 (over z).
Axes of the slice: x: 4, y: 4, z: 4, core: 2. Of those that a mesh axis runs over, the one named last changes fastest.
Arguments:
- boundary_copies: bfloat16 [2, 2, 32, 128, 4096], P('section', None, 'dp', None, 'tensor'), may hold values from -6 to 6
- arriving: bfloat16 [2, 16, 128, 4096], P('section', 'dp', None, 'tensor'), may hold values from -7 to 7
- first_delta: bfloat16 [2, 16, 128, 4096], P(None, 'dp', None, 'tensor'), may hold values from -7 to 7
- sample_index: int32 [4, 16], P(None, 'dp'), may hold values from 0 to 1
- exponents: int32 [3, 32], P(None, 'tensor'), may hold values from -3 to -1
- norm_gain: float32 [2, 4096], P('section'), may hold values from 0.25 to 1.75
- w_query: bfloat16 [2, 4096, 4096], P('section', 'dp', 'tensor'), may hold values from -0.09375 to 0.09375
- w_key: bfloat16 [2, 4096, 512], P('section', 'dp', 'tensor'), may hold values from -0.09375 to 0.09375
- w_value: bfloat16 [2, 4096, 512], P('section', 'dp', 'tensor'), may hold values from -0.09375 to 0.09375
- w_out: bfloat16 [2, 4096, 4096], P('section', 'tensor', 'dp'), may hold values from -0.09375 to 0.09375
- out_grad: bfloat16 [2, 3, 16, 128, 4096], P('section', None, 'dp'), may hold values from -6 to 6
Outputs:
- copies_new: bfloat16 [2, 2, 32, 128, 4096], P('section', None, 'dp', None, 'tensor')
- grad_query: bfloat16 [2, 4096, 4096], P('section', 'dp', 'tensor')
- grad_value: bfloat16 [2, 4096, 512], P('section', 'dp', 'tensor')
The draws below stay inside these ranges and needn't reach their ends.
All inputs are finite; a program needn't handle non-finite values.
Results may differ from the reference program's by a relative error of at most 0.025.
Values may be sent and summed in bfloat16 or wider, within the bound.
No kernel may reach another device: no remote copies, remote signals or barrier semaphores. Data moves between devices by JAX's collectives and lax.ppermute only.
A program may use at most 128 MiB of HBM per device.

```python
import jax
import jax.numpy as jnp
from jax import lax

D = 4096
HQ = 32
HK = 4
HD = 128
QB = 128
SEQ = 128
SAMP_DEV = 2
TICKS = 3
NL = 2
BATCH = 16
SAMPLES = 32
MICRO = 4
BOUNDS = 3
N_TENSOR = 4


def place_ends(result, key, least, top_value):
    place = [jax.random.randint(jax.random.fold_in(key, axis), (), 0, length) for axis, length in enumerate(result.shape)]
    main_axis = result.shape.index(max(result.shape))
    neighbour = place[:main_axis] + [(place[main_axis] + 1) % result.shape[main_axis]] + place[main_axis + 1:]
    return result.at[tuple(place)].set(least).at[tuple(neighbour)].set(top_value)


def block_levels(own_key, dims, pieces, low, top_value):
    level = 1.0
    for axis_at, parts in pieces:
        steps = jax.random.uniform(jax.random.fold_in(jax.random.fold_in(own_key, 6), axis_at), (parts,), jnp.float32, low / len(pieces), top_value / len(pieces))
        level = level * jnp.repeat(jnp.exp(steps), dims[axis_at] // parts).reshape((-1,) + (1,) * (len(dims) - 1 - axis_at))
    return level


def centred(own_key, shape, scale, most, split=(), kind=jnp.bfloat16):
    array = jax.random.normal(own_key, shape, jnp.float32) * scale
    if len(split) > 0:
        array = block_levels(own_key, shape, split, -0.22, 0.18) * array
    return jnp.clip(array, min=-most, max=most).astype(kind)


def setup_inputs(seed: int = 0) -> dict:
    streams_of = jax.random.split(jax.random.key(seed), 12)
    boundary_copies = centred(streams_of[0], (NL, 2, SAMPLES, SEQ, D), 1.0, 6.0, ((0, 2), (2, 16), (4, 4)))
    arriving = jnp.clip(jax.random.uniform(streams_of[1], (NL, BATCH, SEQ, D), jnp.float32, -7.0, 7.0) * block_levels(streams_of[1], (NL, BATCH, SEQ, D), ((0, 2), (1, 16), (3, 4)), -0.4, 0.0), -7.0, 7.0).astype(jnp.bfloat16)
    first_delta = jnp.clip(jax.random.uniform(streams_of[2], (TICKS - 1, BATCH, SEQ, D), jnp.float32, -7.0, 7.0) * block_levels(streams_of[2], (TICKS - 1, BATCH, SEQ, D), ((1, 16), (3, 4)), -0.4, 0.0), -7.0, 7.0).astype(jnp.bfloat16)
    sample_index = place_ends(jax.random.randint(streams_of[3], (MICRO, BATCH), 0, SAMP_DEV), jax.random.fold_in(streams_of[3], 1), 0, SAMP_DEV - 1).astype(jnp.int32)
    exponents = place_ends(jax.random.randint(streams_of[4], (BOUNDS, D // QB), -3, 0), jax.random.fold_in(streams_of[4], 1), -3, -1).astype(jnp.int32)
    norm_gain = jnp.clip(1.0 + 0.15 * jax.random.normal(streams_of[5], (NL, D), jnp.float32), 0.25, 1.75)
    w_query = centred(streams_of[6], (NL, D, HQ * HD), D ** -0.5, 0.09375, ((0, 2), (1, 16), (2, 4)))
    w_key = centred(streams_of[7], (NL, D, HK * HD), D ** -0.5, 0.09375, ((0, 2), (1, 16), (2, 4)))
    w_value = centred(streams_of[8], (NL, D, HK * HD), D ** -0.5, 0.09375, ((0, 2), (1, 16), (2, 4)))
    w_out = centred(streams_of[9], (NL, HQ * HD, D), (HQ * HD) ** -0.5, 0.09375, ((0, 2), (1, 4), (2, 16)))
    out_grad = centred(streams_of[10], (NL, TICKS, BATCH, SEQ, D), 1.0, 6.0, ((0, 2), (2, 16)))
    return {"boundary_copies": boundary_copies, "arriving": arriving, "first_delta": first_delta, "sample_index": sample_index, "exponents": exponents, "norm_gain": norm_gain, "w_query": w_query, "w_key": w_key, "w_value": w_value, "w_out": w_out, "out_grad": out_grad}


eps_norm = 1e-05
qmax = 7.0

def normalize(inputs, gain):
    values = inputs.astype(jnp.float32)
    square = lax.optimization_barrier(jnp.mean(values * values, axis=-1, keepdims=True))
    return (values * lax.rsqrt(square + eps_norm) * gain).astype(jnp.bfloat16)

def attend(query, key_in, value_in):
    length = query.shape[0]
    group = HQ // HK
    scale = HD ** (-0.5)
    qf = query.astype(jnp.float32).reshape(length, -1, group, HD)
    kf = key_in.astype(jnp.float32).reshape(length, -1, HD)
    vf = value_in.astype(jnp.float32).reshape(length, -1, HD)
    scores = jnp.einsum('sngd,tnd->ngst', qf, kf) * scale
    causal = jnp.arange(length)[:, None] >= jnp.arange(length)[None, :]
    scores = jnp.where(causal, scores, -1e+30)
    probs = jax.nn.softmax(scores, axis=-1)
    rounded = lax.optimization_barrier(probs.astype(jnp.bfloat16)).astype(jnp.float32)
    mixed = jnp.einsum('ngst,tnd->sngd', rounded, vf).reshape(length, -1)
    return (mixed.astype(jnp.bfloat16), probs, rounded)

def attend_back(query, key_in, value_in, probs, rounded, d_mixed):
    length = query.shape[0]
    group = HQ // HK
    scale = HD ** (-0.5)
    kf = key_in.astype(jnp.float32).reshape(length, -1, HD)
    vf = value_in.astype(jnp.float32).reshape(length, -1, HD)
    df = d_mixed.astype(jnp.float32).reshape(length, -1, group, HD)
    d_probs = jnp.einsum('sngd,tnd->ngst', df, vf)
    d_scores = probs * (d_probs - lax.optimization_barrier(jnp.sum(d_probs * probs, axis=-1, keepdims=True))) * scale
    d_query = jnp.einsum('ngst,tnd->sngd', d_scores, kf).reshape(length, -1)
    d_value = jnp.einsum('ngst,sngd->tnd', rounded, df).reshape(length, -1)
    return (d_query.astype(jnp.bfloat16), d_value.astype(jnp.bfloat16))

def replica_sum(left, right):
    total = jnp.zeros((left.shape[-1], right.shape[-1]), jnp.float32)
    for replica in range(BATCH):
        lhs = left[:, replica].reshape(-1, left.shape[-1])
        rhs = right[:, replica].reshape(-1, right.shape[-1])
        term = lax.dot_general(lhs, rhs, (((0,), (0,)), ((), ())), preferred_element_type=jnp.float32)
        total = total + lax.optimization_barrier(term.astype(jnp.bfloat16)).astype(jnp.float32)
    return total.astype(jnp.bfloat16)

def reference(boundary_copies, arriving, first_delta, sample_index, exponents, norm_gain, w_query, w_key, w_value, w_out, out_grad):
    sections = NL
    width = HQ * HD // N_TENSOR
    power = exponents.astype(jnp.float32)
    scale_full = jnp.repeat(jnp.exp2(power), QB, axis=1)
    inverse_full = jnp.repeat(jnp.exp2(-power), QB, axis=1)
    state_in = [boundary_copies[s, 0].reshape(BATCH, SAMP_DEV, SEQ, D) for s in range(sections)]
    state_out = [boundary_copies[s, 1].reshape(BATCH, SAMP_DEV, SEQ, D) for s in range(sections)]
    saved = [[] for s in range(sections)]
    replicas = jnp.arange(BATCH)
    previous = []
    attend_all = jax.vmap(attend)
    back_all = jax.vmap(attend_back)
    for tick in range(TICKS):
        outgoing = []
        for s in range(sections):
            if tick == 0:
                delta = arriving[s]
            elif s == 0:
                delta = first_delta[tick - 1]
            else:
                delta = previous[s - 1]
            micro = tick - s + sections - 1
            slots = sample_index[micro]
            old_in = state_in[s][replicas, slots]
            inputs = (old_in.astype(jnp.float32) + scale_full[s] * delta.astype(jnp.float32)).astype(jnp.bfloat16)
            state_in[s] = state_in[s].at[replicas, slots].set(inputs)
            normed = normalize(inputs, norm_gain[s])
            flat = normed.reshape(-1, D)
            query = jnp.dot(flat, w_query[s], preferred_element_type=jnp.float32).astype(jnp.bfloat16).reshape(BATCH, SEQ, -1)
            key_in = jnp.dot(flat, w_key[s], preferred_element_type=jnp.float32).astype(jnp.bfloat16).reshape(BATCH, SEQ, -1)
            value_in = jnp.dot(flat, w_value[s], preferred_element_type=jnp.float32).astype(jnp.bfloat16).reshape(BATCH, SEQ, -1)
            mixed, probs, rounded = attend_all(query, key_in, value_in)
            mixed_rows = mixed.reshape(-1, HQ * HD)
            total = jnp.zeros((BATCH * SEQ, D), jnp.float32)
            for part in range(N_TENSOR):
                piece = jnp.dot(mixed_rows[:, part * width:(part + 1) * width], w_out[s][part * width:(part + 1) * width], preferred_element_type=jnp.float32)
                total = total + lax.optimization_barrier(piece.astype(jnp.bfloat16)).astype(jnp.float32)
            output = (inputs.reshape(-1, D).astype(jnp.float32) + total).astype(jnp.bfloat16).reshape(BATCH, SEQ, D)
            old_out = state_out[s][replicas, slots]
            sent = jnp.clip((output.astype(jnp.float32) - old_out.astype(jnp.float32)) * inverse_full[s + 1], -qmax, qmax)
            sent = lax.optimization_barrier(sent.astype(jnp.bfloat16))
            renewed = (old_out.astype(jnp.float32) + scale_full[s + 1] * sent.astype(jnp.float32)).astype(jnp.bfloat16)
            state_out[s] = state_out[s].at[replicas, slots].set(renewed)
            outgoing.append(sent)
            upstream = out_grad[s, tick]
            d_mixed = lax.dot_general(upstream.reshape(-1, D), w_out[s], (((1,), (1,)), ((), ())), preferred_element_type=jnp.float32)
            d_mixed = d_mixed.astype(jnp.bfloat16).reshape(BATCH, SEQ, -1)
            d_query, d_value = back_all(query, key_in, value_in, probs, rounded, d_mixed)
            saved[s].append((normed, d_query, d_value))
        previous = outgoing
    grads_q, grads_v, copies = ([], [], [])
    for s in range(sections):
        normed = jnp.stack([item[0] for item in saved[s]])
        d_query = jnp.stack([item[1] for item in saved[s]])
        d_value = jnp.stack([item[2] for item in saved[s]])
        grads_q.append(replica_sum(normed, d_query))
        grads_v.append(replica_sum(normed, d_value))
        copies.append(jnp.stack([state_in[s].reshape(SAMPLES, SEQ, D), state_out[s].reshape(SAMPLES, SEQ, D)]))
    return (jnp.stack(copies), jnp.stack(grads_q), jnp.stack(grads_v))
```

```python
import jax
import jax.numpy as jnp
from jax import lax
from jax.sharding import Mesh, PartitionSpec as P

HQ = 32
HK = 4
HD = 128
QB = 128
SEQ = 128

eps_norm = 1e-05
qmax = 7.0
f32 = jnp.float32
bf16 = jnp.bfloat16


def normalize(inputs, gain):
    values = inputs.astype(f32)
    square = jnp.mean(values * values, axis=-1, keepdims=True)
    return (values * lax.rsqrt(square + eps_norm) * gain).astype(bf16)


def heads(rows, units):
    return rows.reshape(units, SEQ, -1, HD)


def softmax_probs(query, key_in, units):
    scores = (
        jnp.einsum(
            "usgd,utd->ugst",
            heads(query, units),
            key_in.reshape(units, SEQ, HD),
            preferred_element_type=f32,
        )
        * HD ** (-0.5)
    )
    causal = jnp.arange(SEQ)[:, None] >= jnp.arange(SEQ)[None, :]
    return jax.nn.softmax(jnp.where(causal, scores, -1e30), axis=-1)


def attend(query, key_in, value_in, units):
    rounded = softmax_probs(query, key_in, units).astype(bf16)
    mixed = jnp.einsum(
        "ugst,utd->usgd", rounded, value_in.reshape(units, SEQ, HD), preferred_element_type=f32
    )
    return mixed.reshape(units * SEQ, -1).astype(bf16)


def attend_back(query, key_in, value_in, d_mixed, units):
    probs = softmax_probs(query, key_in, units)
    d_heads = heads(d_mixed, units)
    d_probs = jnp.einsum(
        "usgd,utd->ugst", d_heads, value_in.reshape(units, SEQ, HD), preferred_element_type=f32
    )
    d_scores = probs * (d_probs - jnp.sum(d_probs * probs, axis=-1, keepdims=True)) * HD ** (-0.5)
    d_query = jnp.einsum(
        "ugst,utd->usgd",
        d_scores.astype(bf16),
        key_in.reshape(units, SEQ, HD),
        preferred_element_type=f32,
    )
    d_value = jnp.einsum("ugst,usgd->utd", probs.astype(bf16), d_heads, preferred_element_type=f32)
    return (
        d_query.reshape(units * SEQ, -1).astype(bf16),
        d_value.reshape(units * SEQ, HD).astype(bf16),
    )


def pick(state, slot):
    return jnp.where(slot == 0, state[0], state[1])


def put(state, slot, new, active=True):
    mask = (jnp.arange(2) == slot) & active
    return jnp.where(mask[:, None, None], new[None], state)


def pass_on(shard):
    return lax.ppermute(shard, "section", [(0, 1)])


def gather_tensor(shard):
    return lax.all_gather(shard, "tensor", axis=1, tiled=True)


def reduce_tensor(partial):
    rows = partial.shape[0]
    parts = partial.reshape(rows, 4, -1).swapaxes(0, 1)
    got = lax.all_to_all(parts, "tensor", split_axis=0, concat_axis=0, tiled=True)
    return jnp.sum(got.astype(f32), axis=0)


def on_device(
    boundary_copies,
    arriving,
    first_delta,
    sample_index,
    exponents,
    norm_gain,
    w_query,
    w_key,
    w_value,
    w_out,
    out_grad,
):
    section = lax.axis_index("section")
    first = section == 0
    packed = jnp.concatenate([w_query[0], w_key[0], w_value[0], w_out[0].T], axis=1)
    full = lax.all_gather(packed, ("y", "x"), axis=0, tiled=True)
    full_qkv = full[:, :1280]
    full_o = full[:, 1280:]

    power = exponents.astype(f32)
    scale_full = jnp.repeat(jnp.exp2(power), QB, axis=1)
    inverse_full = jnp.repeat(jnp.exp2(-power), QB, axis=1)
    scale_in = jnp.where(first, scale_full[0], scale_full[1])
    scale_next = jnp.where(first, scale_full[1], scale_full[2])
    inverse_next = jnp.where(first, inverse_full[1], inverse_full[2])
    gain = norm_gain[0]
    slots = sample_index[:, 0]
    slot = [jnp.where(first, slots[k + 1], slots[k]) for k in range(3)]

    def receive(state, at, delta):
        return (pick(state, at).astype(f32) + scale_in * delta.astype(f32)).astype(bf16)

    def deliver(state, at, inputs, summed):
        output = (inputs.astype(f32) + summed).astype(bf16)
        old = pick(state, at)
        sent = jnp.clip(
            (output.astype(f32) - old.astype(f32)) * inverse_next, -qmax, qmax
        ).astype(bf16)
        renewed = (old.astype(f32) + scale_next * sent.astype(f32)).astype(bf16)
        return sent, renewed

    state_in, state_out = boundary_copies[0, 0], boundary_copies[0, 1]
    xa0 = receive(state_in, slot[0], arriving[0, 0])
    state_in = put(state_in, slot[0], xa0)
    xa1 = receive(state_in, slot[1], first_delta[0, 0])
    state_in = put(state_in, slot[1], xa1, first)
    xa = jnp.concatenate([xa0, xa1], 0)
    normed_a = normalize(gather_tensor(xa), gain)
    qkv_a = jnp.dot(normed_a, full_qkv, preferred_element_type=f32).astype(bf16)
    mixed_a = attend(qkv_a[:, :1024], qkv_a[:, 1024:1152], qkv_a[:, 1152:], 2)
    partial_a = lax.dot_general(
        mixed_a, full_o, (((1,), (1,)), ((), ())), preferred_element_type=f32
    ).astype(bf16)
    summed_a = reduce_tensor(partial_a)
    sent_a0, renewed = deliver(state_out, slot[0], xa0, summed_a[:SEQ])
    state_out = put(state_out, slot[0], renewed)
    sent_a1, renewed = deliver(state_out, slot[1], xa1, summed_a[SEQ:])
    state_out = put(state_out, slot[1], renewed, first)
    passed = pass_on(jnp.concatenate([sent_a0, sent_a1], 0))

    at_b0 = jnp.where(first, slot[2], slot[1])
    xb0 = receive(state_in, at_b0, jnp.where(first, first_delta[1, 0], passed[:SEQ]))
    state_in = put(state_in, at_b0, xb0)
    xb1 = receive(state_in, slot[2], passed[SEQ:])
    state_in = put(state_in, slot[2], xb1, ~first)
    xb = jnp.concatenate([xb0, xb1], 0)
    normed_b = normalize(gather_tensor(xb), gain)
    qkv_b = jnp.dot(normed_b, full_qkv, preferred_element_type=f32).astype(bf16)
    mixed_b = attend(qkv_b[:, :1024], qkv_b[:, 1024:1152], qkv_b[:, 1152:], 2)
    partial_b = lax.dot_general(
        mixed_b, full_o, (((1,), (1,)), ((), ())), preferred_element_type=f32
    ).astype(bf16)
    summed_b = reduce_tensor(partial_b)
    _, renewed = deliver(state_out, at_b0, xb0, summed_b[:SEQ])
    state_out = put(state_out, at_b0, renewed)
    _, renewed = deliver(state_out, slot[2], xb1, summed_b[SEQ:])
    state_out = put(state_out, slot[2], renewed, ~first)

    up = out_grad[0, :, 0].reshape(3 * SEQ, -1)
    d_mixed = jnp.dot(up, full_o, preferred_element_type=f32).astype(bf16)
    d_mixed = jnp.concatenate(
        [
            d_mixed[:SEQ],
            jnp.where(first, d_mixed[SEQ : 2 * SEQ], d_mixed[2 * SEQ :]),
            jnp.where(first, d_mixed[2 * SEQ :], d_mixed[SEQ : 2 * SEQ]),
        ],
        0,
    )

    def three(a, b):
        return jnp.concatenate([a[:SEQ], jnp.where(first, a[SEQ:], b[SEQ:]), b[:SEQ]], 0)

    qkv = three(qkv_a, qkv_b)
    normed = three(normed_a, normed_b)
    d_query, d_value = attend_back(qkv[:, :1024], qkv[:, 1024:1152], qkv[:, 1152:], d_mixed, 3)
    d_rows = jnp.concatenate([d_query, d_value], 1)
    term = lax.dot_general(
        normed, d_rows, (((0,), (0,)), ((), ())), preferred_element_type=f32
    ).astype(bf16)
    grad = lax.psum_scatter(term, ("y", "x"), scatter_dimension=0, tiled=True)
    copies_new = jnp.stack([state_in, state_out])[None]
    return (copies_new, grad[None, :, :1024], grad[None, :, 1024:])


def solution(mesh):
    shape = dict(mesh.shape)
    grid = Mesh(
        mesh.devices.reshape(shape["section"], 4, shape["dp"] // 4, shape["tensor"]),
        ("section", "y", "x", "tensor"),
    )
    dp = ("y", "x")
    return jax.shard_map(
        on_device,
        mesh=grid,
        in_specs=(
            P("section", None, dp, None, "tensor"),
            P("section", dp, None, "tensor"),
            P(None, dp, None, "tensor"),
            P(None, dp),
            P(None, "tensor"),
            P("section", None),
            P("section", dp, "tensor"),
            P("section", dp, "tensor"),
            P("section", dp, "tensor"),
            P("section", "tensor", dp),
            P("section", None, dp, None, None),
        ),
        out_specs=(
            P("section", None, dp, None, "tensor"),
            P("section", dp, "tensor"),
            P("section", dp, "tensor"),
        ),
        check_vma=False,
    )
```

```python
import jax
import jax.numpy as jnp
from jax import lax
from jax.experimental import pallas as pl
from jax.experimental.pallas import tpu as pltpu
from jax.sharding import Mesh, PartitionSpec as P

HQ = 32
HK = 4
HD = 128
QB = 128
SEQ = 128

eps_norm = 1e-05
qmax = 7.0
f32 = jnp.float32
bf16 = jnp.bfloat16


def normalize(inputs, gain):
    values = inputs.astype(f32)
    square = jnp.mean(values * values, axis=-1, keepdims=True)
    return (values * lax.rsqrt(square + eps_norm) * gain).astype(bf16)


GROUP = HQ // HK
NT = (((1,), (1,)), ((), ()))
TN = (((0,), (0,)), ((), ()))


def stacked(rows):
    return jnp.concatenate([rows[:, h * HD : (h + 1) * HD] for h in range(GROUP)], axis=0)


def side_by_side(rows):
    return jnp.concatenate([rows[h * SEQ : (h + 1) * SEQ] for h in range(GROUP)], axis=1)


def probs_of(query, key_in):
    scores = lax.dot_general(query, key_in, NT, preferred_element_type=f32) * HD ** (-0.5)
    at = lax.broadcasted_iota(jnp.int32, scores.shape, 0) % SEQ
    key_at = lax.broadcasted_iota(jnp.int32, scores.shape, 1)
    scores = jnp.where(at >= key_at, scores, -1e30)
    weight = jnp.exp(scores - jnp.max(scores, axis=-1, keepdims=True))
    return weight / jnp.sum(weight, axis=-1, keepdims=True)


def attend_kernel(qkv_ref, mixed_ref):
    wide = GROUP * HD
    probs = probs_of(stacked(qkv_ref[:, :wide]), qkv_ref[:, wide : wide + HD])
    mixed = jnp.dot(
        probs.astype(bf16), qkv_ref[:, wide + HD :], preferred_element_type=f32
    ).astype(bf16)
    mixed_ref[...] = side_by_side(mixed)


def attend_back_kernel(qkv_ref, d_mixed_ref, out_ref):
    wide = GROUP * HD
    key_in = qkv_ref[:, wide : wide + HD]
    probs = probs_of(stacked(qkv_ref[:, :wide]), key_in)
    d_rows = stacked(d_mixed_ref[...])
    d_probs = lax.dot_general(d_rows, qkv_ref[:, wide + HD :], NT, preferred_element_type=f32)
    d_scores = (
        probs * (d_probs - jnp.sum(d_probs * probs, axis=-1, keepdims=True)) * HD ** (-0.5)
    )
    d_query = jnp.dot(d_scores.astype(bf16), key_in, preferred_element_type=f32).astype(bf16)
    d_value = lax.dot_general(probs.astype(bf16), d_rows, TN, preferred_element_type=f32)
    out_ref[:, :wide] = side_by_side(d_query)
    out_ref[:, wide:] = d_value.astype(bf16)


def attend(qkv):
    rows = qkv.shape[0]
    return pl.pallas_call(
        attend_kernel,
        grid=(rows // SEQ,),
        in_specs=[pl.BlockSpec((SEQ, (GROUP + 2) * HD), lambda u: (u, 0))],
        out_specs=pl.BlockSpec((SEQ, GROUP * HD), lambda u: (u, 0)),
        out_shape=jax.ShapeDtypeStruct((rows, GROUP * HD), bf16),
        compiler_params=pltpu.CompilerParams(vmem_limit_bytes=32 * 1024 * 1024),
        cost_estimate=pl.CostEstimate(
            flops=rows * SEQ * GROUP * HD * 4,
            bytes_accessed=rows * 2304 * 2,
            transcendentals=rows * SEQ * GROUP,
        ),
        name="attend",
    )(qkv)


def attend_back(qkv, d_mixed):
    rows = qkv.shape[0]
    return pl.pallas_call(
        attend_back_kernel,
        grid=(rows // SEQ,),
        in_specs=[
            pl.BlockSpec((SEQ, (GROUP + 2) * HD), lambda u: (u, 0)),
            pl.BlockSpec((SEQ, GROUP * HD), lambda u: (u, 0)),
        ],
        out_specs=pl.BlockSpec((SEQ, (GROUP + 1) * HD), lambda u: (u, 0)),
        out_shape=jax.ShapeDtypeStruct((rows, (GROUP + 1) * HD), bf16),
        compiler_params=pltpu.CompilerParams(vmem_limit_bytes=32 * 1024 * 1024),
        cost_estimate=pl.CostEstimate(
            flops=rows * SEQ * GROUP * HD * 8,
            bytes_accessed=rows * 3456 * 2,
            transcendentals=rows * SEQ * GROUP,
        ),
        name="attend_back",
    )(qkv, d_mixed)


def around(shard, axis, by):
    return lax.ppermute(shard, axis, [(i, (i + by) % 4) for i in range(4)])


def from_first(shard, by, to_section):
    return lax.ppermute(
        shard, ("section", "tensor"), [(i, 4 * to_section + (i + by) % 4) for i in range(4)]
    )


def ring(shard, axis, at):
    me = lax.axis_index(axis)
    half = shard.shape[0] // 2
    left = around(shard, axis, 1)
    right = around(shard, axis, -1)
    far_a = around(left[:half], axis, 1)
    far_b = around(right[half:], axis, -1)
    out = jnp.zeros(shard.shape[:at] + (4,) + shard.shape[at:], shard.dtype)

    def place(out, piece, index, offset=0):
        start = [0] * out.ndim
        if offset:
            start[0 if at else 1] = offset
        start[at] = index
        return lax.dynamic_update_slice(out, jnp.expand_dims(piece, at), start)

    out = place(out, shard, me)
    out = place(out, left, (me + 3) % 4)
    out = place(out, right, (me + 1) % 4)
    out = place(out, far_a, (me + 2) % 4)
    return place(out, far_b, (me + 2) % 4, half), left


def pick(state, slot):
    return jnp.where(slot == 0, state[0], state[1])


def put(state, slot, new, active=True):
    mask = (jnp.arange(2) == slot) & active
    return jnp.where(mask[:, None, None], new[None], state)


def on_device(
    boundary_copies,
    arriving,
    first_delta,
    sample_index,
    exponents,
    norm_gain,
    w_query,
    w_key,
    w_value,
    w_out,
    out_grad,
):
    first = lax.axis_index("section") == 0
    z = lax.axis_index("tensor")

    part_a, began = ring(w_query[0, :, :640], "x", 0)
    part_b, _ = ring(jnp.concatenate([w_query[0, :, 640:], w_key[0], w_value[0]], axis=1), "y", 0)
    out_shard, _ = lax.optimization_barrier((w_out[0].T, began))
    full_o = lax.all_gather(out_shard, ("y", "x"), axis=0, tiled=True)
    full_a, _ = ring(part_a, "y", 0)
    full_b, _ = ring(part_b, "x", 1)
    full_a = full_a.reshape(4096, 640)
    full_b = full_b.reshape(4096, 640)

    power = exponents.astype(f32)
    scale_full = jnp.repeat(jnp.exp2(power), QB, axis=1)
    inverse_full = jnp.repeat(jnp.exp2(-power), QB, axis=1)
    scale_in = jnp.where(first, scale_full[0], scale_full[1])
    scale_next = jnp.where(first, scale_full[1], scale_full[2])
    inverse_next = jnp.where(first, inverse_full[1], inverse_full[2])
    gain = norm_gain[0]
    slots = sample_index[:, 0]
    slot = [jnp.where(first, slots[k + 1], slots[k]) for k in range(3)]

    def receive(state, at, delta):
        return (pick(state, at).astype(f32) + scale_in * delta.astype(f32)).astype(bf16)

    def deliver(state, at, inputs, summed):
        output = (inputs.astype(f32) + summed).astype(bf16)
        old = pick(state, at)
        sent = jnp.clip(
            (output.astype(f32) - old.astype(f32)) * inverse_next, -qmax, qmax
        ).astype(bf16)
        step = scale_next * sent.astype(f32)
        return step.astype(bf16), (old.astype(f32) + step).astype(bf16)

    def project(normed):
        return jnp.concatenate(
            [
                jnp.dot(normed, full_a, preferred_element_type=f32).astype(bf16),
                jnp.dot(normed, full_b, preferred_element_type=f32).astype(bf16),
            ],
            axis=1,
        )

    state_in, state_out = boundary_copies[0, 0], boundary_copies[0, 1]
    x0 = receive(state_in, slot[0], arriving[0, 0])
    state_in = put(state_in, slot[0], x0)
    x1 = receive(state_in, slot[1], first_delta[0, 0])
    state_1 = put(state_in, slot[1], x1)
    x2 = receive(state_1, slot[2], first_delta[1, 0])
    state_2 = put(state_1, slot[2], x2)
    known = jnp.concatenate(
        [jnp.where(first, x0, state_in[0]), jnp.where(first, x1, state_in[1]), x2], 0
    )
    known = lax.all_to_all(
        jnp.broadcast_to(known[None], (4,) + known.shape),
        "tensor",
        split_axis=0,
        concat_axis=0,
        tiled=True,
    )
    known = known.swapaxes(0, 1).reshape(3, SEQ, -1)

    whole_a = jnp.concatenate(
        [jnp.where(first | (slot[0] == 0), known[0], known[1]), known[1]], 0
    )
    normed_a = normalize(whole_a, gain)
    qkv_a = project(normed_a)
    mixed_a = attend(qkv_a)
    pieces = {}
    for by in (2, 1, 3, 0):
        rows = lax.dynamic_slice_in_dim(full_o, ((z + by) % 4) * 1024, 1024, 0)
        piece = lax.dot_general(mixed_a, rows, NT, preferred_element_type=f32).astype(bf16)
        pieces[by] = piece if by == 0 else from_first(piece, by, 0)
    summed = sum(pieces[by].astype(f32) for by in range(4))
    step_0, renewed = deliver(state_out, slot[0], x0, summed[:SEQ])
    out_1 = put(state_out, slot[0], renewed)
    step_1, renewed = deliver(out_1, slot[1], x1, summed[SEQ:])
    out_2 = put(out_1, slot[1], renewed)
    steps = jnp.concatenate([step_0, step_1], 0)
    got = [from_first(steps, by, 1) for by in range(4)]

    arrived = jnp.zeros((2 * SEQ, 4, 1024), bf16)
    for by in range(4):
        arrived = lax.dynamic_update_slice(arrived, got[by][:, None], (0, (z + 4 - by) % 4, 0))
    arrived = arrived.reshape(2, SEQ, -1)

    def added(state, at, step):
        return (pick(state, at).astype(f32) + step.astype(f32)).astype(bf16)

    whole_1 = added(known, slot[1], arrived[0])
    whole_2 = added(put(known[:2], slot[1], whole_1), slot[2], arrived[1])
    whole_b = jnp.concatenate([jnp.where(first, known[2], whole_1), whole_2], 0)
    normed_b = normalize(whole_b, gain)
    qkv_b = project(normed_b)
    mixed_b = attend(qkv_b)
    y1 = added(state_in, slot[1], got[0][:SEQ])
    after_1 = put(state_in, slot[1], y1)
    y2 = added(after_1, slot[2], got[0][SEQ:])
    new_in = jnp.where(first, state_2, put(after_1, slot[2], y2))

    up = out_grad[0, :, 0].reshape(3 * SEQ, -1)
    d_mixed = jnp.dot(up, full_o, preferred_element_type=f32).astype(bf16)
    d_a = attend_back(qkv_a, d_mixed[: 2 * SEQ])
    d_mixed_b = jnp.concatenate(
        [jnp.where(first, d_mixed[2 * SEQ :], d_mixed[SEQ : 2 * SEQ]), d_mixed[2 * SEQ :]], 0
    )
    d_b = attend_back(qkv_b, d_mixed_b)

    def three(a, b):
        return jnp.concatenate([a[:SEQ], jnp.where(first, a[SEQ:], b[SEQ:]), b[:SEQ]], 0)

    term = lax.dot_general(
        three(normed_a, normed_b), three(d_a, d_b), TN, preferred_element_type=f32
    ).astype(bf16)
    grad = lax.psum_scatter(term, ("y", "x"), scatter_dimension=0, tiled=True)

    mixed_f = jnp.concatenate([jnp.where(first, mixed_b[:SEQ], mixed_a[:SEQ]), mixed_b], 0)
    mixed_f, _ = lax.optimization_barrier((mixed_f, term))
    partial = lax.dot_general(mixed_f, full_o, NT, preferred_element_type=f32).astype(bf16)
    parts = partial.reshape(3 * SEQ, 4, -1).swapaxes(0, 1)
    parts = lax.all_to_all(parts, "tensor", split_axis=0, concat_axis=0, tiled=True)
    summed = jnp.sum(parts.astype(f32), axis=0)
    _, renewed = deliver(out_2, slot[2], x2, summed[:SEQ])
    new_out_first = put(out_2, slot[2], renewed)
    _, renewed = deliver(state_out, slot[0], x0, summed[:SEQ])
    out_1 = put(state_out, slot[0], renewed)
    _, renewed = deliver(out_1, slot[1], y1, summed[SEQ : 2 * SEQ])
    out_1 = put(out_1, slot[1], renewed)
    _, renewed = deliver(out_1, slot[2], y2, summed[2 * SEQ :])
    new_out = jnp.where(first, new_out_first, put(out_1, slot[2], renewed))

    copies_new = jnp.stack([new_in, new_out])[None]
    return (copies_new, grad[None, :, :1024], grad[None, :, 1024:])


def solution(mesh):
    shape = dict(mesh.shape)
    grid = Mesh(
        mesh.devices.reshape(shape["section"], 4, shape["dp"] // 4, shape["tensor"]),
        ("section", "y", "x", "tensor"),
    )
    dp = ("y", "x")
    return jax.shard_map(
        on_device,
        mesh=grid,
        in_specs=(
            P("section", None, dp, None, "tensor"),
            P("section", dp, None, "tensor"),
            P(None, dp, None, "tensor"),
            P(None, dp),
            P(None, "tensor"),
            P("section", None),
            P("section", dp, "tensor"),
            P("section", dp, "tensor"),
            P("section", dp, "tensor"),
            P("section", "tensor", dp),
            P("section", None, dp, None, None),
        ),
        out_specs=(
            P("section", None, dp, None, "tensor"),
            P("section", dp, "tensor"),
            P("section", dp, "tensor"),
        ),
        check_vma=False,
    )
```

```python
import functools

import jax
import jax.numpy as jnp
from jax import lax
from jax.experimental import pallas as pl
from jax.experimental.pallas import tpu as pltpu
from jax.sharding import Mesh, PartitionSpec as P

HQ = 32
HK = 4
HD = 128
QB = 128
SEQ = 128

eps_norm = 1e-05
qmax = 7.0
f32 = jnp.float32
bf16 = jnp.bfloat16


GROUP = HQ // HK
NT = (((1,), (1,)), ((), ()))
TN = (((0,), (0,)), ((), ()))


def stacked(rows):
    return jnp.concatenate([rows[:, h * HD : (h + 1) * HD] for h in range(GROUP)], axis=0)


def side_by_side(rows):
    return jnp.concatenate([rows[h * SEQ : (h + 1) * SEQ] for h in range(GROUP)], axis=1)


def probs_of(query, key_in):
    scores = lax.dot_general(query, key_in, NT, preferred_element_type=f32) * HD ** (-0.5)
    at = lax.broadcasted_iota(jnp.int32, scores.shape, 0) % SEQ
    key_at = lax.broadcasted_iota(jnp.int32, scores.shape, 1)
    scores = jnp.where(at >= key_at, scores, -1e30)
    weight = jnp.exp(scores - jnp.max(scores, axis=-1, keepdims=True))
    return weight / jnp.sum(weight, axis=-1, keepdims=True)


def attend_unit(qkv):
    wide = GROUP * HD
    probs = probs_of(stacked(qkv[:, :wide]), qkv[:, wide : wide + HD])
    mixed = jnp.dot(probs.astype(bf16), qkv[:, wide + HD :], preferred_element_type=f32)
    return side_by_side(mixed.astype(bf16))


def attend_back_kernel(qkv_ref, d_mixed_ref, out_ref):
    wide = GROUP * HD
    key_in = qkv_ref[:, wide : wide + HD]
    probs = probs_of(stacked(qkv_ref[:, :wide]), key_in)
    d_rows = stacked(d_mixed_ref[...])
    d_probs = lax.dot_general(d_rows, qkv_ref[:, wide + HD :], NT, preferred_element_type=f32)
    d_scores = (
        probs * (d_probs - jnp.sum(d_probs * probs, axis=-1, keepdims=True)) * HD ** (-0.5)
    )
    d_query = jnp.dot(d_scores.astype(bf16), key_in, preferred_element_type=f32).astype(bf16)
    d_value = lax.dot_general(probs.astype(bf16), d_rows, TN, preferred_element_type=f32)
    out_ref[:, :wide] = side_by_side(d_query)
    out_ref[:, wide:] = d_value.astype(bf16)


def attend_back(qkv, d_mixed):
    rows = qkv.shape[0]
    return pl.pallas_call(
        attend_back_kernel,
        grid=(rows // SEQ,),
        in_specs=[
            pl.BlockSpec((SEQ, (GROUP + 2) * HD), lambda u: (u, 0)),
            pl.BlockSpec((SEQ, GROUP * HD), lambda u: (u, 0)),
        ],
        out_specs=pl.BlockSpec((SEQ, (GROUP + 1) * HD), lambda u: (u, 0)),
        out_shape=jax.ShapeDtypeStruct((rows, (GROUP + 1) * HD), bf16),
        compiler_params=pltpu.CompilerParams(vmem_limit_bytes=32 * 1024 * 1024),
        cost_estimate=pl.CostEstimate(
            flops=rows * SEQ * GROUP * HD * 8,
            bytes_accessed=rows * 3456 * 2,
            transcendentals=rows * SEQ * GROUP,
        ),
        name="attend_back",
    )(qkv, d_mixed)


ROWS = 16
HALF = 640
ORDER = (0, 3, 1, 2)


def known_a(flags, known_ref, x_ref):
    from_0 = (flags[0] == 1) | (flags[1] == 0)

    def step(i, carry):
        at = pl.multiple_of(i * ROWS, ROWS)
        for j in range(4):
            one = known_ref[j, pl.ds(at, ROWS), :]
            two = known_ref[j, pl.ds(at + SEQ, ROWS), :]
            columns = slice(j * 1024, (j + 1) * 1024)
            x_ref[pl.ds(at, ROWS), columns] = jnp.where(from_0, one, two)
            x_ref[pl.ds(at + SEQ, ROWS), columns] = two
        return carry

    lax.fori_loop(0, SEQ // ROWS, step, 0)


def known_b(flags, known_ref, got_refs, x_ref):
    first = flags[0] == 1
    slot_1, slot_2 = flags[2], flags[3]

    def step(i, carry):
        at = pl.multiple_of(i * ROWS, ROWS)
        for by in range(4):
            j = lax.rem(flags[6] + 4 - by, 4)
            one = known_ref[j, pl.ds(at, ROWS), :].astype(f32)
            two = known_ref[j, pl.ds(at + SEQ, ROWS), :].astype(f32)
            third = known_ref[j, pl.ds(at + 2 * SEQ, ROWS), :]
            step_1 = got_refs[by][pl.ds(at, ROWS), :].astype(f32)
            step_2 = got_refs[by][pl.ds(at + SEQ, ROWS), :].astype(f32)
            x_1 = (jnp.where(slot_1 == 0, one, two) + step_1).astype(bf16)
            old = jnp.where(
                slot_1 == slot_2, x_1.astype(f32), jnp.where(slot_2 == 0, one, two)
            )
            columns = pl.ds(pl.multiple_of(j * 1024, 1024), 1024)
            x_ref[pl.ds(at, ROWS), columns] = jnp.where(first, third, x_1)
            x_ref[pl.ds(at + SEQ, ROWS), columns] = (old + step_2).astype(bf16)
        return carry

    lax.fori_loop(0, SEQ // ROWS, step, 0)


def project_kernel(stage, flags, gain_ref, known_ref, *refs):
    got_refs, refs = refs[: 4 * stage], refs[4 * stage :]
    pieces, refs = refs[:16], refs[16:]
    normed_ref, qkv_ref, mixed_ref, held, sems = refs
    copies = []
    for i in range(16):
        half, at, pair = i // 8, (i // 2) % 4, i % 2
        copies.append(
            pltpu.make_async_copy(pieces[i], held.at[half, at, pl.ds(2 * pair, 2)], sems.at[i])
        )
        copies[-1].start()
    if stage:
        known_b(flags, known_ref, got_refs, normed_ref)
    else:
        known_a(flags, known_ref, normed_ref)

    def normalize(i, carry):
        rows = pl.ds(pl.multiple_of(i * ROWS, ROWS), ROWS)
        values = normed_ref[rows, :].astype(f32)
        square = jnp.mean(values * values, axis=-1, keepdims=True)
        normed_ref[rows, :] = (values * lax.rsqrt(square + eps_norm) * gain_ref[...]).astype(bf16)
        return carry

    lax.fori_loop(0, 2 * SEQ // ROWS, normalize, 0)
    totals = [None, None]
    for at in range(4):
        for half in range(2):
            lhs = []
            for block in range(4):
                along, across = ORDER[at], ORDER[block]
                dy, dx = (along, across) if half == 0 else (across, along)
                row = lax.rem(flags[5] + dy, 4) * 4 + lax.rem(flags[4] + dx, 4)
                lhs.append(normed_ref[:, pl.ds(pl.multiple_of(row * 256, 256), 256)])
            for pair in range(2):
                copies[half * 8 + at * 2 + pair].wait()
            part = jnp.dot(
                jnp.concatenate(lhs, axis=1),
                held[half, at].reshape(1024, HALF),
                preferred_element_type=f32,
            )
            totals[half] = part if totals[half] is None else totals[half] + part
    for half in range(2):
        qkv_ref[:, half * HALF : (half + 1) * HALF] = totals[half].astype(bf16)
    for unit in range(2):
        rows = slice(unit * SEQ, (unit + 1) * SEQ)
        mixed_ref[rows, :] = attend_unit(qkv_ref[rows, :])


def project(stage, flags, gain, known, got, pieces):
    vmem = pl.BlockSpec(memory_space=pltpu.VMEM)
    rows = 2 * SEQ
    return pl.pallas_call(
        functools.partial(project_kernel, stage),
        in_specs=[pl.BlockSpec(memory_space=pltpu.SMEM)]
        + [vmem] * (2 + len(got))
        + [pl.BlockSpec(memory_space=pl.ANY)] * 16,
        out_specs=[vmem] * 3,
        out_shape=[
            jax.ShapeDtypeStruct((rows, 4096), bf16),
            jax.ShapeDtypeStruct((rows, 2 * HALF), bf16),
            jax.ShapeDtypeStruct((rows, GROUP * HD), bf16),
        ],
        scratch_shapes=[
            pltpu.VMEM((2, 4, 4, 256, HALF), bf16),
            pltpu.SemaphoreType.DMA((16,)),
        ],
        compiler_params=pltpu.CompilerParams(vmem_limit_bytes=40 * 1024 * 1024),
        cost_estimate=pl.CostEstimate(
            flops=2 * rows * 4096 * 2 * HALF, bytes_accessed=18 * 2**20, transcendentals=rows * 1024
        ),
        name=("project_a", "project_b")[stage],
    )(flags, gain, known, *got, *pieces)


def around(shard, axis, by):
    return lax.ppermute(shard, axis, [(i, (i + by) % 4) for i in range(4)])


def from_first(shard, by, to_section):
    return lax.ppermute(
        shard, ("section", "tensor"), [(i, 4 * to_section + (i + by) % 4) for i in range(4)]
    )


def near_and_far(shard, axis):
    half = shard.shape[0] // 2
    before = around(shard, axis, 1)
    after = around(shard, axis, -1)
    far = [around(before[:half], axis, 1), around(after[half:], axis, -1)]
    return before, after, far


def gathered(shard, axis, then):
    before, after, far = near_and_far(shard, axis)
    near = jnp.stack([shard, before])
    other = jnp.stack([after, jnp.concatenate(far, 0)])
    near_before, near_after = around(near, then, 1), around(near, then, -1)
    other_before, other_after = around(other, then, 1), around(other, then, -1)
    near_far, other_far = around(near_before, then, 1), around(other_after, then, -1)
    return [near, other, near_before, other_before, near_after, other_after, near_far, other_far]


def pick(state, slot):
    return jnp.where(slot == 0, state[0], state[1])


def put(state, slot, new, active=True):
    mask = (jnp.arange(2) == slot) & active
    return jnp.where(mask[:, None, None], new[None], state)


def on_device(
    boundary_copies,
    arriving,
    first_delta,
    sample_index,
    exponents,
    norm_gain,
    w_query,
    w_key,
    w_value,
    w_out,
    out_grad,
):
    first = lax.axis_index("section") == 0
    z = lax.axis_index("tensor")

    full_o = lax.all_gather(w_out[0].T, ("y", "x"), axis=0, tiled=True)
    pieces = gathered(w_query[0, :, :HALF], "x", "y")
    pieces += gathered(
        jnp.concatenate([w_query[0, :, HALF:], w_key[0], w_value[0]], axis=1), "y", "x"
    )

    power = exponents.astype(f32)
    scale_full = jnp.repeat(jnp.exp2(power), QB, axis=1)
    inverse_full = jnp.repeat(jnp.exp2(-power), QB, axis=1)
    scale_in = jnp.where(first, scale_full[0], scale_full[1])
    scale_next = jnp.where(first, scale_full[1], scale_full[2])
    inverse_next = jnp.where(first, inverse_full[1], inverse_full[2])
    slots = sample_index[:, 0]
    slot = [jnp.where(first, slots[k + 1], slots[k]) for k in range(3)]

    def receive(state, at, delta):
        return (pick(state, at).astype(f32) + scale_in * delta.astype(f32)).astype(bf16)

    def deliver(state, at, inputs, summed):
        output = (inputs.astype(f32) + summed).astype(bf16)
        old = pick(state, at)
        sent = jnp.clip(
            (output.astype(f32) - old.astype(f32)) * inverse_next, -qmax, qmax
        ).astype(bf16)
        step = scale_next * sent.astype(f32)
        return step.astype(bf16), (old.astype(f32) + step).astype(bf16)

    state_in, state_out = boundary_copies[0, 0], boundary_copies[0, 1]
    x0 = receive(state_in, slot[0], arriving[0, 0])
    state_in = put(state_in, slot[0], x0)
    x1 = receive(state_in, slot[1], first_delta[0, 0])
    state_1 = put(state_in, slot[1], x1)
    x2 = receive(state_1, slot[2], first_delta[1, 0])
    state_2 = put(state_1, slot[2], x2)
    known = jnp.concatenate(
        [jnp.where(first, x0, state_in[0]), jnp.where(first, x1, state_in[1]), x2], 0
    )
    known = lax.all_to_all(
        jnp.broadcast_to(known[None], (4,) + known.shape),
        "tensor",
        split_axis=0,
        concat_axis=0,
        tiled=True,
    )

    flags = jnp.stack(
        [first.astype(jnp.int32), *slot, lax.axis_index("x"), lax.axis_index("y"), z]
    ).astype(jnp.int32)
    normed_a, qkv_a, mixed_a = project(0, flags, norm_gain, known, [], pieces)
    parts = {}
    for by in (2, 1, 3, 0):
        rows = lax.dynamic_slice_in_dim(full_o, ((z + by) % 4) * 1024, 1024, 0)
        piece = lax.dot_general(mixed_a, rows, NT, preferred_element_type=f32).astype(bf16)
        parts[by] = piece if by == 0 else from_first(piece, by, 0)
    summed = sum(parts[by].astype(f32) for by in range(4))
    step_0, renewed = deliver(state_out, slot[0], x0, summed[:SEQ])
    out_1 = put(state_out, slot[0], renewed)
    step_1, renewed = deliver(out_1, slot[1], x1, summed[SEQ:])
    out_2 = put(out_1, slot[1], renewed)
    steps = jnp.concatenate([step_0, step_1], 0)
    got = [from_first(steps, by, 1) for by in range(4)]

    def added(state, at, step):
        return (pick(state, at).astype(f32) + step.astype(f32)).astype(bf16)

    normed_b, qkv_b, mixed_b = project(1, flags, norm_gain, known, got, pieces)
    y1 = added(state_in, slot[1], got[0][:SEQ])
    after_1 = put(state_in, slot[1], y1)
    y2 = added(after_1, slot[2], got[0][SEQ:])
    new_in = jnp.where(first, state_2, put(after_1, slot[2], y2))

    up = out_grad[0, :, 0].reshape(3 * SEQ, -1)
    d_mixed = jnp.dot(up, full_o, preferred_element_type=f32).astype(bf16)
    d_a = attend_back(qkv_a, d_mixed[: 2 * SEQ])
    d_mixed_b = jnp.concatenate(
        [jnp.where(first, d_mixed[2 * SEQ :], d_mixed[SEQ : 2 * SEQ]), d_mixed[2 * SEQ :]], 0
    )
    d_b = attend_back(qkv_b, d_mixed_b)

    def three(a, b):
        return jnp.concatenate([a[:SEQ], jnp.where(first, a[SEQ:], b[SEQ:]), b[:SEQ]], 0)

    term = lax.dot_general(
        three(normed_a, normed_b), three(d_a, d_b), TN, preferred_element_type=f32
    ).astype(bf16)
    grad = lax.psum_scatter(term, ("y", "x"), scatter_dimension=0, tiled=True)

    mixed_f = jnp.concatenate([jnp.where(first, mixed_b[:SEQ], mixed_a[:SEQ]), mixed_b], 0)
    mixed_f, _ = lax.optimization_barrier((mixed_f, term))
    partial = lax.dot_general(mixed_f, full_o, NT, preferred_element_type=f32).astype(bf16)
    parts = partial.reshape(3 * SEQ, 4, -1).swapaxes(0, 1)
    parts = lax.all_to_all(parts, "tensor", split_axis=0, concat_axis=0, tiled=True)
    summed = jnp.sum(parts.astype(f32), axis=0)
    _, renewed = deliver(out_2, slot[2], x2, summed[:SEQ])
    new_out_first = put(out_2, slot[2], renewed)
    _, renewed = deliver(state_out, slot[0], x0, summed[:SEQ])
    out_1 = put(state_out, slot[0], renewed)
    _, renewed = deliver(out_1, slot[1], y1, summed[SEQ : 2 * SEQ])
    out_1 = put(out_1, slot[1], renewed)
    _, renewed = deliver(out_1, slot[2], y2, summed[2 * SEQ :])
    new_out = jnp.where(first, new_out_first, put(out_1, slot[2], renewed))

    copies_new = jnp.stack([new_in, new_out])[None]
    return (copies_new, grad[None, :, :1024], grad[None, :, 1024:])


def solution(mesh):
    shape = dict(mesh.shape)
    grid = Mesh(
        mesh.devices.reshape(shape["section"], 4, shape["dp"] // 4, shape["tensor"]),
        ("section", "y", "x", "tensor"),
    )
    dp = ("y", "x")
    return jax.shard_map(
        on_device,
        mesh=grid,
        in_specs=(
            P("section", None, dp, None, "tensor"),
            P("section", dp, None, "tensor"),
            P(None, dp, None, "tensor"),
            P(None, dp),
            P(None, "tensor"),
            P("section", None),
            P("section", dp, "tensor"),
            P("section", dp, "tensor"),
            P("section", dp, "tensor"),
            P("section", "tensor", dp),
            P("section", None, dp, None, None),
        ),
        out_specs=(
            P("section", None, dp, None, "tensor"),
            P("section", dp, "tensor"),
            P("section", dp, "tensor"),
        ),
        check_vma=False,
    )
```

```python
import functools

import jax
import jax.numpy as jnp
from jax import lax
from jax.experimental import pallas as pl
from jax.experimental.pallas import tpu as pltpu
from jax.sharding import Mesh, PartitionSpec as P

HQ = 32
HK = 4
HD = 128
QB = 128
SEQ = 128

eps_norm = 1e-05
qmax = 7.0
f32 = jnp.float32
bf16 = jnp.bfloat16


GROUP = HQ // HK
NT = (((1,), (1,)), ((), ()))
TN = (((0,), (0,)), ((), ()))


def stacked(rows):
    return jnp.concatenate([rows[:, h * HD : (h + 1) * HD] for h in range(GROUP)], axis=0)


def side_by_side(rows):
    return jnp.concatenate([rows[h * SEQ : (h + 1) * SEQ] for h in range(GROUP)], axis=1)


def probs_of(query, key_in):
    scores = lax.dot_general(query, key_in, NT, preferred_element_type=f32) * HD ** (-0.5)
    at = lax.broadcasted_iota(jnp.int32, scores.shape, 0) % SEQ
    key_at = lax.broadcasted_iota(jnp.int32, scores.shape, 1)
    scores = jnp.where(at >= key_at, scores, -1e30)
    weight = jnp.exp(scores - jnp.max(scores, axis=-1, keepdims=True))
    return weight / jnp.sum(weight, axis=-1, keepdims=True)


def attend_unit(qkv):
    wide = GROUP * HD
    probs = probs_of(stacked(qkv[:, :wide]), qkv[:, wide : wide + HD])
    mixed = jnp.dot(probs.astype(bf16), qkv[:, wide + HD :], preferred_element_type=f32)
    return side_by_side(mixed.astype(bf16))


def attend_back_kernel(qkv_ref, d_mixed_ref, out_ref):
    wide = GROUP * HD
    key_in = qkv_ref[:, wide : wide + HD]
    probs = probs_of(stacked(qkv_ref[:, :wide]), key_in)
    d_rows = stacked(d_mixed_ref[...])
    d_probs = lax.dot_general(d_rows, qkv_ref[:, wide + HD :], NT, preferred_element_type=f32)
    d_scores = (
        probs * (d_probs - jnp.sum(d_probs * probs, axis=-1, keepdims=True)) * HD ** (-0.5)
    )
    d_query = jnp.dot(d_scores.astype(bf16), key_in, preferred_element_type=f32).astype(bf16)
    d_value = lax.dot_general(probs.astype(bf16), d_rows, TN, preferred_element_type=f32)
    out_ref[:, :wide] = side_by_side(d_query)
    out_ref[:, wide:] = d_value.astype(bf16)


def attend_back(qkv, d_mixed):
    rows = qkv.shape[0]
    return pl.pallas_call(
        attend_back_kernel,
        grid=(rows // SEQ,),
        in_specs=[
            pl.BlockSpec((SEQ, (GROUP + 2) * HD), lambda u: (u, 0)),
            pl.BlockSpec((SEQ, GROUP * HD), lambda u: (u, 0)),
        ],
        out_specs=pl.BlockSpec((SEQ, (GROUP + 1) * HD), lambda u: (u, 0)),
        out_shape=jax.ShapeDtypeStruct((rows, (GROUP + 1) * HD), bf16),
        compiler_params=pltpu.CompilerParams(vmem_limit_bytes=32 * 1024 * 1024),
        cost_estimate=pl.CostEstimate(
            flops=rows * SEQ * GROUP * HD * 8,
            bytes_accessed=rows * 3456 * 2,
            transcendentals=rows * SEQ * GROUP,
        ),
        name="attend_back",
    )(qkv, d_mixed)


ROWS = 16
HALF = 640
ORDER = (0, 3, 1, 2)


def known_a(flags, known_ref, x_ref):
    from_0 = (flags[0] == 1) | (flags[1] == 0)

    def step(i, carry):
        at = pl.multiple_of(i * ROWS, ROWS)
        for j in range(4):
            one = known_ref[j, pl.ds(at, ROWS), :]
            two = known_ref[j, pl.ds(at + SEQ, ROWS), :]
            columns = slice(j * 1024, (j + 1) * 1024)
            x_ref[pl.ds(at, ROWS), columns] = jnp.where(from_0, one, two)
            x_ref[pl.ds(at + SEQ, ROWS), columns] = two
        return carry

    lax.fori_loop(0, SEQ // ROWS, step, 0)


def known_b(flags, known_ref, got_refs, x_ref):
    first = flags[0] == 1
    slot_1, slot_2 = flags[2], flags[3]

    def step(i, carry):
        at = pl.multiple_of(i * ROWS, ROWS)
        for by in range(4):
            j = lax.rem(flags[6] + 4 - by, 4)
            one = known_ref[j, pl.ds(at, ROWS), :].astype(f32)
            two = known_ref[j, pl.ds(at + SEQ, ROWS), :].astype(f32)
            third = known_ref[j, pl.ds(at + 2 * SEQ, ROWS), :]
            step_1 = got_refs[by][pl.ds(at, ROWS), :].astype(f32)
            step_2 = got_refs[by][pl.ds(at + SEQ, ROWS), :].astype(f32)
            x_1 = (jnp.where(slot_1 == 0, one, two) + step_1).astype(bf16)
            old = jnp.where(
                slot_1 == slot_2, x_1.astype(f32), jnp.where(slot_2 == 0, one, two)
            )
            columns = pl.ds(pl.multiple_of(j * 1024, 1024), 1024)
            x_ref[pl.ds(at, ROWS), columns] = jnp.where(first, third, x_1)
            x_ref[pl.ds(at + SEQ, ROWS), columns] = (old + step_2).astype(bf16)
        return carry

    lax.fori_loop(0, SEQ // ROWS, step, 0)


def normalize(gain_ref, x_ref):
    def step(i, carry):
        rows = pl.ds(pl.multiple_of(i * ROWS, ROWS), ROWS)
        values = x_ref[rows, :].astype(f32)
        square = jnp.mean(values * values, axis=-1, keepdims=True)
        x_ref[rows, :] = (values * lax.rsqrt(square + eps_norm) * gain_ref[...]).astype(bf16)
        return carry

    lax.fori_loop(0, 2 * SEQ // ROWS, step, 0)


def prepare_kernel(flags, gain_ref, known_ref, normed_ref):
    known_a(flags, known_ref, normed_ref)
    normalize(gain_ref, normed_ref)


VMEM = pl.BlockSpec(memory_space=pltpu.VMEM)
SMEM = pl.BlockSpec(memory_space=pltpu.SMEM)
ANY = pl.BlockSpec(memory_space=pl.ANY)
GRANT = pltpu.CompilerParams(vmem_limit_bytes=60 * 1024 * 1024)


def prepare(flags, gain, known):
    return pl.pallas_call(
        prepare_kernel,
        in_specs=[SMEM, VMEM, VMEM],
        out_specs=VMEM,
        out_shape=jax.ShapeDtypeStruct((2 * SEQ, 4096), bf16),
        compiler_params=pltpu.CompilerParams(vmem_limit_bytes=32 * 1024 * 1024),
        cost_estimate=pl.CostEstimate(flops=2**23, bytes_accessed=5 * 2**20, transcendentals=0),
        name="prepare",
    )(flags, gain, known)


def project_kernel(flags, pieces, normed_ref, qkv_ref, mixed_ref, held, sems, begin):
    copies = []
    for i in range(16):
        half, at, pair = i // 8, (i // 2) % 4, i % 2
        copies.append(
            pltpu.make_async_copy(pieces[i], held.at[half, at, pl.ds(2 * pair, 2)], sems.at[i])
        )
        copies[-1].start()
    begin()
    totals = [None, None]
    for at in range(4):
        for half in range(2):
            lhs = []
            for block in range(4):
                along, across = ORDER[at], ORDER[block]
                dy, dx = (along, across) if half == 0 else (across, along)
                row = lax.rem(flags[5] + dy, 4) * 4 + lax.rem(flags[4] + dx, 4)
                lhs.append(normed_ref[:, pl.ds(pl.multiple_of(row * 256, 256), 256)])
            for pair in range(2):
                copies[half * 8 + at * 2 + pair].wait()
            part = jnp.dot(
                jnp.concatenate(lhs, axis=1),
                held[half, at].reshape(1024, HALF),
                preferred_element_type=f32,
            )
            totals[half] = part if totals[half] is None else totals[half] + part
    for half in range(2):
        qkv_ref[:, half * HALF : (half + 1) * HALF] = totals[half].astype(bf16)
    for unit in range(2):
        rows = slice(unit * SEQ, (unit + 1) * SEQ)
        mixed_ref[rows, :] = attend_unit(qkv_ref[rows, :])


def project_a_kernel(flags, normed_ref, *refs):
    pieces, (qkv_ref, mixed_ref, held, sems) = refs[:16], refs[16:]
    project_kernel(flags, pieces, normed_ref, qkv_ref, mixed_ref, held, sems, lambda: None)


def project_b_kernel(flags, gain_ref, known_ref, *refs):
    got_refs, pieces = refs[:4], refs[4:20]
    normed_ref, qkv_ref, mixed_ref, held, sems = refs[20:]

    def begin():
        known_b(flags, known_ref, got_refs, normed_ref)
        normalize(gain_ref, normed_ref)

    project_kernel(flags, pieces, normed_ref, qkv_ref, mixed_ref, held, sems, begin)


def project_call(kernel, name, operands, pieces, with_normed):
    rows = 2 * SEQ
    shapes = [
        jax.ShapeDtypeStruct((rows, 4096), bf16),
        jax.ShapeDtypeStruct((rows, 2 * HALF), bf16),
        jax.ShapeDtypeStruct((rows, GROUP * HD), bf16),
    ][0 if with_normed else 1 :]
    return pl.pallas_call(
        kernel,
        in_specs=[SMEM] + [VMEM] * (len(operands) - 1) + [ANY] * 16,
        out_specs=[VMEM] * len(shapes),
        out_shape=shapes,
        scratch_shapes=[
            pltpu.VMEM((2, 4, 4, 256, HALF), bf16),
            pltpu.SemaphoreType.DMA((16,)),
        ],
        compiler_params=GRANT,
        cost_estimate=pl.CostEstimate(
            flops=2 * rows * 4096 * 2 * HALF, bytes_accessed=18 * 2**20, transcendentals=rows * 1024
        ),
        name=name,
    )(*operands, *pieces)


def spread_kernel(flags, mixed_ref, full_o_ref, *refs):
    outs, (held, sems) = refs[:4], refs[4:]
    copies = []
    for i, by in enumerate((2, 1, 3, 0)):
        row = pl.multiple_of(lax.rem(flags[6] + by, 4) * 1024, 1024)
        copies.append(
            pltpu.make_async_copy(full_o_ref.at[pl.ds(row, 1024)], held.at[i], sems.at[i])
        )
        copies[-1].start()
    for i in range(4):
        copies[i].wait()
        outs[i][...] = lax.dot_general(
            mixed_ref[...], held[i], NT, preferred_element_type=f32
        ).astype(bf16)


def spread(flags, mixed, full_o):
    rows = mixed.shape[0]
    return pl.pallas_call(
        spread_kernel,
        in_specs=[SMEM, VMEM, ANY],
        out_specs=[VMEM] * 4,
        out_shape=[jax.ShapeDtypeStruct((rows, 1024), bf16)] * 4,
        scratch_shapes=[pltpu.VMEM((4, 1024, 1024), bf16), pltpu.SemaphoreType.DMA((4,))],
        compiler_params=GRANT,
        cost_estimate=pl.CostEstimate(
            flops=2 * rows * 4096 * 1024, bytes_accessed=12 * 2**20, transcendentals=0
        ),
        name="spread",
    )(flags, mixed, full_o)


def around(shard, axis, by):
    return lax.ppermute(shard, axis, [(i, (i + by) % 4) for i in range(4)])


def from_first(shard, by, to_section):
    return lax.ppermute(
        shard, ("section", "tensor"), [(i, 4 * to_section + (i + by) % 4) for i in range(4)]
    )


def near_and_far(shard, axis):
    half = shard.shape[0] // 2
    before = around(shard, axis, 1)
    after = around(shard, axis, -1)
    far = [around(before[:half], axis, 1), around(after[half:], axis, -1)]
    return before, after, far


def gathered(shard, axis, then):
    before, after, far = near_and_far(shard, axis)
    near = jnp.stack([shard, before])
    other = jnp.stack([after, jnp.concatenate(far, 0)])
    near_before, near_after = around(near, then, 1), around(near, then, -1)
    other_before, other_after = around(other, then, 1), around(other, then, -1)
    near_far, other_far = around(near_before, then, 1), around(other_after, then, -1)
    return [near, other, near_before, other_before, near_after, other_after, near_far, other_far]


def pick(state, slot):
    return jnp.where(slot == 0, state[0], state[1])


def put(state, slot, new, active=True):
    mask = (jnp.arange(2) == slot) & active
    return jnp.where(mask[:, None, None], new[None], state)


def on_device(
    boundary_copies,
    arriving,
    first_delta,
    sample_index,
    exponents,
    norm_gain,
    w_query,
    w_key,
    w_value,
    w_out,
    out_grad,
):
    first = lax.axis_index("section") == 0
    z = lax.axis_index("tensor")

    full_o = lax.all_gather(w_out[0].T, ("y", "x"), axis=0, tiled=True)
    pieces = gathered(w_query[0, :, :HALF], "x", "y")
    pieces += gathered(
        jnp.concatenate([w_query[0, :, HALF:], w_key[0], w_value[0]], axis=1), "y", "x"
    )

    power = exponents.astype(f32)
    scale_full = jnp.repeat(jnp.exp2(power), QB, axis=1)
    inverse_full = jnp.repeat(jnp.exp2(-power), QB, axis=1)
    scale_in = jnp.where(first, scale_full[0], scale_full[1])
    scale_next = jnp.where(first, scale_full[1], scale_full[2])
    inverse_next = jnp.where(first, inverse_full[1], inverse_full[2])
    slots = sample_index[:, 0]
    slot = [jnp.where(first, slots[k + 1], slots[k]) for k in range(3)]

    def receive(state, at, delta):
        return (pick(state, at).astype(f32) + scale_in * delta.astype(f32)).astype(bf16)

    def deliver(state, at, inputs, summed):
        output = (inputs.astype(f32) + summed).astype(bf16)
        old = pick(state, at)
        sent = jnp.clip(
            (output.astype(f32) - old.astype(f32)) * inverse_next, -qmax, qmax
        ).astype(bf16)
        step = scale_next * sent.astype(f32)
        return step.astype(bf16), (old.astype(f32) + step).astype(bf16)

    arriving, first_delta, pieces[0], pieces[8] = lax.optimization_barrier(
        (arriving, first_delta, pieces[0], pieces[8])
    )
    state_in, state_out = boundary_copies[0, 0], boundary_copies[0, 1]
    x0 = receive(state_in, slot[0], arriving[0, 0])
    state_in = put(state_in, slot[0], x0)
    x1 = receive(state_in, slot[1], first_delta[0, 0])
    state_1 = put(state_in, slot[1], x1)
    x2 = receive(state_1, slot[2], first_delta[1, 0])
    state_2 = put(state_1, slot[2], x2)
    known = jnp.concatenate(
        [jnp.where(first, x0, state_in[0]), jnp.where(first, x1, state_in[1]), x2], 0
    )
    known = lax.all_to_all(
        jnp.broadcast_to(known[None], (4,) + known.shape),
        "tensor",
        split_axis=0,
        concat_axis=0,
        tiled=True,
    )

    flags = jnp.stack(
        [first.astype(jnp.int32), *slot, lax.axis_index("x"), lax.axis_index("y"), z]
    ).astype(jnp.int32)
    normed_a = prepare(flags, norm_gain, known)
    qkv_a, mixed_a = project_call(project_a_kernel, "project_a", [flags, normed_a], pieces, False)
    far, near_1, near_3, own = spread(flags, mixed_a, full_o)
    parts = [own] + [
        from_first(piece, by, 0) for piece, by in ((far, 2), (near_1, 1), (near_3, 3))
    ]
    summed = sum(part.astype(f32) for part in parts)
    step_0, renewed = deliver(state_out, slot[0], x0, summed[:SEQ])
    out_1 = put(state_out, slot[0], renewed)
    step_1, renewed = deliver(out_1, slot[1], x1, summed[SEQ:])
    out_2 = put(out_1, slot[1], renewed)
    steps = jnp.concatenate([step_0, step_1], 0)
    got = [from_first(steps, by, 1) for by in range(4)]

    def added(state, at, step):
        return (pick(state, at).astype(f32) + step.astype(f32)).astype(bf16)

    normed_b, qkv_b, mixed_b = project_call(
        project_b_kernel, "project_b", [flags, norm_gain, known, *got], pieces, True
    )
    y1 = added(state_in, slot[1], got[0][:SEQ])
    after_1 = put(state_in, slot[1], y1)
    y2 = added(after_1, slot[2], got[0][SEQ:])
    new_in = jnp.where(first, state_2, put(after_1, slot[2], y2))

    up = out_grad[0, :, 0].reshape(3 * SEQ, -1)
    d_mixed = jnp.dot(up, full_o, preferred_element_type=f32).astype(bf16)
    d_a = attend_back(qkv_a, d_mixed[: 2 * SEQ])
    d_mixed_b = jnp.concatenate(
        [jnp.where(first, d_mixed[2 * SEQ :], d_mixed[SEQ : 2 * SEQ]), d_mixed[2 * SEQ :]], 0
    )
    d_b = attend_back(qkv_b, d_mixed_b)

    def three(a, b):
        return jnp.concatenate([a[:SEQ], jnp.where(first, a[SEQ:], b[SEQ:]), b[:SEQ]], 0)

    term = lax.dot_general(
        three(normed_a, normed_b), three(d_a, d_b), TN, preferred_element_type=f32
    ).astype(bf16)
    grad = lax.psum_scatter(term, ("y", "x"), scatter_dimension=0, tiled=True)

    mixed_f = jnp.concatenate([jnp.where(first, mixed_b[:SEQ], mixed_a[:SEQ]), mixed_b], 0)
    mixed_f, _ = lax.optimization_barrier((mixed_f, term))
    partial = lax.dot_general(mixed_f, full_o, NT, preferred_element_type=f32).astype(bf16)
    parts = partial.reshape(3 * SEQ, 4, -1).swapaxes(0, 1)
    parts = lax.all_to_all(parts, "tensor", split_axis=0, concat_axis=0, tiled=True)
    summed = jnp.sum(parts.astype(f32), axis=0)
    _, renewed = deliver(out_2, slot[2], x2, summed[:SEQ])
    new_out_first = put(out_2, slot[2], renewed)
    _, renewed = deliver(state_out, slot[0], x0, summed[:SEQ])
    out_1 = put(state_out, slot[0], renewed)
    _, renewed = deliver(out_1, slot[1], y1, summed[SEQ : 2 * SEQ])
    out_1 = put(out_1, slot[1], renewed)
    _, renewed = deliver(out_1, slot[2], y2, summed[2 * SEQ :])
    new_out = jnp.where(first, new_out_first, put(out_1, slot[2], renewed))

    copies_new = jnp.stack([new_in, new_out])[None]
    return (copies_new, grad[None, :, :1024], grad[None, :, 1024:])


def solution(mesh):
    shape = dict(mesh.shape)
    grid = Mesh(
        mesh.devices.reshape(shape["section"], 4, shape["dp"] // 4, shape["tensor"]),
        ("section", "y", "x", "tensor"),
    )
    dp = ("y", "x")
    return jax.shard_map(
        on_device,
        mesh=grid,
        in_specs=(
            P("section", None, dp, None, "tensor"),
            P("section", dp, None, "tensor"),
            P(None, dp, None, "tensor"),
            P(None, dp),
            P(None, "tensor"),
            P("section", None),
            P("section", dp, "tensor"),
            P("section", dp, "tensor"),
            P("section", dp, "tensor"),
            P("section", "tensor", dp),
            P("section", None, dp, None, None),
        ),
        out_specs=(
            P("section", None, dp, None, "tensor"),
            P("section", dp, "tensor"),
            P("section", dp, "tensor"),
        ),
        check_vma=False,
    )
```

```python
import functools

import jax
import jax.numpy as jnp
from jax import lax
from jax.experimental import pallas as pl
from jax.experimental.pallas import tpu as pltpu
from jax.sharding import Mesh, PartitionSpec as P

HQ = 32
HK = 4
HD = 128
QB = 128
SEQ = 128

eps_norm = 1e-05
qmax = 7.0
f32 = jnp.float32
bf16 = jnp.bfloat16


GROUP = HQ // HK
NT = (((1,), (1,)), ((), ()))
TN = (((0,), (0,)), ((), ()))


def stacked(rows):
    return jnp.concatenate([rows[:, h * HD : (h + 1) * HD] for h in range(GROUP)], axis=0)


def side_by_side(rows):
    return jnp.concatenate([rows[h * SEQ : (h + 1) * SEQ] for h in range(GROUP)], axis=1)


def probs_of(query, key_in):
    scores = lax.dot_general(query, key_in, NT, preferred_element_type=f32) * HD ** (-0.5)
    at = lax.broadcasted_iota(jnp.int32, scores.shape, 0) % SEQ
    key_at = lax.broadcasted_iota(jnp.int32, scores.shape, 1)
    scores = jnp.where(at >= key_at, scores, -1e30)
    weight = jnp.exp(scores - jnp.max(scores, axis=-1, keepdims=True))
    return weight / jnp.sum(weight, axis=-1, keepdims=True)


def attend_unit(qkv):
    wide = GROUP * HD
    probs = probs_of(stacked(qkv[:, :wide]), qkv[:, wide : wide + HD])
    mixed = jnp.dot(probs.astype(bf16), qkv[:, wide + HD :], preferred_element_type=f32)
    return side_by_side(mixed.astype(bf16))


def attend_back_kernel(qkv_ref, d_mixed_ref, out_ref):
    wide = GROUP * HD
    key_in = qkv_ref[:, wide : wide + HD]
    probs = probs_of(stacked(qkv_ref[:, :wide]), key_in)
    d_rows = stacked(d_mixed_ref[...])
    d_probs = lax.dot_general(d_rows, qkv_ref[:, wide + HD :], NT, preferred_element_type=f32)
    d_scores = (
        probs * (d_probs - jnp.sum(d_probs * probs, axis=-1, keepdims=True)) * HD ** (-0.5)
    )
    d_query = jnp.dot(d_scores.astype(bf16), key_in, preferred_element_type=f32).astype(bf16)
    d_value = lax.dot_general(probs.astype(bf16), d_rows, TN, preferred_element_type=f32)
    out_ref[:, :wide] = side_by_side(d_query)
    out_ref[:, wide:] = d_value.astype(bf16)


def attend_back(qkv, d_mixed):
    rows = qkv.shape[0]
    return pl.pallas_call(
        attend_back_kernel,
        grid=(rows // SEQ,),
        in_specs=[
            pl.BlockSpec((SEQ, (GROUP + 2) * HD), lambda u: (u, 0)),
            pl.BlockSpec((SEQ, GROUP * HD), lambda u: (u, 0)),
        ],
        out_specs=pl.BlockSpec((SEQ, (GROUP + 1) * HD), lambda u: (u, 0)),
        out_shape=jax.ShapeDtypeStruct((rows, (GROUP + 1) * HD), bf16),
        compiler_params=pltpu.CompilerParams(vmem_limit_bytes=32 * 1024 * 1024),
        cost_estimate=pl.CostEstimate(
            flops=rows * SEQ * GROUP * HD * 8,
            bytes_accessed=rows * 3456 * 2,
            transcendentals=rows * SEQ * GROUP,
        ),
        name="attend_back",
    )(qkv, d_mixed)


ROWS = 16
HALF = 512
ORDER = (0, 3, 1, 2)


def known_a(flags, known_ref, x_ref):
    from_0 = (flags[0] == 1) | (flags[1] == 0)

    def step(i, carry):
        at = pl.multiple_of(i * ROWS, ROWS)
        for j in range(4):
            one = known_ref[j, pl.ds(at, ROWS), :]
            two = known_ref[j, pl.ds(at + SEQ, ROWS), :]
            columns = slice(j * 1024, (j + 1) * 1024)
            x_ref[pl.ds(at, ROWS), columns] = jnp.where(from_0, one, two)
            x_ref[pl.ds(at + SEQ, ROWS), columns] = two
        return carry

    lax.fori_loop(0, SEQ // ROWS, step, 0)


def known_b(flags, known_ref, got_refs, x_ref):
    first = flags[0] == 1
    slot_1, slot_2 = flags[2], flags[3]

    def step(i, carry):
        at = pl.multiple_of(i * ROWS, ROWS)
        for by in range(4):
            j = lax.rem(flags[6] + 4 - by, 4)
            one = known_ref[j, pl.ds(at, ROWS), :].astype(f32)
            two = known_ref[j, pl.ds(at + SEQ, ROWS), :].astype(f32)
            third = known_ref[j, pl.ds(at + 2 * SEQ, ROWS), :]
            step_1 = got_refs[by][pl.ds(at, ROWS), :].astype(f32)
            step_2 = got_refs[by][pl.ds(at + SEQ, ROWS), :].astype(f32)
            x_1 = (jnp.where(slot_1 == 0, one, two) + step_1).astype(bf16)
            old = jnp.where(
                slot_1 == slot_2, x_1.astype(f32), jnp.where(slot_2 == 0, one, two)
            )
            columns = pl.ds(pl.multiple_of(j * 1024, 1024), 1024)
            x_ref[pl.ds(at, ROWS), columns] = jnp.where(first, third, x_1)
            x_ref[pl.ds(at + SEQ, ROWS), columns] = (old + step_2).astype(bf16)
        return carry

    lax.fori_loop(0, SEQ // ROWS, step, 0)


def normalize(gain_ref, x_ref):
    def step(i, carry):
        rows = pl.ds(pl.multiple_of(i * ROWS, ROWS), ROWS)
        values = x_ref[rows, :].astype(f32)
        square = jnp.mean(values * values, axis=-1, keepdims=True)
        x_ref[rows, :] = (values * lax.rsqrt(square + eps_norm) * gain_ref[...]).astype(bf16)
        return carry

    lax.fori_loop(0, 2 * SEQ // ROWS, step, 0)


def prepare_kernel(flags, gain_ref, known_ref, normed_ref):
    known_a(flags, known_ref, normed_ref)
    normalize(gain_ref, normed_ref)


VMEM = pl.BlockSpec(memory_space=pltpu.VMEM)
SMEM = pl.BlockSpec(memory_space=pltpu.SMEM)
ANY = pl.BlockSpec(memory_space=pl.ANY)
GRANT = pltpu.CompilerParams(vmem_limit_bytes=60 * 1024 * 1024)


def prepare(flags, gain, known):
    return pl.pallas_call(
        prepare_kernel,
        in_specs=[SMEM, VMEM, VMEM],
        out_specs=VMEM,
        out_shape=jax.ShapeDtypeStruct((2 * SEQ, 4096), bf16),
        compiler_params=pltpu.CompilerParams(vmem_limit_bytes=32 * 1024 * 1024),
        cost_estimate=pl.CostEstimate(flops=2**23, bytes_accessed=5 * 2**20, transcendentals=0),
        name="prepare",
    )(flags, gain, known)


def project_kernel(flags, pieces, normed_ref, qkv_ref, mixed_ref, held, held_kv, sems, begin):
    full_ref, pieces = pieces[0], pieces[1:]
    copies = []
    for at in range(5):
        for half in range(2):
            target = held.at[half, at] if at < 3 else held.at[half, 3, pl.ds(2 * (at - 3), 2)]
            copies.append(
                pltpu.make_async_copy(pieces[half * 5 + at], target, sems.at[2 * at + half])
            )
    copies.append(pltpu.make_async_copy(full_ref.at[:, pl.ds(1024, 256)], held_kv, sems.at[10]))
    for copy in copies:
        copy.start()
    begin()
    totals = [None, None]
    for at in range(4):
        for half in range(2):
            lhs = []
            for block in range(4):
                along, across = ORDER[at], ORDER[block]
                dy, dx = (along, across) if half == 0 else (across, along)
                row = lax.rem(flags[5] + dy, 4) * 4 + lax.rem(flags[4] + dx, 4)
                lhs.append(normed_ref[:, pl.ds(pl.multiple_of(row * 256, 256), 256)])
            copies[2 * at + half].wait()
            if at == 3:
                copies[8 + half].wait()
            part = jnp.dot(
                jnp.concatenate(lhs, axis=1),
                held[half, at].reshape(1024, HALF),
                preferred_element_type=f32,
            )
            totals[half] = part if totals[half] is None else totals[half] + part
    for half in range(2):
        qkv_ref[:, half * HALF : (half + 1) * HALF] = totals[half].astype(bf16)
    copies[10].wait()
    qkv_ref[:, 1024:] = jnp.dot(
        normed_ref[...], held_kv[...], preferred_element_type=f32
    ).astype(bf16)
    for unit in range(2):
        rows = slice(unit * SEQ, (unit + 1) * SEQ)
        mixed_ref[rows, :] = attend_unit(qkv_ref[rows, :])


def project_a_kernel(flags, normed_ref, *refs):
    pieces, (qkv_ref, mixed_ref, held, held_kv, sems) = refs[:11], refs[11:]
    project_kernel(flags, pieces, normed_ref, qkv_ref, mixed_ref, held, held_kv, sems, lambda: None)


def project_b_kernel(flags, gain_ref, known_ref, *refs):
    got_refs, pieces = refs[:4], refs[4:15]
    normed_ref, qkv_ref, mixed_ref, held, held_kv, sems = refs[15:]

    def begin():
        known_b(flags, known_ref, got_refs, normed_ref)
        normalize(gain_ref, normed_ref)

    project_kernel(flags, pieces, normed_ref, qkv_ref, mixed_ref, held, held_kv, sems, begin)


def project_call(kernel, name, operands, pieces, with_normed):
    rows = 2 * SEQ
    shapes = [
        jax.ShapeDtypeStruct((rows, 4096), bf16),
        jax.ShapeDtypeStruct((rows, (GROUP + 2) * HD), bf16),
        jax.ShapeDtypeStruct((rows, GROUP * HD), bf16),
    ][0 if with_normed else 1 :]
    return pl.pallas_call(
        kernel,
        in_specs=[SMEM] + [VMEM] * (len(operands) - 1) + [ANY] * 11,
        out_specs=[VMEM] * len(shapes),
        out_shape=shapes,
        scratch_shapes=[
            pltpu.VMEM((2, 4, 4, 256, HALF), bf16),
            pltpu.VMEM((4096, 256), bf16),
            pltpu.SemaphoreType.DMA((11,)),
        ],
        compiler_params=GRANT,
        cost_estimate=pl.CostEstimate(
            flops=2 * rows * 4096 * 2 * HALF, bytes_accessed=18 * 2**20, transcendentals=rows * 1024
        ),
        name=name,
    )(*operands, *pieces)


def spread_kernel(flags, mixed_ref, full_ref, *refs):
    outs, (held, sems) = refs[:4], refs[4:]
    copies = []
    for i, by in enumerate((2, 1, 3, 0)):
        row = pl.multiple_of(lax.rem(flags[6] + by, 4) * 1024, 1024)
        copies.append(
            pltpu.make_async_copy(full_ref.at[pl.ds(row, 1024), pl.ds(0, 1024)], held.at[i], sems.at[i])
        )
        copies[-1].start()
    for i in range(4):
        copies[i].wait()
        outs[i][...] = lax.dot_general(
            mixed_ref[...], held[i], NT, preferred_element_type=f32
        ).astype(bf16)


def spread(flags, mixed, full):
    rows = mixed.shape[0]
    return pl.pallas_call(
        spread_kernel,
        in_specs=[SMEM, VMEM, ANY],
        out_specs=[VMEM] * 4,
        out_shape=[jax.ShapeDtypeStruct((rows, 1024), bf16)] * 4,
        scratch_shapes=[pltpu.VMEM((4, 1024, 1024), bf16), pltpu.SemaphoreType.DMA((4,))],
        compiler_params=GRANT,
        cost_estimate=pl.CostEstimate(
            flops=2 * rows * 4096 * 1024, bytes_accessed=12 * 2**20, transcendentals=0
        ),
        name="spread",
    )(flags, mixed, full)


def around(shard, axis, by):
    return lax.ppermute(shard, axis, [(i, (i + by) % 4) for i in range(4)])


def from_first(shard, by, to_section):
    return lax.ppermute(
        shard, ("section", "tensor"), [(i, 4 * to_section + (i + by) % 4) for i in range(4)]
    )


def gathered(shard, axis):
    before, after, far = around(shard, axis, 1), around(shard, axis, -1), around(shard, axis, 2)
    return jnp.stack([shard, before, after, far])


def spread_on(own, then):
    before, after = around(own, then, 1), around(own, then, -1)
    return [own, before, after, around(before[:2], then, 1), around(after[2:], then, -1)]


def pick(state, slot):
    return jnp.where(slot == 0, state[0], state[1])


def put(state, slot, new, active=True):
    mask = (jnp.arange(2) == slot) & active
    return jnp.where(mask[:, None, None], new[None], state)


def on_device(
    boundary_copies,
    arriving,
    first_delta,
    sample_index,
    exponents,
    norm_gain,
    w_query,
    w_key,
    w_value,
    w_out,
    out_grad,
):
    first = lax.axis_index("section") == 0
    z = lax.axis_index("tensor")

    packed = jnp.concatenate([w_out[0].T, w_key[0], w_value[0]], axis=1)
    full = lax.all_gather(packed, ("y", "x"), axis=0, tiled=True)
    full_o = full[:, :1024]
    own_a = gathered(w_query[0, :, :HALF], "x")
    own_b = gathered(w_query[0, :, HALF:], "y")
    arriving, first_delta, own_a, own_b = lax.optimization_barrier(
        (arriving, first_delta, own_a, own_b)
    )
    pieces = [full] + spread_on(own_a, "y") + spread_on(own_b, "x")

    power = exponents.astype(f32)
    scale_full = jnp.repeat(jnp.exp2(power), QB, axis=1)
    inverse_full = jnp.repeat(jnp.exp2(-power), QB, axis=1)
    scale_in = jnp.where(first, scale_full[0], scale_full[1])
    scale_next = jnp.where(first, scale_full[1], scale_full[2])
    inverse_next = jnp.where(first, inverse_full[1], inverse_full[2])
    slots = sample_index[:, 0]
    slot = [jnp.where(first, slots[k + 1], slots[k]) for k in range(3)]

    def receive(state, at, delta):
        return (pick(state, at).astype(f32) + scale_in * delta.astype(f32)).astype(bf16)

    def deliver(state, at, inputs, summed):
        output = (inputs.astype(f32) + summed).astype(bf16)
        old = pick(state, at)
        sent = jnp.clip(
            (output.astype(f32) - old.astype(f32)) * inverse_next, -qmax, qmax
        ).astype(bf16)
        step = scale_next * sent.astype(f32)
        return step.astype(bf16), (old.astype(f32) + step).astype(bf16)

    state_in, state_out = boundary_copies[0, 0], boundary_copies[0, 1]
    x0 = receive(state_in, slot[0], arriving[0, 0])
    state_in = put(state_in, slot[0], x0)
    x1 = receive(state_in, slot[1], first_delta[0, 0])
    state_1 = put(state_in, slot[1], x1)
    x2 = receive(state_1, slot[2], first_delta[1, 0])
    state_2 = put(state_1, slot[2], x2)
    known = jnp.concatenate(
        [jnp.where(first, x0, state_in[0]), jnp.where(first, x1, state_in[1]), x2], 0
    )
    known = lax.all_to_all(
        jnp.broadcast_to(known[None], (4,) + known.shape),
        "tensor",
        split_axis=0,
        concat_axis=0,
        tiled=True,
    )

    flags = jnp.stack(
        [first.astype(jnp.int32), *slot, lax.axis_index("x"), lax.axis_index("y"), z]
    ).astype(jnp.int32)
    normed_a = prepare(flags, norm_gain, known)
    qkv_a, mixed_a = project_call(project_a_kernel, "project_a", [flags, normed_a], pieces, False)
    far, near_1, near_3, own = spread(flags, mixed_a, full)
    parts = [own] + [
        from_first(piece, by, 0) for piece, by in ((far, 2), (near_1, 1), (near_3, 3))
    ]
    summed = sum(part.astype(f32) for part in parts)
    step_0, renewed = deliver(state_out, slot[0], x0, summed[:SEQ])
    out_1 = put(state_out, slot[0], renewed)
    step_1, renewed = deliver(out_1, slot[1], x1, summed[SEQ:])
    out_2 = put(out_1, slot[1], renewed)
    steps = jnp.concatenate([step_0, step_1], 0)
    got = [from_first(steps, by, 1) for by in range(4)]

    def added(state, at, step):
        return (pick(state, at).astype(f32) + step.astype(f32)).astype(bf16)

    normed_b, qkv_b, mixed_b = project_call(
        project_b_kernel, "project_b", [flags, norm_gain, known, *got], pieces, True
    )
    y1 = added(state_in, slot[1], got[0][:SEQ])
    after_1 = put(state_in, slot[1], y1)
    y2 = added(after_1, slot[2], got[0][SEQ:])
    new_in = jnp.where(first, state_2, put(after_1, slot[2], y2))

    up = out_grad[0, :, 0].reshape(3 * SEQ, -1)
    d_mixed = jnp.dot(up, full_o, preferred_element_type=f32).astype(bf16)
    d_a = attend_back(qkv_a, d_mixed[: 2 * SEQ])
    d_mixed_b = jnp.concatenate(
        [jnp.where(first, d_mixed[2 * SEQ :], d_mixed[SEQ : 2 * SEQ]), d_mixed[2 * SEQ :]], 0
    )
    d_b = attend_back(qkv_b, d_mixed_b)

    def three(a, b):
        return jnp.concatenate([a[:SEQ], jnp.where(first, a[SEQ:], b[SEQ:]), b[:SEQ]], 0)

    term = lax.dot_general(
        three(normed_a, normed_b), three(d_a, d_b), TN, preferred_element_type=f32
    ).astype(bf16)
    grad = lax.psum_scatter(term, ("y", "x"), scatter_dimension=0, tiled=True)

    mixed_f = jnp.concatenate([jnp.where(first, mixed_b[:SEQ], mixed_a[:SEQ]), mixed_b], 0)
    mixed_f, _ = lax.optimization_barrier((mixed_f, term))
    partial = lax.dot_general(mixed_f, full_o, NT, preferred_element_type=f32).astype(bf16)
    parts = partial.reshape(3 * SEQ, 4, -1).swapaxes(0, 1)
    parts = lax.all_to_all(parts, "tensor", split_axis=0, concat_axis=0, tiled=True)
    summed = jnp.sum(parts.astype(f32), axis=0)
    _, renewed = deliver(out_2, slot[2], x2, summed[:SEQ])
    new_out_first = put(out_2, slot[2], renewed)
    _, renewed = deliver(state_out, slot[0], x0, summed[:SEQ])
    out_1 = put(state_out, slot[0], renewed)
    _, renewed = deliver(out_1, slot[1], y1, summed[SEQ : 2 * SEQ])
    out_1 = put(out_1, slot[1], renewed)
    _, renewed = deliver(out_1, slot[2], y2, summed[2 * SEQ :])
    new_out = jnp.where(first, new_out_first, put(out_1, slot[2], renewed))

    copies_new = jnp.stack([new_in, new_out])[None]
    return (copies_new, grad[None, :, :1024], grad[None, :, 1024:])


def solution(mesh):
    shape = dict(mesh.shape)
    grid = Mesh(
        mesh.devices.reshape(shape["section"], 4, shape["dp"] // 4, shape["tensor"]),
        ("section", "y", "x", "tensor"),
    )
    dp = ("y", "x")
    return jax.shard_map(
        on_device,
        mesh=grid,
        in_specs=(
            P("section", None, dp, None, "tensor"),
            P("section", dp, None, "tensor"),
            P(None, dp, None, "tensor"),
            P(None, dp),
            P(None, "tensor"),
            P("section", None),
            P("section", dp, "tensor"),
            P("section", dp, "tensor"),
            P("section", dp, "tensor"),
            P("section", "tensor", dp),
            P("section", None, dp, None, None),
        ),
        out_specs=(
            P("section", None, dp, None, "tensor"),
            P("section", dp, "tensor"),
            P("section", dp, "tensor"),
        ),
        check_vma=False,
    )
```

```python
import functools

import jax
import jax.numpy as jnp
from jax import lax
from jax.experimental import pallas as pl
from jax.experimental.pallas import tpu as pltpu
from jax.sharding import Mesh, PartitionSpec as P

HQ = 32
HK = 4
HD = 128
QB = 128
SEQ = 128

eps_norm = 1e-05
qmax = 7.0
f32 = jnp.float32
bf16 = jnp.bfloat16


GROUP = HQ // HK
NT = (((1,), (1,)), ((), ()))
TN = (((0,), (0,)), ((), ()))


def stacked(rows):
    return jnp.concatenate([rows[:, h * HD : (h + 1) * HD] for h in range(GROUP)], axis=0)


def side_by_side(rows):
    return jnp.concatenate([rows[h * SEQ : (h + 1) * SEQ] for h in range(GROUP)], axis=1)


def probs_of(query, key_in):
    scores = lax.dot_general(query, key_in, NT, preferred_element_type=f32) * HD ** (-0.5)
    at = lax.broadcasted_iota(jnp.int32, scores.shape, 0) % SEQ
    key_at = lax.broadcasted_iota(jnp.int32, scores.shape, 1)
    scores = jnp.where(at >= key_at, scores, -1e30)
    weight = jnp.exp(scores - jnp.max(scores, axis=-1, keepdims=True))
    return weight / jnp.sum(weight, axis=-1, keepdims=True)


def attend_unit(qkv):
    wide = GROUP * HD
    probs = probs_of(stacked(qkv[:, :wide]), qkv[:, wide : wide + HD])
    mixed = jnp.dot(probs.astype(bf16), qkv[:, wide + HD :], preferred_element_type=f32)
    return side_by_side(mixed.astype(bf16))


def attend_back_kernel(qkv_ref, d_mixed_ref, out_ref):
    wide = GROUP * HD
    key_in = qkv_ref[:, wide : wide + HD]
    probs = probs_of(stacked(qkv_ref[:, :wide]), key_in)
    d_rows = stacked(d_mixed_ref[...])
    d_probs = lax.dot_general(d_rows, qkv_ref[:, wide + HD :], NT, preferred_element_type=f32)
    d_scores = (
        probs * (d_probs - jnp.sum(d_probs * probs, axis=-1, keepdims=True)) * HD ** (-0.5)
    )
    d_query = jnp.dot(d_scores.astype(bf16), key_in, preferred_element_type=f32).astype(bf16)
    d_value = lax.dot_general(probs.astype(bf16), d_rows, TN, preferred_element_type=f32)
    out_ref[:, :wide] = side_by_side(d_query)
    out_ref[:, wide:] = d_value.astype(bf16)


def attend_back(qkv, d_mixed):
    rows = qkv.shape[0]
    return pl.pallas_call(
        attend_back_kernel,
        grid=(rows // SEQ,),
        in_specs=[
            pl.BlockSpec((SEQ, (GROUP + 2) * HD), lambda u: (u, 0)),
            pl.BlockSpec((SEQ, GROUP * HD), lambda u: (u, 0)),
        ],
        out_specs=pl.BlockSpec((SEQ, (GROUP + 1) * HD), lambda u: (u, 0)),
        out_shape=jax.ShapeDtypeStruct((rows, (GROUP + 1) * HD), bf16),
        compiler_params=pltpu.CompilerParams(vmem_limit_bytes=32 * 1024 * 1024),
        cost_estimate=pl.CostEstimate(
            flops=rows * SEQ * GROUP * HD * 8,
            bytes_accessed=rows * 3456 * 2,
            transcendentals=rows * SEQ * GROUP,
        ),
        name="attend_back",
    )(qkv, d_mixed)


ROWS = 16
HALF = 640
HALF_O = 512
ORDER = (0, 3, 1, 2)


def known_a(flags, known_ref, x_ref):
    from_0 = (flags[0] == 1) | (flags[1] == 0)

    def step(i, carry):
        at = pl.multiple_of(i * ROWS, ROWS)
        for j in range(4):
            one = known_ref[j, pl.ds(at, ROWS), :]
            two = known_ref[j, pl.ds(at + SEQ, ROWS), :]
            columns = slice(j * 1024, (j + 1) * 1024)
            x_ref[pl.ds(at, ROWS), columns] = jnp.where(from_0, one, two)
            x_ref[pl.ds(at + SEQ, ROWS), columns] = two
        return carry

    lax.fori_loop(0, SEQ // ROWS, step, 0)


def known_b(flags, known_ref, got_refs, x_ref):
    first = flags[0] == 1
    slot_1, slot_2 = flags[2], flags[3]

    def step(i, carry):
        at = pl.multiple_of(i * ROWS, ROWS)
        for by in range(4):
            j = lax.rem(flags[6] + 4 - by, 4)
            one = known_ref[j, pl.ds(at, ROWS), :].astype(f32)
            two = known_ref[j, pl.ds(at + SEQ, ROWS), :].astype(f32)
            third = known_ref[j, pl.ds(at + 2 * SEQ, ROWS), :]
            step_1 = got_refs[by][pl.ds(at, ROWS), :].astype(f32)
            step_2 = got_refs[by][pl.ds(at + SEQ, ROWS), :].astype(f32)
            x_1 = (jnp.where(slot_1 == 0, one, two) + step_1).astype(bf16)
            old = jnp.where(
                slot_1 == slot_2, x_1.astype(f32), jnp.where(slot_2 == 0, one, two)
            )
            columns = pl.ds(pl.multiple_of(j * 1024, 1024), 1024)
            x_ref[pl.ds(at, ROWS), columns] = jnp.where(first, third, x_1)
            x_ref[pl.ds(at + SEQ, ROWS), columns] = (old + step_2).astype(bf16)
        return carry

    lax.fori_loop(0, SEQ // ROWS, step, 0)


def normalize(gain_ref, x_ref):
    def step(i, carry):
        rows = pl.ds(pl.multiple_of(i * ROWS, ROWS), ROWS)
        values = x_ref[rows, :].astype(f32)
        square = jnp.mean(values * values, axis=-1, keepdims=True)
        x_ref[rows, :] = (values * lax.rsqrt(square + eps_norm) * gain_ref[...]).astype(bf16)
        return carry

    lax.fori_loop(0, 2 * SEQ // ROWS, step, 0)


def prepare_kernel(flags, gain_ref, known_ref, normed_ref):
    known_a(flags, known_ref, normed_ref)
    normalize(gain_ref, normed_ref)


VMEM = pl.BlockSpec(memory_space=pltpu.VMEM)
SMEM = pl.BlockSpec(memory_space=pltpu.SMEM)
ANY = pl.BlockSpec(memory_space=pl.ANY)
GRANT = pltpu.CompilerParams(vmem_limit_bytes=60 * 1024 * 1024)


def fetch(pieces, held, sems):
    copies = []
    for at in range(5):
        for half in range(2):
            target = held.at[half, at] if at < 3 else held.at[half, 3, pl.ds(2 * (at - 3), 2)]
            copies.append(
                pltpu.make_async_copy(pieces[half * 5 + at], target, sems.at[2 * at + half])
            )
            copies[-1].start()
    return copies


def arrived(copies, half, at):
    copies[2 * at + half].wait()
    if at == 3:
        copies[8 + half].wait()


def block_of(flags, half, along, across):
    dy, dx = (along, across) if half == 0 else (across, along)
    return lax.rem(flags[5] + dy, 4) * 4 + lax.rem(flags[4] + dx, 4)


def times_gathered(flags, rows_ref, held, copies):
    totals = [None, None]
    for at in range(4):
        for half in range(2):
            lhs = []
            for block in range(4):
                number = block_of(flags, half, ORDER[at], ORDER[block])
                lhs.append(rows_ref[:, pl.ds(pl.multiple_of(number * 256, 256), 256)])
            arrived(copies, half, at)
            part = jnp.dot(
                jnp.concatenate(lhs, axis=1),
                held[half, at].reshape(1024, held.shape[-1]),
                preferred_element_type=f32,
            )
            totals[half] = part if totals[half] is None else totals[half] + part
    return totals


def prepare(flags, gain, known):
    return pl.pallas_call(
        prepare_kernel,
        in_specs=[SMEM, VMEM, VMEM],
        out_specs=VMEM,
        out_shape=jax.ShapeDtypeStruct((2 * SEQ, 4096), bf16),
        compiler_params=pltpu.CompilerParams(vmem_limit_bytes=32 * 1024 * 1024),
        cost_estimate=pl.CostEstimate(flops=2**23, bytes_accessed=5 * 2**20, transcendentals=0),
        name="prepare",
    )(flags, gain, known)


def project_kernel(flags, pieces, normed_ref, qkv_ref, mixed_ref, held, sems, begin):
    copies = fetch(pieces, held, sems)
    begin()
    totals = times_gathered(flags, normed_ref, held, copies)
    for half in range(2):
        qkv_ref[:, half * HALF : (half + 1) * HALF] = totals[half].astype(bf16)
    for unit in range(2):
        rows = slice(unit * SEQ, (unit + 1) * SEQ)
        mixed_ref[rows, :] = attend_unit(qkv_ref[rows, :])


def project_a_kernel(flags, normed_ref, *refs):
    pieces, (qkv_ref, mixed_ref, held, sems) = refs[:10], refs[10:]
    project_kernel(flags, pieces, normed_ref, qkv_ref, mixed_ref, held, sems, lambda: None)


def project_b_kernel(flags, gain_ref, known_ref, *refs):
    got_refs, pieces = refs[:4], refs[4:14]
    normed_ref, qkv_ref, mixed_ref, held, sems = refs[14:]

    def begin():
        known_b(flags, known_ref, got_refs, normed_ref)
        normalize(gain_ref, normed_ref)

    project_kernel(flags, pieces, normed_ref, qkv_ref, mixed_ref, held, sems, begin)


def with_gathered(kernel, name, operands, pieces, columns, shapes, rows):
    return pl.pallas_call(
        kernel,
        in_specs=[SMEM] + [VMEM] * (len(operands) - 1) + [ANY] * 10,
        out_specs=[VMEM] * len(shapes),
        out_shape=[jax.ShapeDtypeStruct(shape, bf16) for shape in shapes],
        scratch_shapes=[
            pltpu.VMEM((2, 4, 4, 256, columns), bf16),
            pltpu.SemaphoreType.DMA((10,)),
        ],
        compiler_params=GRANT,
        cost_estimate=pl.CostEstimate(
            flops=2 * rows * 4096 * 2 * columns,
            bytes_accessed=4096 * 4 * columns + 6 * 2**20,
            transcendentals=0,
        ),
        name=name,
    )(*operands, *pieces)


def part_outputs(flags, mixed, target, held, out):
    offset = lax.rem(target + 4 - flags[5], 4)
    place = jnp.where(offset == 0, 0, jnp.where(offset == 3, 1, offset + 1))
    for at in range(4):
        part = lax.dot_general(
            mixed[:, :HALF_O], held[0, place, at], NT, preferred_element_type=f32
        ) + lax.dot_general(
            mixed[:, HALF_O:], held[1, at, place], NT, preferred_element_type=f32
        )
        column = pl.multiple_of(lax.rem(flags[4] + ORDER[at], 4) * 256, 256)
        out[:, pl.ds(column, 256)] = part.astype(bf16)


def spread_kernel(flags, mixed_ref, *refs):
    pieces, outs, (held, sems) = refs[:10], refs[10:14], refs[14:]
    copies = fetch(pieces, held, sems)
    for copy in copies:
        copy.wait()
    for out, by in zip(outs, (2, 1, 3, 0)):
        part_outputs(flags, mixed_ref[...], lax.rem(flags[6] + by, 4), held, out)


def outputs_kernel(flags, mixed_ref, *refs):
    pieces, (out_ref, held, sems) = refs[:10], refs[10:]
    copies = fetch(pieces, held, sems)
    for copy in copies:
        copy.wait()
    for target in range(4):
        part_outputs(flags, mixed_ref[...], target, held, out_ref.at[target])


def d_mixed_kernel(flags, up_ref, *refs):
    pieces, (a_ref, b_ref, held, sems) = refs[:10], refs[10:]
    copies = fetch(pieces, held, sems)
    totals = times_gathered(flags, up_ref, held, copies)
    for half in range(2):
        columns = slice(half * HALF_O, (half + 1) * HALF_O)
        value = totals[half].astype(bf16)
        a_ref[:, columns] = value[: 2 * SEQ]
        b_ref[:SEQ, columns] = jnp.where(flags[0] == 1, value[2 * SEQ :], value[SEQ : 2 * SEQ])
        b_ref[SEQ:, columns] = value[2 * SEQ :]


WIDE_A, WIDE_B = 640, 512


def three(flags, a_ref, b_ref, columns):
    middle = jnp.where(flags[0] == 1, a_ref[SEQ:, columns], b_ref[SEQ:, columns])
    return jnp.concatenate([a_ref[:SEQ, columns], middle, b_ref[:SEQ, columns]], axis=0)


def terms(flags, refs, half, along, acrosses, out):
    normed_a, normed_b, d_a, d_b = refs
    lhs = []
    for across in acrosses:
        number = block_of(flags, half, along, across)
        lhs.append(
            three(flags, normed_a, normed_b, pl.ds(pl.multiple_of(number * 256, 256), 256))
        )
    columns = pl.ds(0, WIDE_A) if half == 0 else pl.ds(WIDE_A, WIDE_B)
    out[...] = lax.dot_general(
        jnp.concatenate(lhs, axis=1),
        three(flags, d_a, d_b, columns),
        TN,
        preferred_element_type=f32,
    ).astype(bf16)


def far_terms_kernel(flags, *refs):
    refs, outs = refs[:4], refs[4:]
    for half in range(2):
        for part, acrosses in enumerate(((0, 1), (2, 3))):
            terms(flags, refs, half, 2, acrosses, outs[2 * half + part])


def near_terms_kernel(flags, *refs):
    refs, outs = refs[:4], refs[4:]
    at = 0
    for along in (1, 3, 0):
        for half in range(2):
            for acrosses in ((0, 1), (2, 3)):
                terms(flags, refs, half, along, acrosses, outs[at])
                at += 1


def term_call(kernel, name, operands, copies):
    shapes = [(512, WIDE_A), (512, WIDE_A), (512, WIDE_B), (512, WIDE_B)] * copies
    return pl.pallas_call(
        kernel,
        in_specs=[SMEM] + [VMEM] * 4,
        out_specs=[VMEM] * len(shapes),
        out_shape=[jax.ShapeDtypeStruct(shape, bf16) for shape in shapes],
        compiler_params=GRANT,
        cost_estimate=pl.CostEstimate(
            flops=2 * 3 * SEQ * 1024 * 1152 * copies,
            bytes_accessed=2**21 * copies + 5 * 2**20,
            transcendentals=0,
        ),
        name=name,
    )(*operands)


def around(shard, axis, by):
    return lax.ppermute(shard, axis, [(i, (i + by) % 4) for i in range(4)])


def from_first(shard, by, to_section):
    return lax.ppermute(
        shard, ("section", "tensor"), [(i, 4 * to_section + (i + by) % 4) for i in range(4)]
    )


def gathered(shard, axis):
    before, after, far = around(shard, axis, 1), around(shard, axis, -1), around(shard, axis, 2)
    blocks = (shard, before, after, far)
    return jnp.stack([block[:, :HALF] for block in blocks]), jnp.stack(
        [block[:, HALF:] for block in blocks]
    )


def spread_on(own, then):
    before, after = around(own, then, 1), around(own, then, -1)
    return [own, before, after, around(before[:2], then, 1), around(after[2:], then, -1)]


def plus(*shards):
    return sum(shard.astype(f32) for shard in shards).astype(bf16)


def reduced(far, near, own, along, across):
    by_before = around(far[0], along, 1)
    by_after = around(far[1], along, -1)
    raw_before = around(near[0][1], along, 1)
    raw_after = around(near[1][0], along, -1)
    sum_before = around(plus(near[0][0], by_before), along, 1)
    sum_after = around(plus(near[1][1], by_after), along, -1)
    low = (own[0], sum_before, raw_after)
    high = (own[1], raw_before, sum_after)
    blocks = [plus(*(part[:256] for part in low)), plus(*(part[256:] for part in low))]
    blocks += [plus(*(part[:256] for part in high)), plus(*(part[256:] for part in high))]
    got = [around(blocks[2], across, 2), around(blocks[1], across, 1), around(blocks[3], across, -1)]
    return plus(blocks[0], *got)


def pick(state, slot):
    return jnp.where(slot == 0, state[0], state[1])


def put(state, slot, new, active=True):
    mask = (jnp.arange(2) == slot) & active
    return jnp.where(mask[:, None, None], new[None], state)


def on_device(
    boundary_copies,
    arriving,
    first_delta,
    sample_index,
    exponents,
    norm_gain,
    w_query,
    w_key,
    w_value,
    w_out,
    out_grad,
):
    first = lax.axis_index("section") == 0
    z = lax.axis_index("tensor")

    out_t = w_out[0].T
    shard_a = jnp.concatenate([w_query[0, :, :HALF], out_t[:, :HALF_O]], axis=1)
    shard_b = jnp.concatenate(
        [w_query[0, :, HALF:], w_key[0], w_value[0], out_t[:, HALF_O:]], axis=1
    )
    own_a, late_a = gathered(shard_a, "x")
    own_b, late_b = gathered(shard_b, "y")
    arriving, first_delta, own_a, own_b = lax.optimization_barrier(
        (arriving, first_delta, own_a, own_b)
    )
    pieces = spread_on(own_a, "y") + spread_on(own_b, "x")
    late_a, late_b, pieces[3] = lax.optimization_barrier((late_a, late_b, pieces[3]))
    out_pieces = spread_on(late_a, "y") + spread_on(late_b, "x")

    power = exponents.astype(f32)
    scale_full = jnp.repeat(jnp.exp2(power), QB, axis=1)
    inverse_full = jnp.repeat(jnp.exp2(-power), QB, axis=1)
    scale_in = jnp.where(first, scale_full[0], scale_full[1])
    scale_next = jnp.where(first, scale_full[1], scale_full[2])
    inverse_next = jnp.where(first, inverse_full[1], inverse_full[2])
    slots = sample_index[:, 0]
    slot = [jnp.where(first, slots[k + 1], slots[k]) for k in range(3)]

    def receive(state, at, delta):
        return (pick(state, at).astype(f32) + scale_in * delta.astype(f32)).astype(bf16)

    def deliver(state, at, inputs, summed):
        output = (inputs.astype(f32) + summed).astype(bf16)
        old = pick(state, at)
        sent = jnp.clip(
            (output.astype(f32) - old.astype(f32)) * inverse_next, -qmax, qmax
        ).astype(bf16)
        step = scale_next * sent.astype(f32)
        return step.astype(bf16), (old.astype(f32) + step).astype(bf16)

    state_in, state_out = boundary_copies[0, 0], boundary_copies[0, 1]
    x0 = receive(state_in, slot[0], arriving[0, 0])
    state_in = put(state_in, slot[0], x0)
    x1 = receive(state_in, slot[1], first_delta[0, 0])
    state_1 = put(state_in, slot[1], x1)
    x2 = receive(state_1, slot[2], first_delta[1, 0])
    state_2 = put(state_1, slot[2], x2)
    known = jnp.concatenate(
        [jnp.where(first, x0, state_in[0]), jnp.where(first, x1, state_in[1]), x2], 0
    )
    known = lax.all_to_all(
        jnp.broadcast_to(known[None], (4,) + known.shape),
        "tensor",
        split_axis=0,
        concat_axis=0,
        tiled=True,
    )

    flags = jnp.stack(
        [first.astype(jnp.int32), *slot, lax.axis_index("x"), lax.axis_index("y"), z]
    ).astype(jnp.int32)
    normed_a = prepare(flags, norm_gain, known)
    rows = 2 * SEQ
    qkv_a, mixed_a = with_gathered(
        project_a_kernel,
        "project_a",
        [flags, normed_a],
        pieces,
        HALF,
        [(rows, 2 * HALF), (rows, 1024)],
        rows,
    )
    far, near_1, near_3, own = with_gathered(
        spread_kernel, "spread", [flags, mixed_a], out_pieces, HALF_O, [(rows, 1024)] * 4, rows
    )
    parts = [own] + [
        from_first(piece, by, 0) for piece, by in ((far, 2), (near_1, 1), (near_3, 3))
    ]
    summed = sum(part.astype(f32) for part in parts)
    step_0, renewed = deliver(state_out, slot[0], x0, summed[:SEQ])
    out_1 = put(state_out, slot[0], renewed)
    step_1, renewed = deliver(out_1, slot[1], x1, summed[SEQ:])
    out_2 = put(out_1, slot[1], renewed)
    steps = jnp.concatenate([step_0, step_1], 0)
    got = [from_first(steps, by, 1) for by in range(4)]

    def added(state, at, step):
        return (pick(state, at).astype(f32) + step.astype(f32)).astype(bf16)

    normed_b, qkv_b, mixed_b = with_gathered(
        project_b_kernel,
        "project_b",
        [flags, norm_gain, known, *got],
        pieces,
        HALF,
        [(rows, 4096), (rows, 2 * HALF), (rows, 1024)],
        rows,
    )
    y1 = added(state_in, slot[1], got[0][:SEQ])
    after_1 = put(state_in, slot[1], y1)
    y2 = added(after_1, slot[2], got[0][SEQ:])
    new_in = jnp.where(first, state_2, put(after_1, slot[2], y2))

    up = out_grad[0, :, 0].reshape(3 * SEQ, -1)
    d_mixed_a, d_mixed_b = with_gathered(
        d_mixed_kernel, "d_mixed", [flags, up], out_pieces, HALF_O, [(rows, 1024)] * 2, 3 * SEQ
    )
    d_a = attend_back(qkv_a, d_mixed_a)
    d_b = attend_back(qkv_b, d_mixed_b)
    operands = [flags, normed_a, normed_b, d_a, d_b]
    far = term_call(far_terms_kernel, "far_terms", operands, 1)
    near = term_call(near_terms_kernel, "near_terms", operands, 3)
    grad_a = reduced(far[:2], (near[0:2], near[4:6]), near[8:10], "y", "x")
    grad_b = reduced(far[2:], (near[2:4], near[6:8]), near[10:12], "x", "y")
    grad_query = jnp.concatenate([grad_a, grad_b[:, : 1024 - WIDE_A]], axis=1)
    grad_value = grad_b[:, 1024 - WIDE_A :]

    mixed_f = jnp.concatenate([jnp.where(first, mixed_b[:SEQ], mixed_a[:SEQ]), mixed_b], 0)
    mixed_f, _ = lax.optimization_barrier((mixed_f, near[0]))
    (partial,) = with_gathered(
        outputs_kernel, "outputs", [flags, mixed_f], out_pieces, HALF_O, [(4, 384, 1024)], 3 * SEQ
    )
    parts = lax.all_to_all(partial, "tensor", split_axis=0, concat_axis=0, tiled=True)
    summed = jnp.sum(parts.astype(f32), axis=0)
    _, renewed = deliver(out_2, slot[2], x2, summed[:SEQ])
    new_out_first = put(out_2, slot[2], renewed)
    _, renewed = deliver(state_out, slot[0], x0, summed[:SEQ])
    out_1 = put(state_out, slot[0], renewed)
    _, renewed = deliver(out_1, slot[1], y1, summed[SEQ : 2 * SEQ])
    out_1 = put(out_1, slot[1], renewed)
    _, renewed = deliver(out_1, slot[2], y2, summed[2 * SEQ :])
    new_out = jnp.where(first, new_out_first, put(out_1, slot[2], renewed))

    copies_new = jnp.stack([new_in, new_out])[None]
    return (copies_new, grad_query[None], grad_value[None])


def solution(mesh):
    shape = dict(mesh.shape)
    grid = Mesh(
        mesh.devices.reshape(shape["section"], 4, shape["dp"] // 4, shape["tensor"]),
        ("section", "y", "x", "tensor"),
    )
    dp = ("y", "x")
    return jax.shard_map(
        on_device,
        mesh=grid,
        in_specs=(
            P("section", None, dp, None, "tensor"),
            P("section", dp, None, "tensor"),
            P(None, dp, None, "tensor"),
            P(None, dp),
            P(None, "tensor"),
            P("section", None),
            P("section", dp, "tensor"),
            P("section", dp, "tensor"),
            P("section", dp, "tensor"),
            P("section", "tensor", dp),
            P("section", None, dp, None, None),
        ),
        out_specs=(
            P("section", None, dp, None, "tensor"),
            P("section", dp, "tensor"),
            P("section", dp, "tensor"),
        ),
        check_vma=False,
    )
```

```python
import functools

import jax
import jax.numpy as jnp
from jax import lax
from jax.experimental import pallas as pl
from jax.experimental.pallas import tpu as pltpu
from jax.sharding import Mesh, PartitionSpec as P

HQ = 32
HK = 4
HD = 128
QB = 128
SEQ = 128

eps_norm = 1e-05
qmax = 7.0
f32 = jnp.float32
bf16 = jnp.bfloat16


GROUP = HQ // HK
NT = (((1,), (1,)), ((), ()))
TN = (((0,), (0,)), ((), ()))


def stacked(rows):
    return jnp.concatenate([rows[:, h * HD : (h + 1) * HD] for h in range(GROUP)], axis=0)


def side_by_side(rows):
    return jnp.concatenate([rows[h * SEQ : (h + 1) * SEQ] for h in range(GROUP)], axis=1)


def probs_of(query, key_in):
    scores = lax.dot_general(query, key_in, NT, preferred_element_type=f32) * HD ** (-0.5)
    at = lax.broadcasted_iota(jnp.int32, scores.shape, 0) % SEQ
    key_at = lax.broadcasted_iota(jnp.int32, scores.shape, 1)
    scores = jnp.where(at >= key_at, scores, -1e30)
    weight = jnp.exp(scores - jnp.max(scores, axis=-1, keepdims=True))
    return weight / jnp.sum(weight, axis=-1, keepdims=True)


def attend_unit(qkv):
    wide = GROUP * HD
    probs = probs_of(stacked(qkv[:, :wide]), qkv[:, wide : wide + HD])
    mixed = jnp.dot(probs.astype(bf16), qkv[:, wide + HD :], preferred_element_type=f32)
    return side_by_side(mixed.astype(bf16))


def attend_back_kernel(qkv_ref, d_mixed_ref, out_ref):
    wide = GROUP * HD
    key_in = qkv_ref[:, wide : wide + HD]
    probs = probs_of(stacked(qkv_ref[:, :wide]), key_in)
    d_rows = stacked(d_mixed_ref[...])
    d_probs = lax.dot_general(d_rows, qkv_ref[:, wide + HD :], NT, preferred_element_type=f32)
    d_scores = (
        probs * (d_probs - jnp.sum(d_probs * probs, axis=-1, keepdims=True)) * HD ** (-0.5)
    )
    d_query = jnp.dot(d_scores.astype(bf16), key_in, preferred_element_type=f32).astype(bf16)
    d_value = lax.dot_general(probs.astype(bf16), d_rows, TN, preferred_element_type=f32)
    out_ref[:, :wide] = side_by_side(d_query)
    out_ref[:, wide:] = d_value.astype(bf16)


def attend_back(qkv, d_mixed):
    rows = qkv.shape[0]
    return pl.pallas_call(
        attend_back_kernel,
        grid=(rows // SEQ,),
        in_specs=[
            pl.BlockSpec((SEQ, (GROUP + 2) * HD), lambda u: (u, 0)),
            pl.BlockSpec((SEQ, GROUP * HD), lambda u: (u, 0)),
        ],
        out_specs=pl.BlockSpec((SEQ, (GROUP + 1) * HD), lambda u: (u, 0)),
        out_shape=jax.ShapeDtypeStruct((rows, (GROUP + 1) * HD), bf16),
        compiler_params=pltpu.CompilerParams(vmem_limit_bytes=32 * 1024 * 1024),
        cost_estimate=pl.CostEstimate(
            flops=rows * SEQ * GROUP * HD * 8,
            bytes_accessed=rows * 3456 * 2,
            transcendentals=rows * SEQ * GROUP,
        ),
        name="attend_back",
    )(qkv, d_mixed)


UNITS = 3
ROWS = 16
HALF = 640
HALF_O = 512
ORDER = (0, 3, 1, 2)


def known_b(flags, known_ref, got_refs, x_ref):
    slot_0, slot_1, slot_2 = flags[1], flags[2], flags[3]

    def step(i, carry):
        at = pl.multiple_of(i * ROWS, ROWS)
        for by in range(4):
            j = lax.rem(flags[6] + 4 - by, 4)
            one = known_ref[j, pl.ds(at, ROWS), :]
            two = known_ref[j, pl.ds(at + SEQ, ROWS), :]
            x_0 = jnp.where(slot_0 == 0, one, two)
            one, two = one.astype(f32), two.astype(f32)
            step_1 = got_refs[by][pl.ds(at, ROWS), :].astype(f32)
            step_2 = got_refs[by][pl.ds(at + SEQ, ROWS), :].astype(f32)
            x_1 = (jnp.where(slot_1 == 0, one, two) + step_1).astype(bf16)
            old = jnp.where(
                slot_1 == slot_2, x_1.astype(f32), jnp.where(slot_2 == 0, one, two)
            )
            columns = pl.ds(pl.multiple_of(j * 1024, 1024), 1024)
            x_ref[pl.ds(at, ROWS), columns] = x_0
            x_ref[pl.ds(at + SEQ, ROWS), columns] = x_1
            x_ref[pl.ds(at + 2 * SEQ, ROWS), columns] = (old + step_2).astype(bf16)
        return carry

    lax.fori_loop(0, SEQ // ROWS, step, 0)


def normalize(gain_ref, x_ref):
    def step(i, carry):
        rows = pl.ds(pl.multiple_of(i * ROWS, ROWS), ROWS)
        values = x_ref[rows, :].astype(f32)
        square = jnp.mean(values * values, axis=-1, keepdims=True)
        x_ref[rows, :] = (values * lax.rsqrt(square + eps_norm) * gain_ref[...]).astype(bf16)
        return carry

    lax.fori_loop(0, UNITS * SEQ // ROWS, step, 0)


def prepare_kernel(gain_ref, known_ref, normed_ref):
    def step(i, carry):
        at = pl.multiple_of(i * ROWS, ROWS)
        for j in range(4):
            normed_ref[pl.ds(at, ROWS), j * 1024 : (j + 1) * 1024] = known_ref[
                j, pl.ds(at, ROWS), :
            ]
        return carry

    lax.fori_loop(0, UNITS * SEQ // ROWS, step, 0)
    normalize(gain_ref, normed_ref)


VMEM = pl.BlockSpec(memory_space=pltpu.VMEM)
SMEM = pl.BlockSpec(memory_space=pltpu.SMEM)
ANY = pl.BlockSpec(memory_space=pl.ANY)
GRANT = pltpu.CompilerParams(vmem_limit_bytes=60 * 1024 * 1024)


def prepare(gain, known):
    return pl.pallas_call(
        prepare_kernel,
        in_specs=[VMEM, VMEM],
        out_specs=VMEM,
        out_shape=jax.ShapeDtypeStruct((UNITS * SEQ, 4096), bf16),
        compiler_params=pltpu.CompilerParams(vmem_limit_bytes=32 * 1024 * 1024),
        cost_estimate=pl.CostEstimate(flops=2**23, bytes_accessed=6 * 2**20, transcendentals=0),
        name="prepare",
    )(gain, known)


def fetch(pieces, start, held, sems):
    copies = []
    for at in range(5):
        for half in range(2):
            target = held.at[half, at] if at < 3 else held.at[half, 3, pl.ds(2 * (at - 3), 2)]
            source = pieces[half * 5 + at].at[:, :, pl.ds(start, held.shape[-1])]
            copies.append(pltpu.make_async_copy(source, target, sems.at[2 * at + half]))
            copies[-1].start()
    return copies


def arrived(copies, half, at):
    copies[2 * at + half].wait()
    if at == 3:
        copies[8 + half].wait()


def block_of(flags, half, along, across):
    dy, dx = (along, across) if half == 0 else (across, along)
    return lax.rem(flags[5] + dy, 4) * 4 + lax.rem(flags[4] + dx, 4)


def times_gathered(flags, rows_ref, held, copies):
    totals = [None, None]
    for at in range(4):
        for half in range(2):
            lhs = []
            for block in range(4):
                number = block_of(flags, half, ORDER[at], ORDER[block])
                lhs.append(rows_ref[:, pl.ds(pl.multiple_of(number * 256, 256), 256)])
            arrived(copies, half, at)
            part = jnp.dot(
                jnp.concatenate(lhs, axis=1),
                held[half, at].reshape(1024, held.shape[-1]),
                preferred_element_type=f32,
            )
            totals[half] = part if totals[half] is None else totals[half] + part
    return totals


def project_kernel(flags, pieces, normed_ref, qkv_ref, mixed_ref, held, sems, begin):
    copies = fetch(pieces, 0, held, sems)
    begin()
    totals = times_gathered(flags, normed_ref, held, copies)
    for half in range(2):
        qkv_ref[:, half * HALF : (half + 1) * HALF] = totals[half].astype(bf16)
    for unit in range(UNITS):
        rows = slice(unit * SEQ, (unit + 1) * SEQ)
        mixed_ref[rows, :] = attend_unit(qkv_ref[rows, :])


def project_a_kernel(flags, normed_ref, *refs):
    pieces, (qkv_ref, mixed_ref, held, sems) = refs[:10], refs[10:]
    project_kernel(flags, pieces, normed_ref, qkv_ref, mixed_ref, held, sems, lambda: None)


def project_b_kernel(flags, gain_ref, known_ref, *refs):
    got_refs, pieces = refs[:4], refs[4:14]
    normed_ref, qkv_ref, mixed_ref, held, sems = refs[14:]

    def begin():
        known_b(flags, known_ref, got_refs, normed_ref)
        normalize(gain_ref, normed_ref)

    project_kernel(flags, pieces, normed_ref, qkv_ref, mixed_ref, held, sems, begin)


def with_gathered(kernel, name, operands, pieces, columns, shapes, rows):
    return pl.pallas_call(
        kernel,
        in_specs=[SMEM] + [VMEM] * (len(operands) - 1) + [ANY] * 10,
        out_specs=[VMEM] * len(shapes),
        out_shape=[jax.ShapeDtypeStruct(shape, bf16) for shape in shapes],
        scratch_shapes=[
            pltpu.VMEM((2, 4, 4, 256, columns), bf16),
            pltpu.SemaphoreType.DMA((10,)),
        ],
        compiler_params=GRANT,
        cost_estimate=pl.CostEstimate(
            flops=2 * rows * 4096 * 2 * columns,
            bytes_accessed=4096 * 4 * columns + 6 * 2**20,
            transcendentals=0,
        ),
        name=name,
    )(*operands, *pieces)


def part_outputs(flags, mixed, target, held, store):
    offset = lax.rem(target + 4 - flags[5], 4)
    place = jnp.where(offset == 0, 0, jnp.where(offset == 3, 1, offset + 1))
    for at in range(4):
        part = lax.dot_general(
            mixed[:, :HALF_O], held[0, place, at], NT, preferred_element_type=f32
        ) + lax.dot_general(
            mixed[:, HALF_O:], held[1, at, place], NT, preferred_element_type=f32
        )
        column = pl.multiple_of(lax.rem(flags[4] + ORDER[at], 4) * 256, 256)
        store(pl.ds(column, 256), part.astype(bf16))


def spread_kernel(flags, mixed_ref, *refs):
    pieces, outs, (third_ref, held, sems) = refs[:10], refs[10:14], refs[14:]
    copies = fetch(pieces, HALF, held, sems)
    for copy in copies:
        copy.wait()
    for out, by in zip(outs, (2, 1, 3, 0)):
        target = lax.rem(flags[6] + by, 4)

        def store(columns, part, out=out, target=target):
            out[:, columns] = part[: 2 * SEQ]
            third_ref[target, :, columns] = part[2 * SEQ :]

        part_outputs(flags, mixed_ref[...], target, held, store)


def outputs_kernel(flags, mixed_ref, third_ref, *refs):
    pieces, (out_ref, held, sems) = refs[:10], refs[10:]
    copies = fetch(pieces, HALF, held, sems)
    for copy in copies:
        copy.wait()
    for target in range(4):

        def store(columns, part, target=target):
            out_ref[target, :SEQ, columns] = jnp.where(
                flags[0] == 1, third_ref[target, :, columns], part[:SEQ]
            )
            out_ref[target, SEQ:, columns] = part[SEQ:]

        part_outputs(flags, mixed_ref[...], target, held, store)


def d_mixed_kernel(flags, up_ref, *refs):
    pieces, (out_ref, held, sems) = refs[:10], refs[10:]
    copies = fetch(pieces, HALF, held, sems)
    totals = times_gathered(flags, up_ref, held, copies)
    for half in range(2):
        out_ref[:, half * HALF_O : (half + 1) * HALF_O] = totals[half].astype(bf16)


def along(shard, second, by):
    pairs = []
    for y in range(4):
        for x in range(4):
            by_x, by_y = y * 4 + (x + by) % 4, (y + by) % 4 * 4 + x
            pairs.append((y * 4 + x, by_y if second else by_x))
            pairs.append((16 + y * 4 + x, 16 + (by_x if second else by_y)))
    return lax.ppermute(shard, ("section", "y", "x"), pairs)


def from_first(shard, by, to_section):
    return lax.ppermute(
        shard, ("section", "tensor"), [(i, 4 * to_section + (i + by) % 4) for i in range(4)]
    )


def first_phase(shard):
    before, after, far = along(shard, False, 1), along(shard, False, -1), along(shard, False, 2)
    return jnp.stack([shard, before, after, far]), before


def second_phase(own):
    before, after = along(own, True, 1), along(own, True, -1)
    return [own, before, after, along(before[:2], True, 1), along(after[2:], True, -1)]


def handed_over(pieces, pairs):
    return [lax.ppermute(piece, "section", pairs) for piece in pieces]


def pick(state, slot):
    return jnp.where(slot == 0, state[0], state[1])


def put(state, slot, new, active=True):
    mask = (jnp.arange(2) == slot) & active
    return jnp.where(mask[:, None, None], new[None], state)


def on_device(
    boundary_copies,
    arriving,
    first_delta,
    sample_index,
    exponents,
    norm_gain,
    w_query,
    w_key,
    w_value,
    w_out,
    out_grad,
):
    first = lax.axis_index("section") == 0
    z = lax.axis_index("tensor")

    out_t = w_out[0].T
    side_a = jnp.concatenate([w_query[0, :, :HALF], out_t[:, :HALF_O]], axis=1)
    side_b = jnp.concatenate(
        [w_query[0, :, HALF:], w_key[0], w_value[0], out_t[:, HALF_O:]], axis=1
    )
    kept = jnp.where(first, side_a, side_b)
    swapped = lax.ppermute(jnp.where(first, side_b, side_a), "section", [(0, 1), (1, 0)])
    own_0, begun = first_phase(jnp.where(first, kept, swapped))
    arriving, first_delta, begun = lax.optimization_barrier((arriving, first_delta, begun))
    local_0 = second_phase(own_0)
    shard_1, local_0[1], local_0[2] = lax.optimization_barrier(
        (jnp.where(first, swapped, kept), local_0[1], local_0[2])
    )
    own_1, _ = first_phase(shard_1)
    local_1 = second_phase(own_1)
    pieces_0 = local_0 + handed_over(local_0, [(1, 0)])
    pieces_1 = handed_over(local_1, [(0, 1)]) + local_1

    power = exponents.astype(f32)
    scale_full = jnp.repeat(jnp.exp2(power), QB, axis=1)
    inverse_full = jnp.repeat(jnp.exp2(-power), QB, axis=1)
    scale_in = jnp.where(first, scale_full[0], scale_full[1])
    scale_next = jnp.where(first, scale_full[1], scale_full[2])
    inverse_next = jnp.where(first, inverse_full[1], inverse_full[2])
    slots = sample_index[:, 0]
    slot = [jnp.where(first, slots[k + 1], slots[k]) for k in range(3)]

    def receive(state, at, delta):
        return (pick(state, at).astype(f32) + scale_in * delta.astype(f32)).astype(bf16)

    def deliver(state, at, inputs, summed):
        output = (inputs.astype(f32) + summed).astype(bf16)
        old = pick(state, at)
        sent = jnp.clip(
            (output.astype(f32) - old.astype(f32)) * inverse_next, -qmax, qmax
        ).astype(bf16)
        step = scale_next * sent.astype(f32)
        return step.astype(bf16), (old.astype(f32) + step).astype(bf16)

    state_in, state_out = boundary_copies[0, 0], boundary_copies[0, 1]
    x0 = receive(state_in, slot[0], arriving[0, 0])
    state_in = put(state_in, slot[0], x0)
    x1 = receive(state_in, slot[1], first_delta[0, 0])
    state_1 = put(state_in, slot[1], x1)
    x2 = receive(state_1, slot[2], first_delta[1, 0])
    state_2 = put(state_1, slot[2], x2)
    known = jnp.concatenate(
        [jnp.where(first, x0, state_in[0]), jnp.where(first, x1, state_in[1]), x2], 0
    )
    known = lax.all_to_all(
        jnp.broadcast_to(known[None], (4,) + known.shape),
        "tensor",
        split_axis=0,
        concat_axis=0,
        tiled=True,
    )

    flags = jnp.stack(
        [first.astype(jnp.int32), *slot, lax.axis_index("x"), lax.axis_index("y"), z]
    ).astype(jnp.int32)
    rows = UNITS * SEQ
    normed_a = prepare(norm_gain, known)
    qkv_a, mixed_a = with_gathered(
        project_a_kernel,
        "project_a",
        [flags, normed_a],
        pieces_0,
        HALF,
        [(rows, 2 * HALF), (rows, 1024)],
        rows,
    )
    far, near_1, near_3, own, third = with_gathered(
        spread_kernel,
        "spread",
        [flags, mixed_a],
        pieces_0,
        HALF_O,
        [(2 * SEQ, 1024)] * 4 + [(4, SEQ, 1024)],
        rows,
    )
    parts = [own] + [
        from_first(piece, by, 0) for piece, by in ((far, 2), (near_1, 1), (near_3, 3))
    ]
    summed = sum(part.astype(f32) for part in parts)
    step_0, renewed = deliver(state_out, slot[0], x0, summed[:SEQ])
    out_1 = put(state_out, slot[0], renewed)
    step_1, renewed = deliver(out_1, slot[1], x1, summed[SEQ:])
    out_2 = put(out_1, slot[1], renewed)
    steps = jnp.concatenate([step_0, step_1], 0)
    got = [from_first(steps, by, 1) for by in range(4)]

    def added(state, at, step):
        return (pick(state, at).astype(f32) + step.astype(f32)).astype(bf16)

    normed_b, qkv_b, mixed_b = with_gathered(
        project_b_kernel,
        "project_b",
        [flags, norm_gain, known, *got],
        pieces_1,
        HALF,
        [(rows, 4096), (rows, 2 * HALF), (rows, 1024)],
        rows,
    )
    y1 = added(state_in, slot[1], got[0][:SEQ])
    after_1 = put(state_in, slot[1], y1)
    y2 = added(after_1, slot[2], got[0][SEQ:])
    new_in = jnp.where(first, state_2, put(after_1, slot[2], y2))

    up = out_grad[0, :, 0].reshape(rows, -1)
    (d_mixed_a,) = with_gathered(
        d_mixed_kernel, "d_mixed_a", [flags, up], pieces_0, HALF_O, [(rows, 1024)], rows
    )
    (d_mixed_b,) = with_gathered(
        d_mixed_kernel, "d_mixed_b", [flags, up], pieces_1, HALF_O, [(rows, 1024)], rows
    )
    d_a = attend_back(qkv_a, d_mixed_a)
    d_b = attend_back(qkv_b, d_mixed_b)
    term = lax.dot_general(
        jnp.where(first, normed_a, normed_b),
        jnp.where(first, d_a, d_b),
        TN,
        preferred_element_type=f32,
    ).astype(bf16)
    grad = lax.psum_scatter(term, ("y", "x"), scatter_dimension=0, tiled=True)

    mixed_f, _ = lax.optimization_barrier((mixed_b, term))
    (partial,) = with_gathered(
        outputs_kernel, "outputs", [flags, mixed_f, third], pieces_1, HALF_O, [(4, rows, 1024)], rows
    )
    parts = lax.all_to_all(partial, "tensor", split_axis=0, concat_axis=0, tiled=True)
    summed = jnp.sum(parts.astype(f32), axis=0)
    _, renewed = deliver(out_2, slot[2], x2, summed[:SEQ])
    new_out_first = put(out_2, slot[2], renewed)
    _, renewed = deliver(state_out, slot[0], x0, summed[:SEQ])
    out_1 = put(state_out, slot[0], renewed)
    _, renewed = deliver(out_1, slot[1], y1, summed[SEQ : 2 * SEQ])
    out_1 = put(out_1, slot[1], renewed)
    _, renewed = deliver(out_1, slot[2], y2, summed[2 * SEQ :])
    new_out = jnp.where(first, new_out_first, put(out_1, slot[2], renewed))

    copies_new = jnp.stack([new_in, new_out])[None]
    return (copies_new, grad[None, :, :1024], grad[None, :, 1024:])


def solution(mesh):
    shape = dict(mesh.shape)
    grid = Mesh(
        mesh.devices.reshape(shape["section"], 4, shape["dp"] // 4, shape["tensor"]),
        ("section", "y", "x", "tensor"),
    )
    dp = ("y", "x")
    return jax.shard_map(
        on_device,
        mesh=grid,
        in_specs=(
            P("section", None, dp, None, "tensor"),
            P("section", dp, None, "tensor"),
            P(None, dp, None, "tensor"),
            P(None, dp),
            P(None, "tensor"),
            P("section", None),
            P("section", dp, "tensor"),
            P("section", dp, "tensor"),
            P("section", dp, "tensor"),
            P("section", "tensor", dp),
            P("section", None, dp, None, None),
        ),
        out_specs=(
            P("section", None, dp, None, "tensor"),
            P("section", dp, "tensor"),
            P("section", dp, "tensor"),
        ),
        check_vma=False,
    )
```

```python
import functools

import jax
import jax.numpy as jnp
from jax import lax
from jax.experimental import pallas as pl
from jax.experimental.pallas import tpu as pltpu
from jax.sharding import Mesh, PartitionSpec as P

HQ = 32
HK = 4
HD = 128
QB = 128
SEQ = 128

eps_norm = 1e-05
qmax = 7.0
f32 = jnp.float32
bf16 = jnp.bfloat16


GROUP = HQ // HK
NT = (((1,), (1,)), ((), ()))
TN = (((0,), (0,)), ((), ()))


def stacked(rows):
    return jnp.concatenate([rows[:, h * HD : (h + 1) * HD] for h in range(GROUP)], axis=0)


def side_by_side(rows):
    return jnp.concatenate([rows[h * SEQ : (h + 1) * SEQ] for h in range(GROUP)], axis=1)


def probs_of(query, key_in):
    scores = lax.dot_general(query, key_in, NT, preferred_element_type=f32) * HD ** (-0.5)
    at = lax.broadcasted_iota(jnp.int32, scores.shape, 0) % SEQ
    key_at = lax.broadcasted_iota(jnp.int32, scores.shape, 1)
    scores = jnp.where(at >= key_at, scores, -1e30)
    weight = jnp.exp(scores - jnp.max(scores, axis=-1, keepdims=True))
    return weight / jnp.sum(weight, axis=-1, keepdims=True)


def attend_unit(qkv):
    wide = GROUP * HD
    probs = probs_of(stacked(qkv[:, :wide]), qkv[:, wide : wide + HD])
    mixed = jnp.dot(probs.astype(bf16), qkv[:, wide + HD :], preferred_element_type=f32)
    return side_by_side(mixed.astype(bf16))


def attend_back_kernel(qkv_ref, d_mixed_ref, out_ref):
    wide = GROUP * HD
    key_in = qkv_ref[:, wide : wide + HD]
    probs = probs_of(stacked(qkv_ref[:, :wide]), key_in)
    d_rows = stacked(d_mixed_ref[...])
    d_probs = lax.dot_general(d_rows, qkv_ref[:, wide + HD :], NT, preferred_element_type=f32)
    d_scores = (
        probs * (d_probs - jnp.sum(d_probs * probs, axis=-1, keepdims=True)) * HD ** (-0.5)
    )
    d_query = jnp.dot(d_scores.astype(bf16), key_in, preferred_element_type=f32).astype(bf16)
    d_value = lax.dot_general(probs.astype(bf16), d_rows, TN, preferred_element_type=f32)
    out_ref[:, :wide] = side_by_side(d_query)
    out_ref[:, wide:] = d_value.astype(bf16)


def attend_back(qkv, d_mixed):
    rows = qkv.shape[0]
    return pl.pallas_call(
        attend_back_kernel,
        grid=(rows // SEQ,),
        in_specs=[
            pl.BlockSpec((SEQ, (GROUP + 2) * HD), lambda u: (u, 0)),
            pl.BlockSpec((SEQ, GROUP * HD), lambda u: (u, 0)),
        ],
        out_specs=pl.BlockSpec((SEQ, (GROUP + 1) * HD), lambda u: (u, 0)),
        out_shape=jax.ShapeDtypeStruct((rows, (GROUP + 1) * HD), bf16),
        compiler_params=pltpu.CompilerParams(vmem_limit_bytes=32 * 1024 * 1024),
        cost_estimate=pl.CostEstimate(
            flops=rows * SEQ * GROUP * HD * 8,
            bytes_accessed=rows * 3456 * 2,
            transcendentals=rows * SEQ * GROUP,
        ),
        name="attend_back",
    )(qkv, d_mixed)


UNITS = 3
ROWS = 16
HALF = 640
HALF_O = 512
ORDER = (0, 3, 1, 2)


def known_b(flags, known_ref, got_refs, x_ref):
    slot_0, slot_1, slot_2 = flags[1], flags[2], flags[3]

    def step(i, carry):
        at = pl.multiple_of(i * ROWS, ROWS)
        for by in range(4):
            j = lax.rem(flags[6] + 4 - by, 4)
            one = known_ref[j, pl.ds(at, ROWS), :]
            two = known_ref[j, pl.ds(at + SEQ, ROWS), :]
            x_0 = jnp.where(slot_0 == 0, one, two)
            one, two = one.astype(f32), two.astype(f32)
            step_1 = got_refs[by][pl.ds(at, ROWS), :].astype(f32)
            step_2 = got_refs[by][pl.ds(at + SEQ, ROWS), :].astype(f32)
            x_1 = (jnp.where(slot_1 == 0, one, two) + step_1).astype(bf16)
            old = jnp.where(
                slot_1 == slot_2, x_1.astype(f32), jnp.where(slot_2 == 0, one, two)
            )
            columns = pl.ds(pl.multiple_of(j * 1024, 1024), 1024)
            x_ref[pl.ds(at, ROWS), columns] = x_0
            x_ref[pl.ds(at + SEQ, ROWS), columns] = x_1
            x_ref[pl.ds(at + 2 * SEQ, ROWS), columns] = (old + step_2).astype(bf16)
        return carry

    lax.fori_loop(0, SEQ // ROWS, step, 0)


def normalize(gain_ref, x_ref):
    def step(i, carry):
        rows = pl.ds(pl.multiple_of(i * ROWS, ROWS), ROWS)
        values = x_ref[rows, :].astype(f32)
        square = jnp.mean(values * values, axis=-1, keepdims=True)
        x_ref[rows, :] = (values * lax.rsqrt(square + eps_norm) * gain_ref[...]).astype(bf16)
        return carry

    lax.fori_loop(0, UNITS * SEQ // ROWS, step, 0)


def prepare_kernel(gain_ref, known_ref, normed_ref):
    def step(i, carry):
        at = pl.multiple_of(i * ROWS, ROWS)
        for j in range(4):
            normed_ref[pl.ds(at, ROWS), j * 1024 : (j + 1) * 1024] = known_ref[
                j, pl.ds(at, ROWS), :
            ]
        return carry

    lax.fori_loop(0, UNITS * SEQ // ROWS, step, 0)
    normalize(gain_ref, normed_ref)


VMEM = pl.BlockSpec(memory_space=pltpu.VMEM)
SMEM = pl.BlockSpec(memory_space=pltpu.SMEM)
ANY = pl.BlockSpec(memory_space=pl.ANY)
GRANT = pltpu.CompilerParams(vmem_limit_bytes=60 * 1024 * 1024)


def prepare(gain, known):
    return pl.pallas_call(
        prepare_kernel,
        in_specs=[VMEM, VMEM],
        out_specs=VMEM,
        out_shape=jax.ShapeDtypeStruct((UNITS * SEQ, 4096), bf16),
        compiler_params=pltpu.CompilerParams(vmem_limit_bytes=32 * 1024 * 1024),
        cost_estimate=pl.CostEstimate(flops=2**23, bytes_accessed=6 * 2**20, transcendentals=0),
        name="prepare",
    )(gain, known)


def chunks(pieces, start, held, sems):
    copies = []
    for at in range(5):
        for half in range(2):
            target = held.at[half, at] if at < 3 else held.at[half, 3, pl.ds(2 * (at - 3), 2)]
            source = pieces[half * 5 + at].at[:, :, pl.ds(start, held.shape[-1])]
            copies.append(pltpu.make_async_copy(source, target, sems.at[2 * at + half]))
    return copies


def fetch(pieces, start, held, sems):
    copies = chunks(pieces, start, held, sems)
    for copy in copies:
        copy.start()
    return copies


def arrived(copies, half, at):
    copies[2 * at + half].wait()
    if at == 3:
        copies[8 + half].wait()
    elif at < 2:
        copies[2 * at + half + 4].start()
        if at == 1:
            copies[8 + half].start()


def block_of(flags, half, along, across):
    dy, dx = (along, across) if half == 0 else (across, along)
    return lax.rem(flags[5] + dy, 4) * 4 + lax.rem(flags[4] + dx, 4)


def times_gathered(flags, rows_ref, held, copies):
    totals = [None, None]
    for at in range(4):
        for half in range(2):
            lhs = []
            for block in range(4):
                number = block_of(flags, half, ORDER[at], ORDER[block])
                lhs.append(rows_ref[:, pl.ds(pl.multiple_of(number * 256, 256), 256)])
            arrived(copies, half, at)
            part = jnp.dot(
                jnp.concatenate(lhs, axis=1),
                held[half, at].reshape(1024, held.shape[-1]),
                preferred_element_type=f32,
            )
            totals[half] = part if totals[half] is None else totals[half] + part
    return totals


def project_kernel(flags, pieces, normed_ref, qkv_ref, mixed_ref, held, sems, begin):
    copies = chunks(pieces, 0, held, sems)
    for copy in copies[:4]:
        copy.start()
    begin()
    totals = times_gathered(flags, normed_ref, held, copies)
    for half in range(2):
        qkv_ref[:, half * HALF : (half + 1) * HALF] = totals[half].astype(bf16)
    for unit in range(UNITS):
        rows = slice(unit * SEQ, (unit + 1) * SEQ)
        mixed_ref[rows, :] = attend_unit(qkv_ref[rows, :])


def project_a_kernel(flags, normed_ref, *refs):
    pieces, (qkv_ref, mixed_ref, held, sems) = refs[:10], refs[10:]
    project_kernel(flags, pieces, normed_ref, qkv_ref, mixed_ref, held, sems, lambda: None)


def project_b_kernel(flags, gain_ref, known_ref, *refs):
    got_refs, pieces = refs[:4], refs[4:14]
    normed_ref, qkv_ref, mixed_ref, held, sems = refs[14:]

    def begin():
        known_b(flags, known_ref, got_refs, normed_ref)
        normalize(gain_ref, normed_ref)

    project_kernel(flags, pieces, normed_ref, qkv_ref, mixed_ref, held, sems, begin)


def with_gathered(kernel, name, operands, pieces, columns, shapes, rows):
    return pl.pallas_call(
        kernel,
        in_specs=[SMEM] + [VMEM] * (len(operands) - 1) + [ANY] * 10,
        out_specs=[VMEM] * len(shapes),
        out_shape=[jax.ShapeDtypeStruct(shape, bf16) for shape in shapes],
        scratch_shapes=[
            pltpu.VMEM((2, 4, 4, 256, columns), bf16),
            pltpu.SemaphoreType.DMA((10,)),
        ],
        compiler_params=GRANT,
        cost_estimate=pl.CostEstimate(
            flops=2 * rows * 4096 * 2 * columns,
            bytes_accessed=4096 * 4 * columns + 6 * 2**20,
            transcendentals=0,
        ),
        name=name,
    )(*operands, *pieces)


def part_outputs(flags, mixed, target, held, store):
    offset = lax.rem(target + 4 - flags[5], 4)
    place = jnp.where(offset == 0, 0, jnp.where(offset == 3, 1, offset + 1))
    for at in range(4):
        part = lax.dot_general(
            mixed[:, :HALF_O], held[0, place, at], NT, preferred_element_type=f32
        ) + lax.dot_general(
            mixed[:, HALF_O:], held[1, at, place], NT, preferred_element_type=f32
        )
        column = pl.multiple_of(lax.rem(flags[4] + ORDER[at], 4) * 256, 256)
        store(pl.ds(column, 256), part.astype(bf16))


def spread_kernel(flags, mixed_ref, *refs):
    pieces, outs, (third_ref, held, sems) = refs[:10], refs[10:14], refs[14:]
    copies = fetch(pieces, HALF, held, sems)
    for copy in copies:
        copy.wait()
    for out, by in zip(outs, (2, 1, 3, 0)):
        target = lax.rem(flags[6] + by, 4)

        def store(columns, part, out=out, target=target):
            out[:, columns] = part[: 2 * SEQ]
            third_ref[target, :, columns] = part[2 * SEQ :]

        part_outputs(flags, mixed_ref[...], target, held, store)


def outputs_kernel(flags, mixed_ref, third_ref, *refs):
    pieces, (out_ref, held, sems) = refs[:10], refs[10:]
    copies = fetch(pieces, HALF, held, sems)
    for copy in copies:
        copy.wait()
    for target in range(4):

        def store(columns, part, target=target):
            out_ref[target, :SEQ, columns] = jnp.where(
                flags[0] == 1, third_ref[target, :, columns], part[:SEQ]
            )
            out_ref[target, SEQ:, columns] = part[SEQ:]

        part_outputs(flags, mixed_ref[...], target, held, store)


def d_mixed_kernel(flags, up_ref, *refs):
    pieces, (out_ref, held, sems) = refs[:10], refs[10:]
    copies = chunks(pieces, HALF, held, sems)
    for copy in copies[:4]:
        copy.start()
    totals = times_gathered(flags, up_ref, held, copies)
    for half in range(2):
        out_ref[:, half * HALF_O : (half + 1) * HALF_O] = totals[half].astype(bf16)


def along(shard, second, by):
    pairs = []
    for y in range(4):
        for x in range(4):
            by_x, by_y = y * 4 + (x + by) % 4, (y + by) % 4 * 4 + x
            pairs.append((y * 4 + x, by_y if second else by_x))
            pairs.append((16 + y * 4 + x, 16 + (by_x if second else by_y)))
    return lax.ppermute(shard, ("section", "y", "x"), pairs)


def from_first(shard, by, to_section):
    return lax.ppermute(
        shard, ("section", "tensor"), [(i, 4 * to_section + (i + by) % 4) for i in range(4)]
    )


def first_phase(shard):
    before, after, far = along(shard, False, 1), along(shard, False, -1), along(shard, False, 2)
    return jnp.stack([shard, before, after, far])


def second_phase(own):
    before, after = along(own, True, 1), along(own, True, -1)
    return [own, before, after, along(before[:2], True, 1), along(after[2:], True, -1)]


def handed_over(pieces, pairs):
    return [lax.ppermute(piece, "section", pairs) for piece in pieces]


def pick(state, slot):
    return jnp.where(slot == 0, state[0], state[1])


def put(state, slot, new, active=True):
    mask = (jnp.arange(2) == slot) & active
    return jnp.where(mask[:, None, None], new[None], state)


def on_device(
    boundary_copies,
    arriving,
    first_delta,
    sample_index,
    exponents,
    norm_gain,
    w_query,
    w_key,
    w_value,
    w_out,
    out_grad,
):
    first = lax.axis_index("section") == 0
    z = lax.axis_index("tensor")

    out_t = w_out[0].T
    side_a = jnp.concatenate([w_query[0, :, :HALF], out_t[:, :HALF_O]], axis=1)
    side_b = jnp.concatenate(
        [w_query[0, :, HALF:], w_key[0], w_value[0], out_t[:, HALF_O:]], axis=1
    )
    kept = jnp.where(first, side_a, side_b)
    swapped = lax.ppermute(jnp.where(first, side_b, side_a), "section", [(0, 1), (1, 0)])
    local_0 = second_phase(first_phase(jnp.where(first, kept, swapped)))
    shard_1, local_0[3], local_0[4] = lax.optimization_barrier(
        (jnp.where(first, swapped, kept), local_0[3], local_0[4])
    )
    local_1 = second_phase(first_phase(shard_1))
    pieces_0 = local_0 + handed_over(local_0, [(1, 0)])
    pieces_1 = handed_over(local_1, [(0, 1)]) + local_1

    power = exponents.astype(f32)
    scale_full = jnp.repeat(jnp.exp2(power), QB, axis=1)
    inverse_full = jnp.repeat(jnp.exp2(-power), QB, axis=1)
    scale_in = jnp.where(first, scale_full[0], scale_full[1])
    scale_next = jnp.where(first, scale_full[1], scale_full[2])
    inverse_next = jnp.where(first, inverse_full[1], inverse_full[2])
    slots = sample_index[:, 0]
    slot = [jnp.where(first, slots[k + 1], slots[k]) for k in range(3)]

    def receive(state, at, delta):
        return (pick(state, at).astype(f32) + scale_in * delta.astype(f32)).astype(bf16)

    def deliver(state, at, inputs, summed):
        output = (inputs.astype(f32) + summed).astype(bf16)
        old = pick(state, at)
        sent = jnp.clip(
            (output.astype(f32) - old.astype(f32)) * inverse_next, -qmax, qmax
        ).astype(bf16)
        step = scale_next * sent.astype(f32)
        return step.astype(bf16), (old.astype(f32) + step).astype(bf16)

    state_in, state_out = boundary_copies[0, 0], boundary_copies[0, 1]
    x0 = receive(state_in, slot[0], arriving[0, 0])
    state_in = put(state_in, slot[0], x0)
    x1 = receive(state_in, slot[1], first_delta[0, 0])
    state_1 = put(state_in, slot[1], x1)
    x2 = receive(state_1, slot[2], first_delta[1, 0])
    state_2 = put(state_1, slot[2], x2)
    known = jnp.concatenate(
        [jnp.where(first, x0, state_in[0]), jnp.where(first, x1, state_in[1]), x2], 0
    )
    known = lax.all_gather(known, "tensor")

    flags = jnp.stack(
        [first.astype(jnp.int32), *slot, lax.axis_index("x"), lax.axis_index("y"), z]
    ).astype(jnp.int32)
    rows = UNITS * SEQ
    normed_a = prepare(norm_gain, known)
    qkv_a, mixed_a = with_gathered(
        project_a_kernel,
        "project_a",
        [flags, normed_a],
        pieces_0,
        HALF,
        [(rows, 2 * HALF), (rows, 1024)],
        rows,
    )
    far, near_1, near_3, own, third = with_gathered(
        spread_kernel,
        "spread",
        [flags, mixed_a],
        pieces_0,
        HALF_O,
        [(2 * SEQ, 1024)] * 4 + [(4, SEQ, 1024)],
        rows,
    )
    parts = [own] + [
        from_first(piece, by, 0) for piece, by in ((far, 2), (near_1, 1), (near_3, 3))
    ]
    up = out_grad[0, :, 0].reshape(rows, -1)
    (d_mixed_a,) = with_gathered(
        d_mixed_kernel, "d_mixed_a", [flags, up], pieces_0, HALF_O, [(rows, 1024)], rows
    )
    d_a = attend_back(qkv_a, d_mixed_a)
    *parts, d_a = lax.optimization_barrier((*parts, d_a))
    summed = sum(part.astype(f32) for part in parts)
    step_0, renewed = deliver(state_out, slot[0], x0, summed[:SEQ])
    out_1 = put(state_out, slot[0], renewed)
    step_1, renewed = deliver(out_1, slot[1], x1, summed[SEQ:])
    out_2 = put(out_1, slot[1], renewed)
    steps = jnp.concatenate([step_0, step_1], 0)
    got = [from_first(steps, by, 1) for by in range(4)]
    (d_mixed_b,) = with_gathered(
        d_mixed_kernel, "d_mixed_b", [flags, up], pieces_1, HALF_O, [(rows, 1024)], rows
    )
    *got, d_mixed_b = lax.optimization_barrier((*got, d_mixed_b))

    def added(state, at, step):
        return (pick(state, at).astype(f32) + step.astype(f32)).astype(bf16)

    normed_b, qkv_b, mixed_b = with_gathered(
        project_b_kernel,
        "project_b",
        [flags, norm_gain, known, *got],
        pieces_1,
        HALF,
        [(rows, 4096), (rows, 2 * HALF), (rows, 1024)],
        rows,
    )
    y1 = added(state_in, slot[1], got[0][:SEQ])
    after_1 = put(state_in, slot[1], y1)
    y2 = added(after_1, slot[2], got[0][SEQ:])
    new_in = jnp.where(first, state_2, put(after_1, slot[2], y2))

    d_b = attend_back(qkv_b, d_mixed_b)
    term = lax.dot_general(
        jnp.where(first, normed_a, normed_b),
        jnp.where(first, d_a, d_b),
        TN,
        preferred_element_type=f32,
    ).astype(bf16)
    grad = lax.psum_scatter(term, ("y", "x"), scatter_dimension=0, tiled=True)

    mixed_f, _ = lax.optimization_barrier((mixed_b, term))
    (partial,) = with_gathered(
        outputs_kernel, "outputs", [flags, mixed_f, third], pieces_1, HALF_O, [(4, rows, 1024)], rows
    )
    parts = lax.all_to_all(partial, "tensor", split_axis=0, concat_axis=0, tiled=True)
    summed = jnp.sum(parts.astype(f32), axis=0)
    _, renewed = deliver(out_2, slot[2], x2, summed[:SEQ])
    new_out_first = put(out_2, slot[2], renewed)
    _, renewed = deliver(state_out, slot[0], x0, summed[:SEQ])
    out_1 = put(state_out, slot[0], renewed)
    _, renewed = deliver(out_1, slot[1], y1, summed[SEQ : 2 * SEQ])
    out_1 = put(out_1, slot[1], renewed)
    _, renewed = deliver(out_1, slot[2], y2, summed[2 * SEQ :])
    new_out = jnp.where(first, new_out_first, put(out_1, slot[2], renewed))

    copies_new = jnp.stack([new_in, new_out])[None]
    return (copies_new, grad[None, :, :1024], grad[None, :, 1024:])


def solution(mesh):
    shape = dict(mesh.shape)
    grid = Mesh(
        mesh.devices.reshape(shape["section"], 4, shape["dp"] // 4, shape["tensor"]),
        ("section", "y", "x", "tensor"),
    )
    dp = ("y", "x")
    return jax.shard_map(
        on_device,
        mesh=grid,
        in_specs=(
            P("section", None, dp, None, "tensor"),
            P("section", dp, None, "tensor"),
            P(None, dp, None, "tensor"),
            P(None, dp),
            P(None, "tensor"),
            P("section", None),
            P("section", dp, "tensor"),
            P("section", dp, "tensor"),
            P("section", dp, "tensor"),
            P("section", "tensor", dp),
            P("section", None, dp, None, None),
        ),
        out_specs=(
            P("section", None, dp, None, "tensor"),
            P("section", dp, "tensor"),
            P("section", dp, "tensor"),
        ),
        check_vma=False,
    )
```

```python
import functools

import jax
import jax.numpy as jnp
from jax import lax
from jax.experimental import pallas as pl
from jax.experimental.pallas import tpu as pltpu
from jax.sharding import Mesh, PartitionSpec as P

HQ = 32
HK = 4
HD = 128
QB = 128
SEQ = 128

eps_norm = 1e-05
qmax = 7.0
f32 = jnp.float32
bf16 = jnp.bfloat16


GROUP = HQ // HK
NT = (((1,), (1,)), ((), ()))
TN = (((0,), (0,)), ((), ()))


def stacked(rows):
    return jnp.concatenate([rows[:, h * HD : (h + 1) * HD] for h in range(GROUP)], axis=0)


def side_by_side(rows):
    return jnp.concatenate([rows[h * SEQ : (h + 1) * SEQ] for h in range(GROUP)], axis=1)


def probs_of(query, key_in):
    scores = lax.dot_general(query, key_in, NT, preferred_element_type=f32) * HD ** (-0.5)
    at = lax.broadcasted_iota(jnp.int32, scores.shape, 0) % SEQ
    key_at = lax.broadcasted_iota(jnp.int32, scores.shape, 1)
    scores = jnp.where(at >= key_at, scores, -1e30)
    weight = jnp.exp(scores - jnp.max(scores, axis=-1, keepdims=True))
    return weight / jnp.sum(weight, axis=-1, keepdims=True)


def attend_unit(qkv):
    wide = GROUP * HD
    probs = probs_of(stacked(qkv[:, :wide]), qkv[:, wide : wide + HD])
    mixed = jnp.dot(probs.astype(bf16), qkv[:, wide + HD :], preferred_element_type=f32)
    return side_by_side(mixed.astype(bf16))


def attend_back_kernel(qkv_ref, d_mixed_ref, out_ref):
    wide = GROUP * HD
    key_in = qkv_ref[:, wide : wide + HD]
    probs = probs_of(stacked(qkv_ref[:, :wide]), key_in)
    d_rows = stacked(d_mixed_ref[...])
    d_probs = lax.dot_general(d_rows, qkv_ref[:, wide + HD :], NT, preferred_element_type=f32)
    d_scores = (
        probs * (d_probs - jnp.sum(d_probs * probs, axis=-1, keepdims=True)) * HD ** (-0.5)
    )
    d_query = jnp.dot(d_scores.astype(bf16), key_in, preferred_element_type=f32).astype(bf16)
    d_value = lax.dot_general(probs.astype(bf16), d_rows, TN, preferred_element_type=f32)
    out_ref[:, :wide] = side_by_side(d_query)
    out_ref[:, wide:] = d_value.astype(bf16)


def attend_back(qkv, d_mixed):
    rows = qkv.shape[0]
    return pl.pallas_call(
        attend_back_kernel,
        grid=(rows // SEQ,),
        in_specs=[
            pl.BlockSpec((SEQ, (GROUP + 2) * HD), lambda u: (u, 0)),
            pl.BlockSpec((SEQ, GROUP * HD), lambda u: (u, 0)),
        ],
        out_specs=pl.BlockSpec((SEQ, (GROUP + 1) * HD), lambda u: (u, 0)),
        out_shape=jax.ShapeDtypeStruct((rows, (GROUP + 1) * HD), bf16),
        compiler_params=pltpu.CompilerParams(vmem_limit_bytes=32 * 1024 * 1024),
        cost_estimate=pl.CostEstimate(
            flops=rows * SEQ * GROUP * HD * 8,
            bytes_accessed=rows * 3456 * 2,
            transcendentals=rows * SEQ * GROUP,
        ),
        name="attend_back",
    )(qkv, d_mixed)


ROWS = 16
ORDER = (0, 3, 1, 2)


def known_a(flags, known_ref, x_ref):
    from_0 = (flags[0] == 1) | (flags[1] == 0)

    def step(i, carry):
        at = pl.multiple_of(i * ROWS, ROWS)
        for j in range(4):
            one = known_ref[j, pl.ds(at, ROWS), :]
            two = known_ref[j, pl.ds(at + SEQ, ROWS), :]
            columns = slice(j * 1024, (j + 1) * 1024)
            x_ref[pl.ds(at, ROWS), columns] = jnp.where(from_0, one, two)
            x_ref[pl.ds(at + SEQ, ROWS), columns] = two
        return carry

    lax.fori_loop(0, SEQ // ROWS, step, 0)


def known_b(flags, known_ref, got_refs, x_ref):
    first = flags[0] == 1
    slot_1, slot_2 = flags[2], flags[3]

    def step(i, carry):
        at = pl.multiple_of(i * ROWS, ROWS)
        for by in range(4):
            j = lax.rem(flags[6] + 4 - by, 4)
            one = known_ref[j, pl.ds(at, ROWS), :].astype(f32)
            two = known_ref[j, pl.ds(at + SEQ, ROWS), :].astype(f32)
            third = known_ref[j, pl.ds(at + 2 * SEQ, ROWS), :]
            step_1 = got_refs[by][pl.ds(at, ROWS), :].astype(f32)
            step_2 = got_refs[by][pl.ds(at + SEQ, ROWS), :].astype(f32)
            x_1 = (jnp.where(slot_1 == 0, one, two) + step_1).astype(bf16)
            old = jnp.where(
                slot_1 == slot_2, x_1.astype(f32), jnp.where(slot_2 == 0, one, two)
            )
            columns = pl.ds(pl.multiple_of(j * 1024, 1024), 1024)
            x_ref[pl.ds(at, ROWS), columns] = jnp.where(first, third, x_1)
            x_ref[pl.ds(at + SEQ, ROWS), columns] = (old + step_2).astype(bf16)
        return carry

    lax.fori_loop(0, SEQ // ROWS, step, 0)


def normalize(gain_ref, x_ref):
    def step(i, carry):
        rows = pl.ds(pl.multiple_of(i * ROWS, ROWS), ROWS)
        values = x_ref[rows, :].astype(f32)
        square = jnp.mean(values * values, axis=-1, keepdims=True)
        x_ref[rows, :] = (values * lax.rsqrt(square + eps_norm) * gain_ref[...]).astype(bf16)
        return carry

    lax.fori_loop(0, 2 * SEQ // ROWS, step, 0)


def prepare_kernel(flags, gain_ref, known_ref, normed_ref):
    known_a(flags, known_ref, normed_ref)
    normalize(gain_ref, normed_ref)


VMEM = pl.BlockSpec(memory_space=pltpu.VMEM)
SMEM = pl.BlockSpec(memory_space=pltpu.SMEM)
ANY = pl.BlockSpec(memory_space=pl.ANY)
GRANT = pltpu.CompilerParams(vmem_limit_bytes=60 * 1024 * 1024)


def prepare(flags, gain, known):
    return pl.pallas_call(
        prepare_kernel,
        in_specs=[SMEM, VMEM, VMEM],
        out_specs=VMEM,
        out_shape=jax.ShapeDtypeStruct((2 * SEQ, 4096), bf16),
        compiler_params=pltpu.CompilerParams(vmem_limit_bytes=32 * 1024 * 1024),
        cost_estimate=pl.CostEstimate(flops=2**23, bytes_accessed=5 * 2**20, transcendentals=0),
        name="prepare",
    )(flags, gain, known)


def project_kernel(flags, pieces, normed_ref, qkv_ref, mixed_ref, held, held_kv, sems, begin):
    full_ref, pieces = pieces[0], pieces[1:]
    copies = []
    for at in range(5):
        target = held.at[at] if at < 3 else held.at[3, pl.ds(2 * (at - 3), 2)]
        copies.append(pltpu.make_async_copy(pieces[at], target, sems.at[at]))
    copies.append(pltpu.make_async_copy(full_ref.at[:, pl.ds(1024, 256)], held_kv, sems.at[5]))
    for copy in copies:
        copy.start()
    begin()
    total = None
    for at in range(4):
        lhs = []
        for block in range(4):
            second, inner = ORDER[at], ORDER[block]
            dy = jnp.where(flags[0] == 1, second, inner)
            dx = jnp.where(flags[0] == 1, inner, second)
            row = lax.rem(flags[5] + dy, 4) * 4 + lax.rem(flags[4] + dx, 4)
            lhs.append(normed_ref[:, pl.ds(pl.multiple_of(row * 256, 256), 256)])
        copies[at].wait()
        if at == 3:
            copies[4].wait()
        part = jnp.dot(
            jnp.concatenate(lhs, axis=1), held[at].reshape(1024, 1024), preferred_element_type=f32
        )
        total = part if total is None else total + part
    qkv_ref[:, :1024] = total.astype(bf16)
    copies[5].wait()
    qkv_ref[:, 1024:] = jnp.dot(
        normed_ref[...], held_kv[...], preferred_element_type=f32
    ).astype(bf16)
    for unit in range(2):
        rows = slice(unit * SEQ, (unit + 1) * SEQ)
        mixed_ref[rows, :] = attend_unit(qkv_ref[rows, :])


def project_a_kernel(flags, normed_ref, *refs):
    pieces, (qkv_ref, mixed_ref, held, held_kv, sems) = refs[:6], refs[6:]
    project_kernel(flags, pieces, normed_ref, qkv_ref, mixed_ref, held, held_kv, sems, lambda: None)


def project_b_kernel(flags, gain_ref, known_ref, *refs):
    got_refs, pieces = refs[:4], refs[4:10]
    normed_ref, qkv_ref, mixed_ref, held, held_kv, sems = refs[10:]

    def begin():
        known_b(flags, known_ref, got_refs, normed_ref)
        normalize(gain_ref, normed_ref)

    project_kernel(flags, pieces, normed_ref, qkv_ref, mixed_ref, held, held_kv, sems, begin)


def project_call(kernel, name, operands, pieces, with_normed):
    rows = 2 * SEQ
    shapes = [
        jax.ShapeDtypeStruct((rows, 4096), bf16),
        jax.ShapeDtypeStruct((rows, (GROUP + 2) * HD), bf16),
        jax.ShapeDtypeStruct((rows, GROUP * HD), bf16),
    ][0 if with_normed else 1 :]
    return pl.pallas_call(
        kernel,
        in_specs=[SMEM] + [VMEM] * (len(operands) - 1) + [ANY] * 6,
        out_specs=[VMEM] * len(shapes),
        out_shape=shapes,
        scratch_shapes=[
            pltpu.VMEM((4, 4, 256, 1024), bf16),
            pltpu.VMEM((4096, 256), bf16),
            pltpu.SemaphoreType.DMA((6,)),
        ],
        compiler_params=GRANT,
        cost_estimate=pl.CostEstimate(
            flops=2 * rows * 4096 * 1280, bytes_accessed=18 * 2**20, transcendentals=rows * 1024
        ),
        name=name,
    )(*operands, *pieces)


def spread_kernel(flags, mixed_ref, full_ref, *refs):
    outs, (held, sems) = refs[:4], refs[4:]
    copies = []
    for i, by in enumerate((2, 1, 3, 0)):
        row = pl.multiple_of(lax.rem(flags[6] + by, 4) * 1024, 1024)
        copies.append(
            pltpu.make_async_copy(full_ref.at[pl.ds(row, 1024), pl.ds(0, 1024)], held.at[i], sems.at[i])
        )
        copies[-1].start()
    for i in range(4):
        copies[i].wait()
        outs[i][...] = lax.dot_general(
            mixed_ref[...], held[i], NT, preferred_element_type=f32
        ).astype(bf16)


def spread(flags, mixed, full):
    rows = mixed.shape[0]
    return pl.pallas_call(
        spread_kernel,
        in_specs=[SMEM, VMEM, ANY],
        out_specs=[VMEM] * 4,
        out_shape=[jax.ShapeDtypeStruct((rows, 1024), bf16)] * 4,
        scratch_shapes=[pltpu.VMEM((4, 1024, 1024), bf16), pltpu.SemaphoreType.DMA((4,))],
        compiler_params=GRANT,
        cost_estimate=pl.CostEstimate(
            flops=2 * rows * 4096 * 1024, bytes_accessed=12 * 2**20, transcendentals=0
        ),
        name="spread",
    )(flags, mixed, full)


def along(shard, second, by):
    pairs = []
    for y in range(4):
        for x in range(4):
            by_x, by_y = y * 4 + (x + by) % 4, (y + by) % 4 * 4 + x
            pairs.append((y * 4 + x, by_y if second else by_x))
            pairs.append((16 + y * 4 + x, 16 + (by_x if second else by_y)))
    return lax.ppermute(shard, ("section", "y", "x"), pairs)


def from_first(shard, by, to_section):
    return lax.ppermute(
        shard, ("section", "tensor"), [(i, 4 * to_section + (i + by) % 4) for i in range(4)]
    )


def gathered(shard):
    before, after, far = along(shard, False, 1), along(shard, False, -1), along(shard, False, 2)
    own = jnp.stack([shard, before, after, far])
    before, after = along(own, True, 1), along(own, True, -1)
    return [own, before, after, along(before[:2], True, 1), along(after[2:], True, -1)]


def pick(state, slot):
    return jnp.where(slot == 0, state[0], state[1])


def put(state, slot, new, active=True):
    mask = (jnp.arange(2) == slot) & active
    return jnp.where(mask[:, None, None], new[None], state)


def on_device(
    boundary_copies,
    arriving,
    first_delta,
    sample_index,
    exponents,
    norm_gain,
    w_query,
    w_key,
    w_value,
    w_out,
    out_grad,
):
    first = lax.axis_index("section") == 0
    z = lax.axis_index("tensor")

    packed = jnp.concatenate([w_out[0].T, w_key[0], w_value[0]], axis=1)
    arriving, first_delta, packed = lax.optimization_barrier((arriving, first_delta, packed))
    full = lax.all_gather(packed, ("y", "x"), axis=0, tiled=True)
    full_o = full[:, :1024]
    pieces = [full] + gathered(w_query[0])

    power = exponents.astype(f32)
    scale_full = jnp.repeat(jnp.exp2(power), QB, axis=1)
    inverse_full = jnp.repeat(jnp.exp2(-power), QB, axis=1)
    scale_in = jnp.where(first, scale_full[0], scale_full[1])
    scale_next = jnp.where(first, scale_full[1], scale_full[2])
    inverse_next = jnp.where(first, inverse_full[1], inverse_full[2])
    slots = sample_index[:, 0]
    slot = [jnp.where(first, slots[k + 1], slots[k]) for k in range(3)]

    def receive(state, at, delta):
        return (pick(state, at).astype(f32) + scale_in * delta.astype(f32)).astype(bf16)

    def deliver(state, at, inputs, summed):
        output = (inputs.astype(f32) + summed).astype(bf16)
        old = pick(state, at)
        sent = jnp.clip(
            (output.astype(f32) - old.astype(f32)) * inverse_next, -qmax, qmax
        ).astype(bf16)
        step = scale_next * sent.astype(f32)
        return step.astype(bf16), (old.astype(f32) + step).astype(bf16)

    state_in, state_out = boundary_copies[0, 0], boundary_copies[0, 1]
    x0 = receive(state_in, slot[0], arriving[0, 0])
    state_in = put(state_in, slot[0], x0)
    x1 = receive(state_in, slot[1], first_delta[0, 0])
    state_1 = put(state_in, slot[1], x1)
    x2 = receive(state_1, slot[2], first_delta[1, 0])
    state_2 = put(state_1, slot[2], x2)
    known = jnp.concatenate(
        [jnp.where(first, x0, state_in[0]), jnp.where(first, x1, state_in[1]), x2], 0
    )
    known = lax.all_to_all(
        jnp.broadcast_to(known[None], (4,) + known.shape),
        "tensor",
        split_axis=0,
        concat_axis=0,
        tiled=True,
    )

    flags = jnp.stack(
        [first.astype(jnp.int32), *slot, lax.axis_index("x"), lax.axis_index("y"), z]
    ).astype(jnp.int32)
    normed_a = prepare(flags, norm_gain, known)
    qkv_a, mixed_a = project_call(project_a_kernel, "project_a", [flags, normed_a], pieces, False)
    far, near_1, near_3, own = spread(flags, mixed_a, full)
    parts = [own] + [
        from_first(piece, by, 0) for piece, by in ((far, 2), (near_1, 1), (near_3, 3))
    ]
    summed = sum(part.astype(f32) for part in parts)
    step_0, renewed = deliver(state_out, slot[0], x0, summed[:SEQ])
    out_1 = put(state_out, slot[0], renewed)
    step_1, renewed = deliver(out_1, slot[1], x1, summed[SEQ:])
    out_2 = put(out_1, slot[1], renewed)
    steps = jnp.concatenate([step_0, step_1], 0)
    got = [from_first(steps, by, 1) for by in range(4)]

    def added(state, at, step):
        return (pick(state, at).astype(f32) + step.astype(f32)).astype(bf16)

    normed_b, qkv_b, mixed_b = project_call(
        project_b_kernel, "project_b", [flags, norm_gain, known, *got], pieces, True
    )
    y1 = added(state_in, slot[1], got[0][:SEQ])
    after_1 = put(state_in, slot[1], y1)
    y2 = added(after_1, slot[2], got[0][SEQ:])
    new_in = jnp.where(first, state_2, put(after_1, slot[2], y2))

    up = out_grad[0, :, 0].reshape(3 * SEQ, -1)
    d_mixed = jnp.dot(up, full_o, preferred_element_type=f32).astype(bf16)
    d_a = attend_back(qkv_a, d_mixed[: 2 * SEQ])
    d_mixed_b = jnp.concatenate(
        [jnp.where(first, d_mixed[2 * SEQ :], d_mixed[SEQ : 2 * SEQ]), d_mixed[2 * SEQ :]], 0
    )
    d_b = attend_back(qkv_b, d_mixed_b)

    def three(a, b):
        return jnp.concatenate([a[:SEQ], jnp.where(first, a[SEQ:], b[SEQ:]), b[:SEQ]], 0)

    term = lax.dot_general(
        three(normed_a, normed_b), three(d_a, d_b), TN, preferred_element_type=f32
    ).astype(bf16)
    grad = lax.psum_scatter(term, ("y", "x"), scatter_dimension=0, tiled=True)

    mixed_f = jnp.concatenate([jnp.where(first, mixed_b[:SEQ], mixed_a[:SEQ]), mixed_b], 0)
    mixed_f, _ = lax.optimization_barrier((mixed_f, term))
    partial = lax.dot_general(mixed_f, full_o, NT, preferred_element_type=f32).astype(bf16)
    parts = partial.reshape(3 * SEQ, 4, -1).swapaxes(0, 1)
    parts = lax.all_to_all(parts, "tensor", split_axis=0, concat_axis=0, tiled=True)
    summed = jnp.sum(parts.astype(f32), axis=0)
    _, renewed = deliver(out_2, slot[2], x2, summed[:SEQ])
    new_out_first = put(out_2, slot[2], renewed)
    _, renewed = deliver(state_out, slot[0], x0, summed[:SEQ])
    out_1 = put(state_out, slot[0], renewed)
    _, renewed = deliver(out_1, slot[1], y1, summed[SEQ : 2 * SEQ])
    out_1 = put(out_1, slot[1], renewed)
    _, renewed = deliver(out_1, slot[2], y2, summed[2 * SEQ :])
    new_out = jnp.where(first, new_out_first, put(out_1, slot[2], renewed))

    copies_new = jnp.stack([new_in, new_out])[None]
    return (copies_new, grad[None, :, :1024], grad[None, :, 1024:])


def solution(mesh):
    shape = dict(mesh.shape)
    grid = Mesh(
        mesh.devices.reshape(shape["section"], 4, shape["dp"] // 4, shape["tensor"]),
        ("section", "y", "x", "tensor"),
    )
    dp = ("y", "x")
    return jax.shard_map(
        on_device,
        mesh=grid,
        in_specs=(
            P("section", None, dp, None, "tensor"),
            P("section", dp, None, "tensor"),
            P(None, dp, None, "tensor"),
            P(None, dp),
            P(None, "tensor"),
            P("section", None),
            P("section", dp, "tensor"),
            P("section", dp, "tensor"),
            P("section", dp, "tensor"),
            P("section", "tensor", dp),
            P("section", None, dp, None, None),
        ),
        out_specs=(
            P("section", None, dp, None, "tensor"),
            P("section", dp, "tensor"),
            P("section", dp, "tensor"),
        ),
        check_vma=False,
    )
```

```python
import functools

import jax
import jax.numpy as jnp
from jax import lax
from jax.experimental import pallas as pl
from jax.experimental.pallas import tpu as pltpu
from jax.sharding import Mesh, PartitionSpec as P

HQ = 32
HK = 4
HD = 128
QB = 128
SEQ = 128

eps_norm = 1e-05
qmax = 7.0
f32 = jnp.float32
bf16 = jnp.bfloat16


GROUP = HQ // HK
NT = (((1,), (1,)), ((), ()))
TN = (((0,), (0,)), ((), ()))


def stacked(rows):
    return jnp.concatenate([rows[:, h * HD : (h + 1) * HD] for h in range(GROUP)], axis=0)


def side_by_side(rows):
    return jnp.concatenate([rows[h * SEQ : (h + 1) * SEQ] for h in range(GROUP)], axis=1)


def probs_of(query, key_in):
    scores = lax.dot_general(query, key_in, NT, preferred_element_type=f32) * HD ** (-0.5)
    at = lax.broadcasted_iota(jnp.int32, scores.shape, 0) % SEQ
    key_at = lax.broadcasted_iota(jnp.int32, scores.shape, 1)
    scores = jnp.where(at >= key_at, scores, -1e30)
    weight = jnp.exp(scores - jnp.max(scores, axis=-1, keepdims=True))
    return weight / jnp.sum(weight, axis=-1, keepdims=True)


def attend_unit(qkv):
    wide = GROUP * HD
    probs = probs_of(stacked(qkv[:, :wide]), qkv[:, wide : wide + HD])
    mixed = jnp.dot(probs.astype(bf16), qkv[:, wide + HD :], preferred_element_type=f32)
    return side_by_side(mixed.astype(bf16))


def attend_back_kernel(qkv_ref, d_mixed_ref, out_ref):
    wide = GROUP * HD
    key_in = qkv_ref[:, wide : wide + HD]
    probs = probs_of(stacked(qkv_ref[:, :wide]), key_in)
    d_rows = stacked(d_mixed_ref[...])
    d_probs = lax.dot_general(d_rows, qkv_ref[:, wide + HD :], NT, preferred_element_type=f32)
    d_scores = (
        probs * (d_probs - jnp.sum(d_probs * probs, axis=-1, keepdims=True)) * HD ** (-0.5)
    )
    d_query = jnp.dot(d_scores.astype(bf16), key_in, preferred_element_type=f32).astype(bf16)
    d_value = lax.dot_general(probs.astype(bf16), d_rows, TN, preferred_element_type=f32)
    out_ref[:, :wide] = side_by_side(d_query)
    out_ref[:, wide:] = d_value.astype(bf16)


def attend_back(qkv, d_mixed):
    rows = qkv.shape[0]
    return pl.pallas_call(
        attend_back_kernel,
        grid=(rows // SEQ,),
        in_specs=[
            pl.BlockSpec((SEQ, (GROUP + 2) * HD), lambda u: (u, 0)),
            pl.BlockSpec((SEQ, GROUP * HD), lambda u: (u, 0)),
        ],
        out_specs=pl.BlockSpec((SEQ, (GROUP + 1) * HD), lambda u: (u, 0)),
        out_shape=jax.ShapeDtypeStruct((rows, (GROUP + 1) * HD), bf16),
        compiler_params=pltpu.CompilerParams(vmem_limit_bytes=32 * 1024 * 1024),
        cost_estimate=pl.CostEstimate(
            flops=rows * SEQ * GROUP * HD * 8,
            bytes_accessed=rows * 3456 * 2,
            transcendentals=rows * SEQ * GROUP,
        ),
        name="attend_back",
    )(qkv, d_mixed)


ROWS = 16
ORDER = (0, 3, 1, 2)


def known_a(flags, known_ref, x_ref):
    from_0 = (flags[0] == 1) | (flags[1] == 0)

    def step(i, carry):
        at = pl.multiple_of(i * ROWS, ROWS)
        for j in range(4):
            one = known_ref[j, pl.ds(at, ROWS), :]
            two = known_ref[j, pl.ds(at + SEQ, ROWS), :]
            columns = slice(j * 1024, (j + 1) * 1024)
            x_ref[pl.ds(at, ROWS), columns] = jnp.where(from_0, one, two)
            x_ref[pl.ds(at + SEQ, ROWS), columns] = two
        return carry

    lax.fori_loop(0, SEQ // ROWS, step, 0)


def known_b(flags, known_ref, got_refs, x_ref):
    first = flags[0] == 1
    slot_1, slot_2 = flags[2], flags[3]

    def step(i, carry):
        at = pl.multiple_of(i * ROWS, ROWS)
        for by in range(4):
            j = lax.rem(flags[6] + 4 - by, 4)
            one = known_ref[j, pl.ds(at, ROWS), :].astype(f32)
            two = known_ref[j, pl.ds(at + SEQ, ROWS), :].astype(f32)
            third = known_ref[j, pl.ds(at + 2 * SEQ, ROWS), :]
            step_1 = got_refs[by][pl.ds(at, ROWS), :].astype(f32)
            step_2 = got_refs[by][pl.ds(at + SEQ, ROWS), :].astype(f32)
            x_1 = (jnp.where(slot_1 == 0, one, two) + step_1).astype(bf16)
            old = jnp.where(
                slot_1 == slot_2, x_1.astype(f32), jnp.where(slot_2 == 0, one, two)
            )
            columns = pl.ds(pl.multiple_of(j * 1024, 1024), 1024)
            x_ref[pl.ds(at, ROWS), columns] = jnp.where(first, third, x_1)
            x_ref[pl.ds(at + SEQ, ROWS), columns] = (old + step_2).astype(bf16)
        return carry

    lax.fori_loop(0, SEQ // ROWS, step, 0)


def normalize(gain_ref, x_ref):
    def step(i, carry):
        rows = pl.ds(pl.multiple_of(i * ROWS, ROWS), ROWS)
        values = x_ref[rows, :].astype(f32)
        square = jnp.mean(values * values, axis=-1, keepdims=True)
        x_ref[rows, :] = (values * lax.rsqrt(square + eps_norm) * gain_ref[...]).astype(bf16)
        return carry

    lax.fori_loop(0, 2 * SEQ // ROWS, step, 0)


def prepare_kernel(flags, gain_ref, known_ref, normed_ref):
    known_a(flags, known_ref, normed_ref)
    normalize(gain_ref, normed_ref)


VMEM = pl.BlockSpec(memory_space=pltpu.VMEM)
SMEM = pl.BlockSpec(memory_space=pltpu.SMEM)
ANY = pl.BlockSpec(memory_space=pl.ANY)
GRANT = pltpu.CompilerParams(vmem_limit_bytes=60 * 1024 * 1024)


def prepare(flags, gain, known):
    return pl.pallas_call(
        prepare_kernel,
        in_specs=[SMEM, VMEM, VMEM],
        out_specs=VMEM,
        out_shape=jax.ShapeDtypeStruct((2 * SEQ, 4096), bf16),
        compiler_params=pltpu.CompilerParams(vmem_limit_bytes=32 * 1024 * 1024),
        cost_estimate=pl.CostEstimate(flops=2**23, bytes_accessed=5 * 2**20, transcendentals=0),
        name="prepare",
    )(flags, gain, known)


def project_kernel(flags, pieces, normed_ref, qkv_ref, mixed_ref, held, held_kv, sems, begin):
    full_ref, pieces = pieces[0], pieces[1:]
    copies = []
    for at in range(5):
        target = held.at[at] if at < 3 else held.at[3, pl.ds(2 * (at - 3), 2)]
        copies.append(pltpu.make_async_copy(pieces[at], target, sems.at[at]))
    copies.append(pltpu.make_async_copy(full_ref.at[:, pl.ds(1024, 256)], held_kv, sems.at[5]))
    for copy in copies:
        copy.start()
    begin()
    total = None
    for at in range(4):
        lhs = []
        for block in range(4):
            second, inner = ORDER[at], ORDER[block]
            dy = jnp.where(flags[0] == 1, second, inner)
            dx = jnp.where(flags[0] == 1, inner, second)
            row = lax.rem(flags[5] + dy, 4) * 4 + lax.rem(flags[4] + dx, 4)
            lhs.append(normed_ref[:, pl.ds(pl.multiple_of(row * 256, 256), 256)])
        copies[at].wait()
        if at == 3:
            copies[4].wait()
        part = jnp.dot(
            jnp.concatenate(lhs, axis=1), held[at].reshape(1024, 1024), preferred_element_type=f32
        )
        total = part if total is None else total + part
    qkv_ref[:, :1024] = total.astype(bf16)
    copies[5].wait()
    qkv_ref[:, 1024:] = jnp.dot(
        normed_ref[...], held_kv[...], preferred_element_type=f32
    ).astype(bf16)
    for unit in range(2):
        rows = slice(unit * SEQ, (unit + 1) * SEQ)
        mixed_ref[rows, :] = attend_unit(qkv_ref[rows, :])


def project_a_kernel(flags, normed_ref, *refs):
    pieces, (qkv_ref, mixed_ref, held, held_kv, sems) = refs[:6], refs[6:]
    project_kernel(flags, pieces, normed_ref, qkv_ref, mixed_ref, held, held_kv, sems, lambda: None)


def project_b_kernel(flags, gain_ref, known_ref, *refs):
    got_refs, pieces = refs[:4], refs[4:10]
    normed_ref, qkv_ref, mixed_ref, held, held_kv, sems = refs[10:]

    def begin():
        known_b(flags, known_ref, got_refs, normed_ref)
        normalize(gain_ref, normed_ref)

    project_kernel(flags, pieces, normed_ref, qkv_ref, mixed_ref, held, held_kv, sems, begin)


def project_call(kernel, name, operands, pieces, with_normed):
    rows = 2 * SEQ
    shapes = [
        jax.ShapeDtypeStruct((rows, 4096), bf16),
        jax.ShapeDtypeStruct((rows, (GROUP + 2) * HD), bf16),
        jax.ShapeDtypeStruct((rows, GROUP * HD), bf16),
    ][0 if with_normed else 1 :]
    return pl.pallas_call(
        kernel,
        in_specs=[SMEM] + [VMEM] * (len(operands) - 1) + [ANY] * 6,
        out_specs=[VMEM] * len(shapes),
        out_shape=shapes,
        scratch_shapes=[
            pltpu.VMEM((4, 4, 256, 1024), bf16),
            pltpu.VMEM((4096, 256), bf16),
            pltpu.SemaphoreType.DMA((6,)),
        ],
        compiler_params=GRANT,
        cost_estimate=pl.CostEstimate(
            flops=2 * rows * 4096 * 1280, bytes_accessed=18 * 2**20, transcendentals=rows * 1024
        ),
        name=name,
    )(*operands, *pieces)


def spread_kernel(flags, mixed_ref, full_ref, *refs):
    outs, (held, sems) = refs[:4], refs[4:]
    copies = []
    for i, by in enumerate((2, 1, 3, 0)):
        row = pl.multiple_of(lax.rem(flags[6] + by, 4) * 1024, 1024)
        copies.append(
            pltpu.make_async_copy(full_ref.at[pl.ds(row, 1024), pl.ds(0, 1024)], held.at[i], sems.at[i])
        )
        copies[-1].start()
    for i in range(4):
        copies[i].wait()
        outs[i][...] = lax.dot_general(
            mixed_ref[...], held[i], NT, preferred_element_type=f32
        ).astype(bf16)


def spread(flags, mixed, full):
    rows = mixed.shape[0]
    return pl.pallas_call(
        spread_kernel,
        in_specs=[SMEM, VMEM, ANY],
        out_specs=[VMEM] * 4,
        out_shape=[jax.ShapeDtypeStruct((rows, 1024), bf16)] * 4,
        scratch_shapes=[pltpu.VMEM((4, 1024, 1024), bf16), pltpu.SemaphoreType.DMA((4,))],
        compiler_params=GRANT,
        cost_estimate=pl.CostEstimate(
            flops=2 * rows * 4096 * 1024, bytes_accessed=12 * 2**20, transcendentals=0
        ),
        name="spread",
    )(flags, mixed, full)


WIDE = (GROUP + 1) * HD


def three(flags, a_ref, b_ref, columns):
    middle = jnp.where(flags[0] == 1, a_ref[SEQ:, columns], b_ref[SEQ:, columns])
    return jnp.concatenate([a_ref[:SEQ, columns], middle, b_ref[:SEQ, columns]], axis=0)


PLACES = (((2, 0), (1, 1)), ((2, 1), (3, 0)), ((1, 0),), ((3, 1),), ((0, 0), (0, 1)))


def terms_kernel(flags, normed_a, normed_b, d_a, d_b, *refs):
    outs, (held, sems) = refs[:5], refs[5:]
    d_rows = three(flags, d_a, d_b, slice(None)).T
    copies = []
    places = [(out, k, place) for out, parts in zip(outs, PLACES) for k, place in enumerate(parts)]
    for i, (out, k, (outer, pair)) in enumerate(places):
        features = []
        for inner in (2 * pair, 2 * pair + 1):
            dy = jnp.where(flags[0] == 1, outer, inner)
            dx = jnp.where(flags[0] == 1, inner, outer)
            row = lax.rem(flags[5] + dy, 4) * 4 + lax.rem(flags[4] + dx, 4)
            columns = pl.ds(pl.multiple_of(row * 256, 256), 256)
            features.append(three(flags, normed_a, normed_b, columns))
        held[i] = jnp.dot(
            d_rows, jnp.concatenate(features, axis=1), preferred_element_type=f32
        ).astype(bf16)
        target = out.at[:, pl.ds(512 * k, 512)]
        copies.append(pltpu.make_async_copy(held.at[i], target, sems.at[i]))
        copies[-1].start()
    for copy in copies:
        copy.wait()


def terms(operands):
    return pl.pallas_call(
        terms_kernel,
        in_specs=[SMEM] + [VMEM] * 4,
        out_specs=[ANY] * 5,
        out_shape=[jax.ShapeDtypeStruct((WIDE, 512 * len(parts)), bf16) for parts in PLACES],
        scratch_shapes=[pltpu.VMEM((8, WIDE, 512), bf16), pltpu.SemaphoreType.DMA((8,))],
        compiler_params=pltpu.CompilerParams(vmem_limit_bytes=32 * 1024 * 1024),
        cost_estimate=pl.CostEstimate(
            flops=2 * 3 * SEQ * 4096 * WIDE, bytes_accessed=14 * 2**20, transcendentals=0
        ),
        name="terms",
    )(*operands)


def along(shard, second, by):
    pairs = []
    for y in range(4):
        for x in range(4):
            by_x, by_y = y * 4 + (x + by) % 4, (y + by) % 4 * 4 + x
            pairs.append((y * 4 + x, by_y if second else by_x))
            pairs.append((16 + y * 4 + x, 16 + (by_x if second else by_y)))
    return lax.ppermute(shard, ("section", "y", "x"), pairs)


def from_first(shard, by, to_section):
    return lax.ppermute(
        shard, ("section", "tensor"), [(i, 4 * to_section + (i + by) % 4) for i in range(4)]
    )


def gathered(shard):
    before, after, far = along(shard, False, 1), along(shard, False, -1), along(shard, False, 2)
    own = jnp.stack([shard, before, after, far])
    before, after = along(own, True, 1), along(own, True, -1)
    return [own, before, after, along(before[:2], True, 1), along(after[2:], True, -1)]


def plus(*shards):
    return sum(shard.astype(f32) for shard in shards).astype(bf16)


def summed_over_plane(operands):
    ahead, back, next_low, last_high, own = terms(operands)
    from_before, from_after = lax.optimization_barrier(
        (along(ahead, True, 1), along(back, True, -1))
    )
    sum_before, sum_after = lax.optimization_barrier(
        (
            along(plus(next_low, from_before[:, :512]), True, 1),
            along(plus(last_high, from_after[:, :512]), True, -1),
        )
    )
    low = (own[:, :512], sum_before, from_after[:, 512:])
    high = (own[:, 512:], from_before[:, 512:], sum_after)
    blocks = []
    for parts in (low, high):
        for columns in (slice(0, 256), slice(256, 512)):
            blocks.append(plus(*(part[:, columns] for part in parts)))
    got = [
        along(blocks[2], False, 2),
        along(blocks[1], False, 1),
        along(blocks[3], False, -1),
    ]
    return plus(blocks[0], *got), own


def pick(state, slot):
    return jnp.where(slot == 0, state[0], state[1])


def put(state, slot, new, active=True):
    mask = (jnp.arange(2) == slot) & active
    return jnp.where(mask[:, None, None], new[None], state)


def on_device(
    boundary_copies,
    arriving,
    first_delta,
    sample_index,
    exponents,
    norm_gain,
    w_query,
    w_key,
    w_value,
    w_out,
    out_grad,
):
    first = lax.axis_index("section") == 0
    z = lax.axis_index("tensor")

    packed = jnp.concatenate([w_out[0].T, w_key[0], w_value[0]], axis=1)
    arriving, first_delta, packed = lax.optimization_barrier((arriving, first_delta, packed))
    full = lax.all_gather(packed, ("y", "x"), axis=0, tiled=True)
    full_o = full[:, :1024]
    pieces = [full] + gathered(w_query[0])

    power = exponents.astype(f32)
    scale_full = jnp.repeat(jnp.exp2(power), QB, axis=1)
    inverse_full = jnp.repeat(jnp.exp2(-power), QB, axis=1)
    scale_in = jnp.where(first, scale_full[0], scale_full[1])
    scale_next = jnp.where(first, scale_full[1], scale_full[2])
    inverse_next = jnp.where(first, inverse_full[1], inverse_full[2])
    slots = sample_index[:, 0]
    slot = [jnp.where(first, slots[k + 1], slots[k]) for k in range(3)]

    def receive(state, at, delta):
        return (pick(state, at).astype(f32) + scale_in * delta.astype(f32)).astype(bf16)

    def deliver(state, at, inputs, summed):
        output = (inputs.astype(f32) + summed).astype(bf16)
        old = pick(state, at)
        sent = jnp.clip(
            (output.astype(f32) - old.astype(f32)) * inverse_next, -qmax, qmax
        ).astype(bf16)
        step = scale_next * sent.astype(f32)
        return step.astype(bf16), (old.astype(f32) + step).astype(bf16)

    state_in, state_out = boundary_copies[0, 0], boundary_copies[0, 1]
    x0 = receive(state_in, slot[0], arriving[0, 0])
    state_in = put(state_in, slot[0], x0)
    x1 = receive(state_in, slot[1], first_delta[0, 0])
    state_1 = put(state_in, slot[1], x1)
    x2 = receive(state_1, slot[2], first_delta[1, 0])
    state_2 = put(state_1, slot[2], x2)
    known = jnp.concatenate(
        [jnp.where(first, x0, state_in[0]), jnp.where(first, x1, state_in[1]), x2], 0
    )
    known = lax.all_to_all(
        jnp.broadcast_to(known[None], (4,) + known.shape),
        "tensor",
        split_axis=0,
        concat_axis=0,
        tiled=True,
    )

    flags = jnp.stack(
        [first.astype(jnp.int32), *slot, lax.axis_index("x"), lax.axis_index("y"), z]
    ).astype(jnp.int32)
    normed_a = prepare(flags, norm_gain, known)
    qkv_a, mixed_a = project_call(project_a_kernel, "project_a", [flags, normed_a], pieces, False)
    far, near_1, near_3, own = spread(flags, mixed_a, full)
    parts = [own] + [
        from_first(piece, by, 0) for piece, by in ((far, 2), (near_1, 1), (near_3, 3))
    ]
    summed = sum(part.astype(f32) for part in parts)
    step_0, renewed = deliver(state_out, slot[0], x0, summed[:SEQ])
    out_1 = put(state_out, slot[0], renewed)
    step_1, renewed = deliver(out_1, slot[1], x1, summed[SEQ:])
    out_2 = put(out_1, slot[1], renewed)
    steps = jnp.concatenate([step_0, step_1], 0)
    got = [from_first(steps, by, 1) for by in range(4)]

    def added(state, at, step):
        return (pick(state, at).astype(f32) + step.astype(f32)).astype(bf16)

    normed_b, qkv_b, mixed_b = project_call(
        project_b_kernel, "project_b", [flags, norm_gain, known, *got], pieces, True
    )
    y1 = added(state_in, slot[1], got[0][:SEQ])
    after_1 = put(state_in, slot[1], y1)
    y2 = added(after_1, slot[2], got[0][SEQ:])
    new_in = jnp.where(first, state_2, put(after_1, slot[2], y2))

    up = out_grad[0, :, 0].reshape(3 * SEQ, -1)
    d_mixed = jnp.dot(up, full_o, preferred_element_type=f32).astype(bf16)
    d_a = attend_back(qkv_a, d_mixed[: 2 * SEQ])
    d_mixed_b = jnp.concatenate(
        [jnp.where(first, d_mixed[2 * SEQ :], d_mixed[SEQ : 2 * SEQ]), d_mixed[2 * SEQ :]], 0
    )
    d_b = attend_back(qkv_b, d_mixed_b)

    grad, own_terms = summed_over_plane([flags, normed_a, normed_b, d_a, d_b])
    grad = grad.T

    mixed_f = jnp.concatenate([jnp.where(first, mixed_b[:SEQ], mixed_a[:SEQ]), mixed_b], 0)
    mixed_f, _ = lax.optimization_barrier((mixed_f, own_terms))
    partial = lax.dot_general(mixed_f, full_o, NT, preferred_element_type=f32).astype(bf16)
    summed = lax.psum_scatter(partial, "tensor", scatter_dimension=1, tiled=True).astype(f32)
    _, renewed = deliver(out_2, slot[2], x2, summed[:SEQ])
    new_out_first = put(out_2, slot[2], renewed)
    _, renewed = deliver(state_out, slot[0], x0, summed[:SEQ])
    out_1 = put(state_out, slot[0], renewed)
    _, renewed = deliver(out_1, slot[1], y1, summed[SEQ : 2 * SEQ])
    out_1 = put(out_1, slot[1], renewed)
    _, renewed = deliver(out_1, slot[2], y2, summed[2 * SEQ :])
    new_out = jnp.where(first, new_out_first, put(out_1, slot[2], renewed))

    copies_new = jnp.stack([new_in, new_out])[None]
    return (copies_new, grad[None, :, :1024], grad[None, :, 1024:])


def solution(mesh):
    shape = dict(mesh.shape)
    grid = Mesh(
        mesh.devices.reshape(shape["section"], 4, shape["dp"] // 4, shape["tensor"]),
        ("section", "y", "x", "tensor"),
    )
    dp = ("y", "x")
    return jax.shard_map(
        on_device,
        mesh=grid,
        in_specs=(
            P("section", None, dp, None, "tensor"),
            P("section", dp, None, "tensor"),
            P(None, dp, None, "tensor"),
            P(None, dp),
            P(None, "tensor"),
            P("section", None),
            P("section", dp, "tensor"),
            P("section", dp, "tensor"),
            P("section", dp, "tensor"),
            P("section", "tensor", dp),
            P("section", None, dp, None, None),
        ),
        out_specs=(
            P("section", None, dp, None, "tensor"),
            P("section", dp, "tensor"),
            P("section", dp, "tensor"),
        ),
        check_vma=False,
    )
```

```python
import functools

import jax
import jax.numpy as jnp
from jax import lax
from jax.experimental import pallas as pl
from jax.experimental.pallas import tpu as pltpu
from jax.sharding import Mesh, PartitionSpec as P

HQ = 32
HK = 4
HD = 128
QB = 128
SEQ = 128

eps_norm = 1e-05
qmax = 7.0
f32 = jnp.float32
bf16 = jnp.bfloat16


GROUP = HQ // HK
UNITS = 3
NT = (((1,), (1,)), ((), ()))
TN = (((0,), (0,)), ((), ()))


def stacked(rows):
    return jnp.concatenate([rows[:, h * HD : (h + 1) * HD] for h in range(GROUP)], axis=0)


def side_by_side(rows):
    return jnp.concatenate([rows[h * SEQ : (h + 1) * SEQ] for h in range(GROUP)], axis=1)


def probs_of(query, key_in):
    scores = lax.dot_general(query, key_in, NT, preferred_element_type=f32) * HD ** (-0.5)
    at = lax.broadcasted_iota(jnp.int32, scores.shape, 0) % SEQ
    key_at = lax.broadcasted_iota(jnp.int32, scores.shape, 1)
    scores = jnp.where(at >= key_at, scores, -1e30)
    weight = jnp.exp(scores - jnp.max(scores, axis=-1, keepdims=True))
    return weight / jnp.sum(weight, axis=-1, keepdims=True)


def attend_unit(qkv):
    wide = GROUP * HD
    probs = probs_of(stacked(qkv[:, :wide]), qkv[:, wide : wide + HD])
    mixed = jnp.dot(probs.astype(bf16), qkv[:, wide + HD :], preferred_element_type=f32)
    return side_by_side(mixed.astype(bf16))


def attend_back_kernel(qkv_ref, d_mixed_ref, out_ref):
    wide = GROUP * HD
    key_in = qkv_ref[:, wide : wide + HD]
    probs = probs_of(stacked(qkv_ref[:, :wide]), key_in)
    d_rows = stacked(d_mixed_ref[...])
    d_probs = lax.dot_general(d_rows, qkv_ref[:, wide + HD :], NT, preferred_element_type=f32)
    d_scores = (
        probs * (d_probs - jnp.sum(d_probs * probs, axis=-1, keepdims=True)) * HD ** (-0.5)
    )
    d_query = jnp.dot(d_scores.astype(bf16), key_in, preferred_element_type=f32).astype(bf16)
    d_value = lax.dot_general(probs.astype(bf16), d_rows, TN, preferred_element_type=f32)
    out_ref[:, :wide] = side_by_side(d_query)
    out_ref[:, wide:] = d_value.astype(bf16)


def attend_back(qkv, d_mixed):
    rows = qkv.shape[0]
    return pl.pallas_call(
        attend_back_kernel,
        grid=(rows // SEQ,),
        in_specs=[
            pl.BlockSpec((SEQ, (GROUP + 2) * HD), lambda u: (u, 0)),
            pl.BlockSpec((SEQ, GROUP * HD), lambda u: (u, 0)),
        ],
        out_specs=pl.BlockSpec((SEQ, (GROUP + 1) * HD), lambda u: (u, 0)),
        out_shape=jax.ShapeDtypeStruct((rows, (GROUP + 1) * HD), bf16),
        compiler_params=pltpu.CompilerParams(vmem_limit_bytes=32 * 1024 * 1024),
        cost_estimate=pl.CostEstimate(
            flops=rows * SEQ * GROUP * HD * 8,
            bytes_accessed=rows * 3456 * 2,
            transcendentals=rows * SEQ * GROUP,
        ),
        name="attend_back",
    )(qkv, d_mixed)


ROWS = 16
ORDER = (0, 3, 1, 2)


def known_a(flags, known_ref, x_ref):
    from_0 = (flags[0] == 1) | (flags[1] == 0)

    def step(i, carry):
        at = pl.multiple_of(i * ROWS, ROWS)
        for j in range(4):
            one = known_ref[j, pl.ds(at, ROWS), :]
            two = known_ref[j, pl.ds(at + SEQ, ROWS), :]
            columns = slice(j * 1024, (j + 1) * 1024)
            x_ref[pl.ds(at, ROWS), columns] = jnp.where(from_0, one, two)
            x_ref[pl.ds(at + SEQ, ROWS), columns] = two
        return carry

    lax.fori_loop(0, SEQ // ROWS, step, 0)


def known_b(flags, known_ref, got_refs, x_ref):
    first = flags[0] == 1
    slot_1, slot_2 = flags[2], flags[3]

    def step(i, carry):
        at = pl.multiple_of(i * ROWS, ROWS)
        for by in range(4):
            j = lax.rem(flags[6] + 4 - by, 4)
            one = known_ref[j, pl.ds(at, ROWS), :].astype(f32)
            two = known_ref[j, pl.ds(at + SEQ, ROWS), :].astype(f32)
            third = known_ref[j, pl.ds(at + 2 * SEQ, ROWS), :]
            step_1 = got_refs[by][pl.ds(at, ROWS), :].astype(f32)
            step_2 = got_refs[by][pl.ds(at + SEQ, ROWS), :].astype(f32)
            x_1 = (jnp.where(slot_1 == 0, one, two) + step_1).astype(bf16)
            old = jnp.where(
                slot_1 == slot_2, x_1.astype(f32), jnp.where(slot_2 == 0, one, two)
            )
            columns = pl.ds(pl.multiple_of(j * 1024, 1024), 1024)
            x_ref[pl.ds(at, ROWS), columns] = jnp.where(first, third, x_1)
            x_ref[pl.ds(at + SEQ, ROWS), columns] = (old + step_2).astype(bf16)
        return carry

    lax.fori_loop(0, SEQ // ROWS, step, 0)


def normalize(gain_ref, x_ref):
    def step(i, carry):
        rows = pl.ds(pl.multiple_of(i * ROWS, ROWS), ROWS)
        values = x_ref[rows, :].astype(f32)
        square = jnp.mean(values * values, axis=-1, keepdims=True)
        x_ref[rows, :] = (values * lax.rsqrt(square + eps_norm) * gain_ref[...]).astype(bf16)
        return carry

    lax.fori_loop(0, 2 * SEQ // ROWS, step, 0)


def prepare_kernel(flags, gain_ref, known_ref, normed_ref):
    known_a(flags, known_ref, normed_ref)
    normalize(gain_ref, normed_ref)


VMEM = pl.BlockSpec(memory_space=pltpu.VMEM)
SMEM = pl.BlockSpec(memory_space=pltpu.SMEM)
ANY = pl.BlockSpec(memory_space=pl.ANY)
GRANT = pltpu.CompilerParams(vmem_limit_bytes=60 * 1024 * 1024)


def prepare(flags, gain, known):
    return pl.pallas_call(
        prepare_kernel,
        in_specs=[SMEM, VMEM, VMEM],
        out_specs=VMEM,
        out_shape=jax.ShapeDtypeStruct((2 * SEQ, 4096), bf16),
        compiler_params=pltpu.CompilerParams(vmem_limit_bytes=32 * 1024 * 1024),
        cost_estimate=pl.CostEstimate(flops=2**23, bytes_accessed=5 * 2**20, transcendentals=0),
        name="prepare",
    )(flags, gain, known)


def project_kernel(flags, pieces, normed_ref, qkv_ref, mixed_ref, held, held_kv, sems, begin):
    full_ref, pieces = pieces[0], pieces[1:]
    copies = []
    for at in range(5):
        target = held.at[at] if at < 3 else held.at[3, pl.ds(2 * (at - 3), 2)]
        copies.append(pltpu.make_async_copy(pieces[at], target, sems.at[at]))
    copies.append(pltpu.make_async_copy(full_ref.at[:, pl.ds(1024, 256)], held_kv, sems.at[5]))
    for copy in copies:
        copy.start()
    begin()
    total = None
    for at in range(4):
        lhs = []
        for block in range(4):
            second, inner = ORDER[at], ORDER[block]
            dy = jnp.where(flags[0] == 1, second, inner)
            dx = jnp.where(flags[0] == 1, inner, second)
            row = lax.rem(flags[5] + dy, 4) * 4 + lax.rem(flags[4] + dx, 4)
            lhs.append(normed_ref[:, pl.ds(pl.multiple_of(row * 256, 256), 256)])
        copies[at].wait()
        if at == 3:
            copies[4].wait()
        part = jnp.dot(
            jnp.concatenate(lhs, axis=1), held[at].reshape(1024, 1024), preferred_element_type=f32
        )
        total = part if total is None else total + part
    qkv_ref[:, :1024] = total.astype(bf16)
    copies[5].wait()
    qkv_ref[:, 1024:] = jnp.dot(
        normed_ref[...], held_kv[...], preferred_element_type=f32
    ).astype(bf16)
    for unit in range(2):
        rows = slice(unit * SEQ, (unit + 1) * SEQ)
        mixed_ref[rows, :] = attend_unit(qkv_ref[rows, :])


def project_a_kernel(flags, normed_ref, *refs):
    pieces, (qkv_ref, mixed_ref, held, held_kv, sems) = refs[:6], refs[6:]
    project_kernel(flags, pieces, normed_ref, qkv_ref, mixed_ref, held, held_kv, sems, lambda: None)


def project_b_kernel(flags, gain_ref, known_ref, *refs):
    got_refs, pieces = refs[:4], refs[4:10]
    normed_ref, qkv_ref, mixed_ref, held, held_kv, sems = refs[10:]

    def begin():
        known_b(flags, known_ref, got_refs, normed_ref)
        normalize(gain_ref, normed_ref)

    project_kernel(flags, pieces, normed_ref, qkv_ref, mixed_ref, held, held_kv, sems, begin)


def project_call(kernel, name, operands, pieces, with_normed):
    rows = 2 * SEQ
    shapes = [
        jax.ShapeDtypeStruct((rows, 4096), bf16),
        jax.ShapeDtypeStruct((rows, (GROUP + 2) * HD), bf16),
        jax.ShapeDtypeStruct((rows, GROUP * HD), bf16),
    ][0 if with_normed else 1 :]
    return pl.pallas_call(
        kernel,
        in_specs=[SMEM] + [VMEM] * (len(operands) - 1) + [ANY] * 6,
        out_specs=[VMEM] * len(shapes),
        out_shape=shapes,
        scratch_shapes=[
            pltpu.VMEM((4, 4, 256, 1024), bf16),
            pltpu.VMEM((4096, 256), bf16),
            pltpu.SemaphoreType.DMA((6,)),
        ],
        compiler_params=GRANT,
        cost_estimate=pl.CostEstimate(
            flops=2 * rows * 4096 * 1280, bytes_accessed=18 * 2**20, transcendentals=rows * 1024
        ),
        name=name,
    )(*operands, *pieces)


def spread_kernel(flags, mixed_ref, full_ref, *refs):
    outs, (held, sems) = refs[:4], refs[4:]
    copies = []
    for i, by in enumerate((2, 1, 3, 0)):
        row = pl.multiple_of(lax.rem(flags[6] + by, 4) * 1024, 1024)
        copies.append(
            pltpu.make_async_copy(full_ref.at[pl.ds(row, 1024), pl.ds(0, 1024)], held.at[i], sems.at[i])
        )
        copies[-1].start()
    for i in range(4):
        copies[i].wait()
        outs[i][...] = lax.dot_general(
            mixed_ref[...], held[i], NT, preferred_element_type=f32
        ).astype(bf16)


def spread(flags, mixed, full):
    rows = mixed.shape[0]
    return pl.pallas_call(
        spread_kernel,
        in_specs=[SMEM, VMEM, ANY],
        out_specs=[VMEM] * 4,
        out_shape=[jax.ShapeDtypeStruct((rows, 1024), bf16)] * 4,
        scratch_shapes=[pltpu.VMEM((4, 1024, 1024), bf16), pltpu.SemaphoreType.DMA((4,))],
        compiler_params=GRANT,
        cost_estimate=pl.CostEstimate(
            flops=2 * rows * 4096 * 1024, bytes_accessed=12 * 2**20, transcendentals=0
        ),
        name="spread",
    )(flags, mixed, full)


WIDE = (GROUP + 1) * HD


def three(flags, a_ref, b_ref, columns):
    middle = jnp.where(flags[0] == 1, a_ref[SEQ:, columns], b_ref[SEQ:, columns])
    return jnp.concatenate([a_ref[:SEQ, columns], middle, b_ref[:SEQ, columns]], axis=0)


PLACES = (((2, 0), (1, 1)), ((2, 1), (3, 0)), ((1, 0),), ((3, 1),), ((0, 0), (0, 1)))


def terms_kernel(flags, normed_a, normed_b, d_a, d_b, *refs):
    outs, (held, sems) = refs[:5], refs[5:]
    d_rows = three(flags, d_a, d_b, slice(None)).T
    copies = []
    places = [(out, k, place) for out, parts in zip(outs, PLACES) for k, place in enumerate(parts)]
    for i, (out, k, (outer, pair)) in enumerate(places):
        features = []
        for inner in (2 * pair, 2 * pair + 1):
            dy = jnp.where(flags[0] == 1, outer, inner)
            dx = jnp.where(flags[0] == 1, inner, outer)
            row = lax.rem(flags[5] + dy, 4) * 4 + lax.rem(flags[4] + dx, 4)
            columns = pl.ds(pl.multiple_of(row * 256, 256), 256)
            features.append(three(flags, normed_a, normed_b, columns))
        held[i] = jnp.dot(
            d_rows, jnp.concatenate(features, axis=1), preferred_element_type=f32
        ).astype(bf16)
        target = out.at[:, pl.ds(512 * k, 512)]
        copies.append(pltpu.make_async_copy(held.at[i], target, sems.at[i]))
        copies[-1].start()
    for copy in copies:
        copy.wait()


def terms(operands):
    return pl.pallas_call(
        terms_kernel,
        in_specs=[SMEM] + [VMEM] * 4,
        out_specs=[ANY] * 5,
        out_shape=[jax.ShapeDtypeStruct((WIDE, 512 * len(parts)), bf16) for parts in PLACES],
        scratch_shapes=[pltpu.VMEM((8, WIDE, 512), bf16), pltpu.SemaphoreType.DMA((8,))],
        compiler_params=pltpu.CompilerParams(vmem_limit_bytes=32 * 1024 * 1024),
        cost_estimate=pl.CostEstimate(
            flops=2 * 3 * SEQ * 4096 * WIDE, bytes_accessed=14 * 2**20, transcendentals=0
        ),
        name="terms",
    )(*operands)


def finish_kernel(flags, new_in, state_out, summed, x_0, x_1, x_2, scale, inverse, copies_ref):
    first = flags[0] == 1
    units = (
        (x_0, jnp.where(first, flags[3], flags[1]), first | True),
        (x_1, flags[2], jnp.logical_not(first)),
        (x_2, flags[3], jnp.logical_not(first)),
    )

    def step(i, carry):
        at = pl.multiple_of(i * ROWS, ROWS)
        rows = pl.ds(at, ROWS)
        states = [state_out[0, rows, :], state_out[1, rows, :]]
        for unit, (inputs, slot, active) in enumerate(units):
            total = summed[pl.ds(at + unit * SEQ, ROWS), :].astype(f32)
            output = (inputs[rows, :].astype(f32) + total).astype(bf16).astype(f32)
            old = jnp.where(slot == 0, states[0], states[1]).astype(f32)
            sent = jnp.clip((output - old) * inverse[...], -qmax, qmax).astype(bf16)
            renewed = (old + scale[...] * sent.astype(f32)).astype(bf16)
            for k in range(2):
                states[k] = jnp.where(active & (slot == k), renewed, states[k])
        for k in range(2):
            copies_ref[0, 0, k, rows, :] = new_in[k, rows, :]
            copies_ref[0, 1, k, rows, :] = states[k]
        return carry

    lax.fori_loop(0, SEQ // ROWS, step, 0)


def finish(*operands):
    return pl.pallas_call(
        finish_kernel,
        in_specs=[SMEM] + [VMEM] * 8,
        out_specs=VMEM,
        out_shape=jax.ShapeDtypeStruct((1, 2, 2, SEQ, 1024), bf16),
        compiler_params=GRANT,
        cost_estimate=pl.CostEstimate(flops=2**23, bytes_accessed=5 * 2**20, transcendentals=0),
        name="finish",
    )(*operands)


def along(shard, second, by):
    pairs = []
    for y in range(4):
        for x in range(4):
            by_x, by_y = y * 4 + (x + by) % 4, (y + by) % 4 * 4 + x
            pairs.append((y * 4 + x, by_y if second else by_x))
            pairs.append((16 + y * 4 + x, 16 + (by_x if second else by_y)))
    return lax.ppermute(shard, ("section", "y", "x"), pairs)


def from_first(shard, by, to_section):
    return lax.ppermute(
        shard, ("section", "tensor"), [(i, 4 * to_section + (i + by) % 4) for i in range(4)]
    )


def gathered(shard):
    before, after, far = along(shard, False, 1), along(shard, False, -1), along(shard, False, 2)
    own = jnp.stack([shard, before, after, far])
    before, after = along(own, True, 1), along(own, True, -1)
    return [own, before, after, along(before[:2], True, 1), along(after[2:], True, -1)]


def plus(*shards):
    return sum(shard.astype(f32) for shard in shards).astype(bf16)


def summed_over_plane(operands):
    ahead, back, next_low, last_high, own = terms(operands)
    from_before, from_after = lax.optimization_barrier(
        (along(ahead, True, 1), along(back, True, -1))
    )
    sum_before, sum_after = lax.optimization_barrier(
        (
            along(plus(next_low, from_before[:, :512]), True, 1),
            along(plus(last_high, from_after[:, :512]), True, -1),
        )
    )
    low = (own[:, :512], sum_before, from_after[:, 512:])
    high = (own[:, 512:], from_before[:, 512:], sum_after)
    blocks = []
    for parts in (low, high):
        for columns in (slice(0, 256), slice(256, 512)):
            blocks.append(plus(*(part[:, columns] for part in parts)))
    got = [
        along(blocks[3], False, -1),
        along(blocks[1], False, 1),
        along(blocks[2], False, 2),
    ]
    return plus(blocks[0], *got), own


def pick(state, slot):
    return jnp.where(slot == 0, state[0], state[1])


def put(state, slot, new, active=True):
    mask = (jnp.arange(2) == slot) & active
    return jnp.where(mask[:, None, None], new[None], state)


def on_device(
    boundary_copies,
    arriving,
    first_delta,
    sample_index,
    exponents,
    norm_gain,
    w_query,
    w_key,
    w_value,
    w_out,
    out_grad,
):
    first = lax.axis_index("section") == 0
    z = lax.axis_index("tensor")

    packed = jnp.concatenate([w_out[0].T, w_key[0], w_value[0]], axis=1)
    arriving, first_delta, packed = lax.optimization_barrier((arriving, first_delta, packed))
    full = lax.all_gather(packed, ("y", "x"), axis=0, tiled=True)
    full_o = full[:, :1024]
    pieces = [full] + gathered(w_query[0])

    power = exponents.astype(f32)
    scale_full = jnp.repeat(jnp.exp2(power), QB, axis=1)
    inverse_full = jnp.repeat(jnp.exp2(-power), QB, axis=1)
    scale_in = jnp.where(first, scale_full[0], scale_full[1])
    scale_next = jnp.where(first, scale_full[1], scale_full[2])
    inverse_next = jnp.where(first, inverse_full[1], inverse_full[2])
    slots = sample_index[:, 0]
    slot = [jnp.where(first, slots[k + 1], slots[k]) for k in range(3)]

    def receive(state, at, delta):
        return (pick(state, at).astype(f32) + scale_in * delta.astype(f32)).astype(bf16)

    def deliver(state, at, inputs, summed):
        output = (inputs.astype(f32) + summed).astype(bf16)
        old = pick(state, at)
        sent = jnp.clip(
            (output.astype(f32) - old.astype(f32)) * inverse_next, -qmax, qmax
        ).astype(bf16)
        step = scale_next * sent.astype(f32)
        return step.astype(bf16), (old.astype(f32) + step).astype(bf16)

    state_in, state_out = boundary_copies[0, 0], boundary_copies[0, 1]
    x0 = receive(state_in, slot[0], arriving[0, 0])
    state_in = put(state_in, slot[0], x0)
    x1 = receive(state_in, slot[1], first_delta[0, 0])
    state_1 = put(state_in, slot[1], x1)
    x2 = receive(state_1, slot[2], first_delta[1, 0])
    state_2 = put(state_1, slot[2], x2)
    known = jnp.concatenate(
        [jnp.where(first, x0, state_in[0]), jnp.where(first, x1, state_in[1]), x2], 0
    )
    known = lax.all_to_all(
        jnp.broadcast_to(known[None], (4,) + known.shape),
        "tensor",
        split_axis=0,
        concat_axis=0,
        tiled=True,
    )

    flags = jnp.stack(
        [first.astype(jnp.int32), *slot, lax.axis_index("x"), lax.axis_index("y"), z]
    ).astype(jnp.int32)
    normed_a = prepare(flags, norm_gain, known)
    qkv_a, mixed_a = project_call(project_a_kernel, "project_a", [flags, normed_a], pieces, False)
    far, near_1, near_3, own = spread(flags, mixed_a, full)
    parts = [own] + [
        from_first(piece, by, 0) for piece, by in ((near_3, 3), (near_1, 1), (far, 2))
    ]
    summed = sum(part.astype(f32) for part in parts)
    step_0, renewed = deliver(state_out, slot[0], x0, summed[:SEQ])
    out_1 = put(state_out, slot[0], renewed)
    step_1, renewed = deliver(out_1, slot[1], x1, summed[SEQ:])
    out_2 = put(out_1, slot[1], renewed)
    steps = jnp.concatenate([step_0, step_1], 0)
    got = [from_first(steps, by, 1) for by in range(4)]

    def added(state, at, step):
        return (pick(state, at).astype(f32) + step.astype(f32)).astype(bf16)

    normed_b, qkv_b, mixed_b = project_call(
        project_b_kernel, "project_b", [flags, norm_gain, known, *got], pieces, True
    )
    y1 = added(state_in, slot[1], got[0][:SEQ])
    after_1 = put(state_in, slot[1], y1)
    y2 = added(after_1, slot[2], got[0][SEQ:])
    new_in = jnp.where(first, state_2, put(after_1, slot[2], y2))

    up = out_grad[0, :, 0].reshape(3 * SEQ, -1)
    d_mixed = jnp.dot(up, full_o, preferred_element_type=f32).astype(bf16)
    d_a = attend_back(qkv_a, d_mixed[: 2 * SEQ])
    d_mixed_b = jnp.concatenate(
        [jnp.where(first, d_mixed[2 * SEQ :], d_mixed[SEQ : 2 * SEQ]), d_mixed[2 * SEQ :]], 0
    )
    d_b = attend_back(qkv_b, d_mixed_b)

    grad, own_terms = summed_over_plane([flags, normed_a, normed_b, d_a, d_b])
    grad = grad.T

    mixed_f = jnp.concatenate([jnp.where(first, mixed_b[:SEQ], mixed_a[:SEQ]), mixed_b], 0)
    mixed_f, _ = lax.optimization_barrier((mixed_f, own_terms))
    partial = lax.dot_general(mixed_f, full_o, NT, preferred_element_type=f32).astype(bf16)
    summed = lax.psum_scatter(partial, "tensor", scatter_dimension=1, tiled=True)
    copies_new = finish(
        flags,
        new_in,
        jnp.where(first, out_2, state_out),
        summed,
        jnp.where(first, x2, x0),
        y1,
        y2,
        scale_next[None],
        inverse_next[None],
    )
    return (copies_new, grad[None, :, :1024], grad[None, :, 1024:])


def solution(mesh):
    shape = dict(mesh.shape)
    grid = Mesh(
        mesh.devices.reshape(shape["section"], 4, shape["dp"] // 4, shape["tensor"]),
        ("section", "y", "x", "tensor"),
    )
    dp = ("y", "x")
    return jax.shard_map(
        on_device,
        mesh=grid,
        in_specs=(
            P("section", None, dp, None, "tensor"),
            P("section", dp, None, "tensor"),
            P(None, dp, None, "tensor"),
            P(None, dp),
            P(None, "tensor"),
            P("section", None),
            P("section", dp, "tensor"),
            P("section", dp, "tensor"),
            P("section", dp, "tensor"),
            P("section", "tensor", dp),
            P("section", None, dp, None, None),
        ),
        out_specs=(
            P("section", None, dp, None, "tensor"),
            P("section", dp, "tensor"),
            P("section", dp, "tensor"),
        ),
        check_vma=False,
    )
```

```python
import functools

import jax
import jax.numpy as jnp
from jax import lax
from jax.experimental import pallas as pl
from jax.experimental.pallas import tpu as pltpu
from jax.sharding import Mesh, PartitionSpec as P

HQ = 32
HK = 4
HD = 128
QB = 128
SEQ = 128

eps_norm = 1e-05
qmax = 7.0
f32 = jnp.float32
bf16 = jnp.bfloat16


GROUP = HQ // HK
UNITS = 3
NT = (((1,), (1,)), ((), ()))
TN = (((0,), (0,)), ((), ()))


def stacked(rows):
    return jnp.concatenate([rows[:, h * HD : (h + 1) * HD] for h in range(GROUP)], axis=0)


def side_by_side(rows):
    return jnp.concatenate([rows[h * SEQ : (h + 1) * SEQ] for h in range(GROUP)], axis=1)


def probs_of(query, key_in):
    scores = lax.dot_general(query, key_in, NT, preferred_element_type=f32) * HD ** (-0.5)
    at = lax.broadcasted_iota(jnp.int32, scores.shape, 0) % SEQ
    key_at = lax.broadcasted_iota(jnp.int32, scores.shape, 1)
    scores = jnp.where(at >= key_at, scores, -1e30)
    weight = jnp.exp(scores - jnp.max(scores, axis=-1, keepdims=True))
    return weight / jnp.sum(weight, axis=-1, keepdims=True)


def attend_unit(qkv):
    wide = GROUP * HD
    probs = probs_of(stacked(qkv[:, :wide]), qkv[:, wide : wide + HD])
    mixed = jnp.dot(probs.astype(bf16), qkv[:, wide + HD :], preferred_element_type=f32)
    return side_by_side(mixed.astype(bf16))


def attend_back_kernel(qkv_ref, d_mixed_ref, out_ref):
    wide = GROUP * HD
    key_in = qkv_ref[:, wide : wide + HD]
    probs = probs_of(stacked(qkv_ref[:, :wide]), key_in)
    d_rows = stacked(d_mixed_ref[...])
    d_probs = lax.dot_general(d_rows, qkv_ref[:, wide + HD :], NT, preferred_element_type=f32)
    d_scores = (
        probs * (d_probs - jnp.sum(d_probs * probs, axis=-1, keepdims=True)) * HD ** (-0.5)
    )
    d_query = jnp.dot(d_scores.astype(bf16), key_in, preferred_element_type=f32).astype(bf16)
    d_value = lax.dot_general(probs.astype(bf16), d_rows, TN, preferred_element_type=f32)
    out_ref[:, :wide] = side_by_side(d_query)
    out_ref[:, wide:] = d_value.astype(bf16)


def attend_back(qkv, d_mixed):
    rows = qkv.shape[0]
    return pl.pallas_call(
        attend_back_kernel,
        grid=(rows // SEQ,),
        in_specs=[
            pl.BlockSpec((SEQ, (GROUP + 2) * HD), lambda u: (u, 0)),
            pl.BlockSpec((SEQ, GROUP * HD), lambda u: (u, 0)),
        ],
        out_specs=pl.BlockSpec((SEQ, (GROUP + 1) * HD), lambda u: (u, 0)),
        out_shape=jax.ShapeDtypeStruct((rows, (GROUP + 1) * HD), bf16),
        compiler_params=pltpu.CompilerParams(vmem_limit_bytes=32 * 1024 * 1024),
        cost_estimate=pl.CostEstimate(
            flops=rows * SEQ * GROUP * HD * 8,
            bytes_accessed=rows * 3456 * 2,
            transcendentals=rows * SEQ * GROUP,
        ),
        name="attend_back",
    )(qkv, d_mixed)


ROWS = 16
ORDER = (0, 3, 1, 2)


def known_a(flags, known_ref, x_ref):
    from_0 = (flags[0] == 1) | (flags[1] == 0)

    def step(i, carry):
        at = pl.multiple_of(i * ROWS, ROWS)
        for j in range(4):
            one = known_ref[j, pl.ds(at, ROWS), :]
            two = known_ref[j, pl.ds(at + SEQ, ROWS), :]
            columns = slice(j * 1024, (j + 1) * 1024)
            x_ref[pl.ds(at, ROWS), columns] = jnp.where(from_0, one, two)
            x_ref[pl.ds(at + SEQ, ROWS), columns] = two
        return carry

    lax.fori_loop(0, SEQ // ROWS, step, 0)


def known_b(flags, known_ref, got_refs, x_ref):
    first = flags[0] == 1
    slot_1, slot_2 = flags[2], flags[3]

    def step(i, carry):
        at = pl.multiple_of(i * ROWS, ROWS)
        for by in range(4):
            j = lax.rem(flags[6] + 4 - by, 4)
            one = known_ref[j, pl.ds(at, ROWS), :].astype(f32)
            two = known_ref[j, pl.ds(at + SEQ, ROWS), :].astype(f32)
            third = known_ref[j, pl.ds(at + 2 * SEQ, ROWS), :]
            step_1 = got_refs[by][pl.ds(at, ROWS), :].astype(f32)
            step_2 = got_refs[by][pl.ds(at + SEQ, ROWS), :].astype(f32)
            x_1 = (jnp.where(slot_1 == 0, one, two) + step_1).astype(bf16)
            old = jnp.where(
                slot_1 == slot_2, x_1.astype(f32), jnp.where(slot_2 == 0, one, two)
            )
            columns = pl.ds(pl.multiple_of(j * 1024, 1024), 1024)
            x_ref[pl.ds(at, ROWS), columns] = jnp.where(first, third, x_1)
            x_ref[pl.ds(at + SEQ, ROWS), columns] = (old + step_2).astype(bf16)
        return carry

    lax.fori_loop(0, SEQ // ROWS, step, 0)


def normalize(gain_ref, x_ref):
    def step(i, carry):
        rows = pl.ds(pl.multiple_of(i * ROWS, ROWS), ROWS)
        values = x_ref[rows, :].astype(f32)
        square = jnp.mean(values * values, axis=-1, keepdims=True)
        x_ref[rows, :] = (values * lax.rsqrt(square + eps_norm) * gain_ref[...]).astype(bf16)
        return carry

    lax.fori_loop(0, 2 * SEQ // ROWS, step, 0)


def prepare_kernel(flags, gain_ref, known_ref, normed_ref):
    known_a(flags, known_ref, normed_ref)
    normalize(gain_ref, normed_ref)


VMEM = pl.BlockSpec(memory_space=pltpu.VMEM)
SMEM = pl.BlockSpec(memory_space=pltpu.SMEM)
ANY = pl.BlockSpec(memory_space=pl.ANY)
GRANT = pltpu.CompilerParams(vmem_limit_bytes=60 * 1024 * 1024)


def prepare(flags, gain, known):
    return pl.pallas_call(
        prepare_kernel,
        in_specs=[SMEM, VMEM, VMEM],
        out_specs=VMEM,
        out_shape=jax.ShapeDtypeStruct((2 * SEQ, 4096), bf16),
        compiler_params=pltpu.CompilerParams(vmem_limit_bytes=32 * 1024 * 1024),
        cost_estimate=pl.CostEstimate(flops=2**23, bytes_accessed=5 * 2**20, transcendentals=0),
        name="prepare",
    )(flags, gain, known)


def project_kernel(flags, pieces, normed_ref, qkv_ref, mixed_ref, held, held_kv, sems, begin):
    full_ref, pieces = pieces[0], pieces[1:]
    copies = []
    for at in range(5):
        target = held.at[at] if at < 3 else held.at[3, pl.ds(2 * (at - 3), 2)]
        copies.append(pltpu.make_async_copy(pieces[at], target, sems.at[at]))
    copies.append(pltpu.make_async_copy(full_ref.at[:, pl.ds(1024, 256)], held_kv, sems.at[5]))
    for copy in copies:
        copy.start()
    begin()
    total = None
    for at in range(4):
        lhs = []
        for block in range(4):
            second, inner = ORDER[at], ORDER[block]
            dy = jnp.where(flags[0] == 1, second, inner)
            dx = jnp.where(flags[0] == 1, inner, second)
            row = lax.rem(flags[5] + dy, 4) * 4 + lax.rem(flags[4] + dx, 4)
            lhs.append(normed_ref[:, pl.ds(pl.multiple_of(row * 256, 256), 256)])
        copies[at].wait()
        if at == 3:
            copies[4].wait()
        part = jnp.dot(
            jnp.concatenate(lhs, axis=1), held[at].reshape(1024, 1024), preferred_element_type=f32
        )
        total = part if total is None else total + part
    qkv_ref[:, :1024] = total.astype(bf16)
    copies[5].wait()
    qkv_ref[:, 1024:] = jnp.dot(
        normed_ref[...], held_kv[...], preferred_element_type=f32
    ).astype(bf16)
    for unit in range(2):
        rows = slice(unit * SEQ, (unit + 1) * SEQ)
        mixed_ref[rows, :] = attend_unit(qkv_ref[rows, :])


def project_a_kernel(flags, normed_ref, *refs):
    pieces, (qkv_ref, mixed_ref, held, held_kv, sems) = refs[:6], refs[6:]
    project_kernel(flags, pieces, normed_ref, qkv_ref, mixed_ref, held, held_kv, sems, lambda: None)


def project_b_kernel(flags, gain_ref, known_ref, *refs):
    got_refs, pieces = refs[:4], refs[4:10]
    normed_ref, qkv_ref, mixed_ref, held, held_kv, sems = refs[10:]

    def begin():
        known_b(flags, known_ref, got_refs, normed_ref)
        normalize(gain_ref, normed_ref)

    project_kernel(flags, pieces, normed_ref, qkv_ref, mixed_ref, held, held_kv, sems, begin)


def project_call(kernel, name, operands, pieces, with_normed):
    rows = 2 * SEQ
    shapes = [
        jax.ShapeDtypeStruct((rows, 4096), bf16),
        jax.ShapeDtypeStruct((rows, (GROUP + 2) * HD), bf16),
        jax.ShapeDtypeStruct((rows, GROUP * HD), bf16),
    ][0 if with_normed else 1 :]
    return pl.pallas_call(
        kernel,
        in_specs=[SMEM] + [VMEM] * (len(operands) - 1) + [ANY] * 6,
        out_specs=[VMEM] * len(shapes),
        out_shape=shapes,
        scratch_shapes=[
            pltpu.VMEM((4, 4, 256, 1024), bf16),
            pltpu.VMEM((4096, 256), bf16),
            pltpu.SemaphoreType.DMA((6,)),
        ],
        compiler_params=GRANT,
        cost_estimate=pl.CostEstimate(
            flops=2 * rows * 4096 * 1280, bytes_accessed=18 * 2**20, transcendentals=rows * 1024
        ),
        name=name,
    )(*operands, *pieces)


def spread_kernel(flags, mixed_ref, full_ref, *refs):
    outs, (held, sems) = refs[:4], refs[4:]
    copies = []
    for i, by in enumerate((2, 1, 3, 0)):
        row = pl.multiple_of(lax.rem(flags[6] + by, 4) * 1024, 1024)
        copies.append(
            pltpu.make_async_copy(full_ref.at[pl.ds(row, 1024), pl.ds(0, 1024)], held.at[i], sems.at[i])
        )
        copies[-1].start()
    for i in range(4):
        copies[i].wait()
        outs[i][...] = lax.dot_general(
            mixed_ref[...], held[i], NT, preferred_element_type=f32
        ).astype(bf16)


def spread(flags, mixed, full):
    rows = mixed.shape[0]
    return pl.pallas_call(
        spread_kernel,
        in_specs=[SMEM, VMEM, ANY],
        out_specs=[VMEM] * 4,
        out_shape=[jax.ShapeDtypeStruct((rows, 1024), bf16)] * 4,
        scratch_shapes=[pltpu.VMEM((4, 1024, 1024), bf16), pltpu.SemaphoreType.DMA((4,))],
        compiler_params=GRANT,
        cost_estimate=pl.CostEstimate(
            flops=2 * rows * 4096 * 1024, bytes_accessed=12 * 2**20, transcendentals=0
        ),
        name="spread",
    )(flags, mixed, full)


WIDE = (GROUP + 1) * HD


def three(flags, a_ref, b_ref, columns):
    middle = jnp.where(flags[0] == 1, a_ref[SEQ:, columns], b_ref[SEQ:, columns])
    return jnp.concatenate([a_ref[:SEQ, columns], middle, b_ref[:SEQ, columns]], axis=0)


PLACES = (((2, 0), (1, 1)), ((2, 1), (3, 0)), ((1, 0),), ((3, 1),), ((0, 0), (0, 1)))


def terms_kernel(flags, normed_a, normed_b, d_a, d_b, *refs):
    outs, (held, sems) = refs[:5], refs[5:]
    d_rows = three(flags, d_a, d_b, slice(None)).T
    copies = []
    places = [(out, k, place) for out, parts in zip(outs, PLACES) for k, place in enumerate(parts)]
    for i, (out, k, (outer, pair)) in enumerate(places):
        features = []
        for inner in (2 * pair, 2 * pair + 1):
            dy = jnp.where(flags[0] == 1, outer, inner)
            dx = jnp.where(flags[0] == 1, inner, outer)
            row = lax.rem(flags[5] + dy, 4) * 4 + lax.rem(flags[4] + dx, 4)
            columns = pl.ds(pl.multiple_of(row * 256, 256), 256)
            features.append(three(flags, normed_a, normed_b, columns))
        held[i] = jnp.dot(
            d_rows, jnp.concatenate(features, axis=1), preferred_element_type=f32
        ).astype(bf16)
        target = out.at[:, pl.ds(512 * k, 512)]
        copies.append(pltpu.make_async_copy(held.at[i], target, sems.at[i]))
        copies[-1].start()
    for copy in copies:
        copy.wait()


def terms(operands):
    return pl.pallas_call(
        terms_kernel,
        in_specs=[SMEM] + [VMEM] * 4,
        out_specs=[ANY] * 5,
        out_shape=[jax.ShapeDtypeStruct((WIDE, 512 * len(parts)), bf16) for parts in PLACES],
        scratch_shapes=[pltpu.VMEM((8, WIDE, 512), bf16), pltpu.SemaphoreType.DMA((8,))],
        compiler_params=pltpu.CompilerParams(vmem_limit_bytes=32 * 1024 * 1024),
        cost_estimate=pl.CostEstimate(
            flops=2 * 3 * SEQ * 4096 * WIDE, bytes_accessed=14 * 2**20, transcendentals=0
        ),
        name="terms",
    )(*operands)


def finish_kernel(flags, new_in, state_out, summed, x_0, x_1, x_2, scale, inverse, copies_ref):
    first = flags[0] == 1
    units = (
        (x_0, jnp.where(first, flags[3], flags[1]), first | True),
        (x_1, flags[2], jnp.logical_not(first)),
        (x_2, flags[3], jnp.logical_not(first)),
    )

    def step(i, carry):
        at = pl.multiple_of(i * ROWS, ROWS)
        rows = pl.ds(at, ROWS)
        states = [state_out[0, rows, :], state_out[1, rows, :]]
        for unit, (inputs, slot, active) in enumerate(units):
            total = summed[pl.ds(at + unit * SEQ, ROWS), :].astype(f32)
            output = (inputs[rows, :].astype(f32) + total).astype(bf16).astype(f32)
            old = jnp.where(slot == 0, states[0], states[1]).astype(f32)
            sent = jnp.clip((output - old) * inverse[...], -qmax, qmax).astype(bf16)
            renewed = (old + scale[...] * sent.astype(f32)).astype(bf16)
            for k in range(2):
                states[k] = jnp.where(active & (slot == k), renewed, states[k])
        for k in range(2):
            copies_ref[0, 0, k, rows, :] = new_in[k, rows, :]
            copies_ref[0, 1, k, rows, :] = states[k]
        return carry

    lax.fori_loop(0, SEQ // ROWS, step, 0)


def finish(*operands):
    return pl.pallas_call(
        finish_kernel,
        in_specs=[SMEM] + [VMEM] * 8,
        out_specs=VMEM,
        out_shape=jax.ShapeDtypeStruct((1, 2, 2, SEQ, 1024), bf16),
        compiler_params=GRANT,
        cost_estimate=pl.CostEstimate(flops=2**23, bytes_accessed=5 * 2**20, transcendentals=0),
        name="finish",
    )(*operands)


def along(shard, second, by):
    pairs = []
    for y in range(4):
        for x in range(4):
            by_x, by_y = y * 4 + (x + by) % 4, (y + by) % 4 * 4 + x
            pairs.append((y * 4 + x, by_y if second else by_x))
            pairs.append((16 + y * 4 + x, 16 + (by_x if second else by_y)))
    return lax.ppermute(shard, ("section", "y", "x"), pairs)


def from_first(shard, by, to_section):
    return lax.ppermute(
        shard, ("section", "tensor"), [(i, 4 * to_section + (i + by) % 4) for i in range(4)]
    )


def gathered(shard):
    before, after, far = along(shard, False, 1), along(shard, False, -1), along(shard, False, 2)
    own = jnp.stack([shard, before, after, far])
    before, after = along(own, True, 1), along(own, True, -1)
    return [own, before, after, along(before[:2], True, 1), along(after[2:], True, -1)]


def plus(*shards):
    return sum(shard.astype(f32) for shard in shards).astype(bf16)


def summed_over_plane(operands):
    ahead, back, next_low, last_high, own = terms(operands)
    from_before, from_after = lax.optimization_barrier(
        (along(ahead, True, 1), along(back, True, -1))
    )
    sum_before, sum_after = lax.optimization_barrier(
        (
            along(plus(next_low, from_before[:, :512]), True, 1),
            along(plus(last_high, from_after[:, :512]), True, -1),
        )
    )
    low = (own[:, :512], sum_before, from_after[:, 512:])
    high = (own[:, 512:], from_before[:, 512:], sum_after)
    blocks = []
    for parts in (low, high):
        for columns in (slice(0, 256), slice(256, 512)):
            blocks.append(plus(*(part[:, columns] for part in parts)))
    got = [
        along(blocks[3], False, -1),
        along(blocks[1], False, 1),
        along(blocks[2], False, 2),
    ]
    return plus(blocks[0], *got), own


def pick(state, slot):
    return jnp.where(slot == 0, state[0], state[1])


def put(state, slot, new, active=True):
    mask = (jnp.arange(2) == slot) & active
    return jnp.where(mask[:, None, None], new[None], state)


def on_device(
    boundary_copies,
    arriving,
    first_delta,
    sample_index,
    exponents,
    norm_gain,
    w_query,
    w_key,
    w_value,
    w_out,
    out_grad,
):
    first = lax.axis_index("section") == 0
    z = lax.axis_index("tensor")

    packed = jnp.concatenate([w_out[0].T, w_key[0], w_value[0]], axis=1)
    arriving, first_delta, packed = lax.optimization_barrier((arriving, first_delta, packed))
    full = lax.all_gather(packed, ("y", "x"), axis=0, tiled=True)
    full_o = full[:, :1024]
    pieces = [full] + gathered(w_query[0])

    power = exponents.astype(f32)
    scale_full = jnp.repeat(jnp.exp2(power), QB, axis=1)
    inverse_full = jnp.repeat(jnp.exp2(-power), QB, axis=1)
    scale_in = jnp.where(first, scale_full[0], scale_full[1])
    scale_next = jnp.where(first, scale_full[1], scale_full[2])
    inverse_next = jnp.where(first, inverse_full[1], inverse_full[2])
    slots = sample_index[:, 0]
    slot = [jnp.where(first, slots[k + 1], slots[k]) for k in range(3)]

    def receive(state, at, delta):
        return (pick(state, at).astype(f32) + scale_in * delta.astype(f32)).astype(bf16)

    def deliver(state, at, inputs, summed):
        output = (inputs.astype(f32) + summed).astype(bf16)
        old = pick(state, at)
        sent = jnp.clip(
            (output.astype(f32) - old.astype(f32)) * inverse_next, -qmax, qmax
        ).astype(bf16)
        step = scale_next * sent.astype(f32)
        return step.astype(bf16), (old.astype(f32) + step).astype(bf16)

    state_in, state_out = boundary_copies[0, 0], boundary_copies[0, 1]
    x0 = receive(state_in, slot[0], arriving[0, 0])
    state_in = put(state_in, slot[0], x0)
    x1 = receive(state_in, slot[1], first_delta[0, 0])
    state_1 = put(state_in, slot[1], x1)
    x2 = receive(state_1, slot[2], first_delta[1, 0])
    state_2 = put(state_1, slot[2], x2)
    known = jnp.concatenate(
        [jnp.where(first, x0, state_in[0]), jnp.where(first, x1, state_in[1]), x2], 0
    )
    known = lax.all_to_all(
        jnp.broadcast_to(known[None], (4,) + known.shape),
        "tensor",
        split_axis=0,
        concat_axis=0,
        tiled=True,
    )

    flags = jnp.stack(
        [first.astype(jnp.int32), *slot, lax.axis_index("x"), lax.axis_index("y"), z]
    ).astype(jnp.int32)
    normed_a = prepare(flags, norm_gain, known)
    qkv_a, mixed_a = project_call(project_a_kernel, "project_a", [flags, normed_a], pieces, False)
    far, near_1, near_3, own = spread(flags, mixed_a, full)
    parts = [own] + [
        from_first(piece, by, 0) for piece, by in ((near_3, 3), (near_1, 1), (far, 2))
    ]
    summed = sum(part.astype(f32) for part in parts)
    step_0, renewed = deliver(state_out, slot[0], x0, summed[:SEQ])
    out_1 = put(state_out, slot[0], renewed)
    step_1, renewed = deliver(out_1, slot[1], x1, summed[SEQ:])
    out_2 = put(out_1, slot[1], renewed)
    steps = jnp.concatenate([step_0, step_1], 0)
    got = [from_first(steps, by, 1) for by in range(4)]

    def added(state, at, step):
        return (pick(state, at).astype(f32) + step.astype(f32)).astype(bf16)

    normed_b, qkv_b, mixed_b = project_call(
        project_b_kernel, "project_b", [flags, norm_gain, known, *got], pieces, True
    )
    y1 = added(state_in, slot[1], got[0][:SEQ])
    after_1 = put(state_in, slot[1], y1)
    y2 = added(after_1, slot[2], got[0][SEQ:])
    new_in = jnp.where(first, state_2, put(after_1, slot[2], y2))

    up = out_grad[0, :, 0].reshape(3 * SEQ, -1)
    d_mixed = jnp.dot(up, full_o, preferred_element_type=f32).astype(bf16)
    d_a = attend_back(qkv_a, d_mixed[: 2 * SEQ])
    d_mixed_b = jnp.concatenate(
        [jnp.where(first, d_mixed[2 * SEQ :], d_mixed[SEQ : 2 * SEQ]), d_mixed[2 * SEQ :]], 0
    )
    d_b = attend_back(qkv_b, d_mixed_b)

    grad, own_terms = summed_over_plane([flags, normed_a, normed_b, d_a, d_b])
    grad = grad.T

    mixed_f = jnp.concatenate([jnp.where(first, mixed_b[:SEQ], mixed_a[:SEQ]), mixed_b], 0)
    mixed_f, _, scale_row, inverse_row = lax.optimization_barrier(
        (mixed_f, own_terms, scale_next[None], inverse_next[None])
    )
    partial = lax.dot_general(mixed_f, full_o, NT, preferred_element_type=f32).astype(bf16)
    summed = lax.psum_scatter(partial, "tensor", scatter_dimension=1, tiled=True)
    copies_new = finish(
        flags,
        new_in,
        jnp.where(first, out_2, state_out),
        summed,
        jnp.where(first, x2, x0),
        y1,
        y2,
        scale_row,
        inverse_row,
    )
    return (copies_new, grad[None, :, :1024], grad[None, :, 1024:])


def solution(mesh):
    shape = dict(mesh.shape)
    grid = Mesh(
        mesh.devices.reshape(shape["section"], 4, shape["dp"] // 4, shape["tensor"]),
        ("section", "y", "x", "tensor"),
    )
    dp = ("y", "x")
    return jax.shard_map(
        on_device,
        mesh=grid,
        in_specs=(
            P("section", None, dp, None, "tensor"),
            P("section", dp, None, "tensor"),
            P(None, dp, None, "tensor"),
            P(None, dp),
            P(None, "tensor"),
            P("section", None),
            P("section", dp, "tensor"),
            P("section", dp, "tensor"),
            P("section", dp, "tensor"),
            P("section", "tensor", dp),
            P("section", None, dp, None, None),
        ),
        out_specs=(
            P("section", None, dp, None, "tensor"),
            P("section", dp, "tensor"),
            P("section", dp, "tensor"),
        ),
        check_vma=False,
    )
```
